32 devices in a mesh: dp: 4 (over y, x), row: 2 (over core), col: 4 (over z).
Axes of the slice: x: 2, y: 2, z: 4, core: 2. Of those that a mesh axis runs over, the one named last changes fastest.
Arguments:
- tokens: bfloat16 [4, 2048, 1600], P('dp', 'row', 'col'), may hold values from -6 to 6
- cotangent: bfloat16 [4, 2048, 1600], P('dp', 'row', 'col'), may hold values from -6 to 6
- w_qkv: bfloat16 [3, 1600, 1600], P(None, 'row', 'col'), may hold values from -0.15625 to 0.15625
- q_bias: float32 [1600], P('col'), may hold values from -3 to 3
- v_bias: float32 [1600], P('col'), may hold values from -0.18 to 0.18
- w_out: bfloat16 [1600, 1600], P('row', 'col'), may hold values from -3 to 3
- out_bias: float32 [1600], P('col'), may hold values from -2 to 2
- w_up: bfloat16 [1600, 6400], P('row', 'col'), may hold values from -0.15625 to 0.15625
- up_bias: float32 [6400], P('col'), may hold values from -3 to 3
- w_down: bfloat16 [6400, 1600], P('row', 'col'), may hold values from -0.078125 to 0.078125
- down_bias: float32 [1600], P('col'), may hold values from -2 to 2
- ln1_gain: float32 [1600], P('col'), may hold values from 0.5 to 1.5
- ln1_bias: float32 [1600], P('col'), may hold values from -1.2 to 1.2
- ln2_gain: float32 [1600], P('col'), may hold values from 0.5 to 1.5
- ln2_bias: float32 [1600], P('col'), may hold values from -1.2 to 1.2
- key_start: int32 [25, 4], replicated, may hold values from 0 to 3, as said below
Outputs:
- outputs: bfloat16 [4, 2048, 1600], P('dp', 'row', 'col')
- input_grad: bfloat16 [4, 2048, 1600], P('dp', 'row', 'col')
- w_qkv_grad: float32 [3, 1600, 1600], P(None, 'row', 'col')
- q_bias_grad: float32 [1600], P('col')
- v_bias_grad: float32 [1600], P('col')
- w_out_grad: float32 [1600, 1600], P('row', 'col')
- out_bias_grad: float32 [1600], P('col')
- w_up_grad: float32 [1600, 6400], P('row', 'col')
- up_bias_grad: float32 [6400], P('col')
- w_down_grad: float32 [6400, 1600], P('row', 'col')
- down_bias_grad: float32 [1600], P('col')
- ln1_gain_grad: float32 [1600], P('col')
- ln1_bias_grad: float32 [1600], P('col')
- ln2_gain_grad: float32 [1600], P('col')
- ln2_bias_grad: float32 [1600], P('col')
The draws below stay inside these ranges and needn't reach their ends.
Inputs may be any that keep to these rules, and one draw needn't show every extreme that they name: key_start[h, b] <= b for every head h and query block b; in every draw one head has 0 for every query block and another has b for every query block b.
All inputs are finite; a program needn't handle non-finite values.
Results may differ from the reference program's by a relative error of at most 0.034.
Values may be sent and summed in bfloat16 or wider, within the bound.
No kernel may reach another device: no remote copies, remote signals or barrier semaphores. Data moves between devices by JAX's collectives and lax.ppermute only.
A program may use at most 320 MiB of HBM per device.

```python
import jax
import jax.numpy as jnp
from jax import lax

D = 1600
HEADS = 25
HD = 64
FF = 6400
SEQ = 2048
BLK = 512
QB = 4
SEQS = 4


def draw_key_start(key, part):
    key = jax.random.fold_in(key, 7)
    first_key, second_key = jax.random.split(key)
    raw = jax.random.randint(first_key, (HEADS, QB), 0, 1 << 20)
    blocks = jnp.arange(QB, dtype=jnp.int32)[None, :]
    starts = raw % (blocks + 1)
    chosen = jax.random.permutation(second_key, HEADS)
    heads = jnp.arange(HEADS, dtype=jnp.int32)[:, None]
    starts = jnp.where(heads == chosen[0], 0, starts)
    starts = jnp.where(heads == chosen[1], blocks, starts)
    return starts.astype(jnp.int32)


def steps_of(rng, extent, cuts, smallest, top_value):
    loudness = 1.0
    for axis_at, parts in cuts:
        steps = jax.random.uniform(jax.random.fold_in(jax.random.fold_in(rng, 6), axis_at), (parts,), jnp.float32, smallest / len(cuts), top_value / len(cuts))
        loudness = loudness * jnp.repeat(jnp.exp(steps), extent[axis_at] // parts).reshape((-1,) + (1,) * (len(extent) - 1 - axis_at))
    return loudness


def gaussian(own_key, extent, width, reach, pieces=(), kind=jnp.bfloat16):
    level = steps_of(own_key, extent, pieces, -0.22, 0.18) if pieces else 1.0
    values = jax.random.normal(own_key, extent, jnp.float32) * width * level
    return jnp.minimum(jnp.maximum(values, -reach), reach).astype(kind)


def setup_inputs(seed: int = 0) -> dict:
    key_list = jax.random.split(jax.random.key(seed), 17)
    tokens = gaussian(key_list[0], (SEQS, SEQ, D), 1.0, 6.0, ((0, 4), (1, 2), (2, 4)))
    cotangent = gaussian(key_list[1], (SEQS, SEQ, D), 1.0, 6.0, ((0, 4), (1, 2), (2, 4)))
    w_qkv = gaussian(key_list[2], (3, D, D), D ** -0.5, 0.15625, ((1, 2), (2, 4)))
    q_bias = gaussian(key_list[3], (D,), 0.5, 3.0, ((0, 4),), jnp.float32)
    v_bias = gaussian(key_list[4], (D,), 0.03, 0.18, ((0, 4),), jnp.float32)
    w_out = gaussian(key_list[5], (D, D), (max(D // 400, 1)) ** -0.5, 3.0, ((0, 2), (1, 4)))
    out_bias = gaussian(key_list[6], (D,), 0.3, 2.0, ((0, 4),), jnp.float32)
    w_up = gaussian(key_list[7], (D, FF), D ** -0.5, 0.15625, ((0, 2), (1, 4)))
    up_bias = gaussian(key_list[8], (FF,), 0.5, 3.0, ((0, 4),), jnp.float32)
    w_down = gaussian(key_list[9], (FF, D), FF ** -0.5, 0.078125, ((0, 2), (1, 4)))
    down_bias = gaussian(key_list[10], (D,), 0.3, 2.0, ((0, 4),), jnp.float32)
    ln1_gain = jnp.clip(1.0 + 0.1 * jax.random.normal(key_list[11], (D,), jnp.float32), 0.5, 1.5)
    ln1_bias = gaussian(key_list[12], (D,), 0.2, 1.2, ((0, 4),), jnp.float32)
    ln2_gain = jnp.clip(1.0 + 0.1 * jax.random.normal(key_list[13], (D,), jnp.float32), 0.5, 1.5)
    ln2_bias = gaussian(key_list[14], (D,), 0.2, 1.2, ((0, 4),), jnp.float32)
    key_start = draw_key_start(jax.random.fold_in(key_list[16], 71), 0)
    return dict(tokens=tokens, cotangent=cotangent, w_qkv=w_qkv, q_bias=q_bias, v_bias=v_bias, w_out=w_out, out_bias=out_bias, w_up=w_up, up_bias=up_bias, w_down=w_down, down_bias=down_bias, ln1_gain=ln1_gain, ln1_bias=ln1_bias, ln2_gain=ln2_gain, ln2_bias=ln2_bias, key_start=key_start)


@jax.custom_vjp
def low(v):
    return lax.optimization_barrier(v.astype(jnp.bfloat16)).astype(jnp.float32)

@jax.custom_vjp
def low_back(v):
    return v

def low_keep(v):
    return (low(v), None)

def low_pass(kept, grad):
    return (grad,)

def back_keep(v):
    return (v, None)

def back_low(kept, grad):
    return (low(grad),)
low.defvjp(low_keep, low_pass)
low_back.defvjp(back_keep, back_low)

def matmul(first_arg, second_arg):
    return jnp.dot(first_arg, second_arg, precision=lax.Precision.HIGHEST)

def layer_norm(values, gain, shift):
    mean = lax.optimization_barrier(jnp.mean(values, axis=-1, keepdims=True))
    centred = values - mean
    variance = lax.optimization_barrier(jnp.mean(centred * centred, axis=-1, keepdims=True))
    return centred * lax.rsqrt(variance + 1e-05) * gain + shift

def head_attention(inputs):
    query, keys, values, starts = inputs
    raw = matmul(query, keys.T)
    scores = low_back(raw) * HD ** (-0.5)
    position = jnp.arange(SEQ, dtype=jnp.int32)
    first_key = jnp.repeat(starts, BLK) * BLK
    visible = (position[None, :] <= position[:, None]) & (position[None, :] >= first_key[:, None])
    scores = jnp.where(visible, scores, -1e+30)
    top = lax.optimization_barrier(jnp.max(scores, axis=-1, keepdims=True))
    weights = jnp.exp(scores - top)
    probs = weights / lax.optimization_barrier(jnp.sum(weights, axis=-1, keepdims=True))
    return matmul(low(probs), values)

def split_heads(values):
    return values.reshape(SEQ, HEADS, HD).transpose(1, 0, 2)

def forward(params, tokens, key_start):
    w_qkv, q_bias, v_bias, w_out, out_bias, w_up, up_bias, w_down, down_bias, ln1_gain, ln1_bias, ln2_gain, ln2_bias = params
    normed = low(layer_norm(tokens, ln1_gain, ln1_bias))
    query = low_back(low(matmul(normed, w_qkv[0]) + q_bias))
    keys = low_back(low(matmul(normed, w_qkv[1])))
    values = low_back(low(matmul(normed, w_qkv[2]) + v_bias))
    mixed = lax.map(jax.checkpoint(head_attention), (split_heads(query), split_heads(keys), split_heads(values), key_start))
    attention = low_back(low(mixed.transpose(1, 0, 2).reshape(SEQ, D)))
    resid = tokens + low_back(matmul(attention, w_out) + out_bias)
    normed_two = low(layer_norm(resid, ln2_gain, ln2_bias))
    upper = low_back(matmul(normed_two, w_up) + up_bias)
    hidden = low(jax.nn.gelu(upper, approximate=True))
    return resid + low_back(matmul(hidden, w_down) + down_bias)

def reference(tokens, cotangent, w_qkv, q_bias, v_bias, w_out, out_bias, w_up, up_bias, w_down, down_bias, ln1_gain, ln1_bias, ln2_gain, ln2_bias, key_start):
    params = tuple((item.astype(jnp.float32) for item in (w_qkv, q_bias, v_bias, w_out, out_bias, w_up, up_bias, w_down, down_bias, ln1_gain, ln1_bias, ln2_gain, ln2_bias)))
    zeros = jax.tree.map(jnp.zeros_like, params)

    def one_sequence(summed, item):
        sequence, upstream = item
        result, pull = jax.vjp(lambda weights, inputs: forward(weights, inputs, key_start), params, sequence.astype(jnp.float32))
        weight_grads, input_grads = pull(upstream.astype(jnp.float32))
        summed = jax.tree.map(lambda held, extra: held + extra, summed, weight_grads)
        return (summed, (result.astype(jnp.bfloat16), input_grads.astype(jnp.bfloat16)))
    summed, (outputs, input_grad) = lax.scan(one_sequence, zeros, (tokens, cotangent))
    return (outputs, input_grad, summed[0], summed[1], summed[2], summed[3], summed[4], summed[5], summed[6], summed[7], summed[8], summed[9], summed[10], summed[11], summed[12])
```

```python
import functools

import jax
import jax.numpy as jnp
from jax import lax
from jax.experimental import pallas as pl
from jax.experimental.pallas import tpu as pltpu
from jax.sharding import PartitionSpec as P

BLK = 512
EPSILON = 1e-05
LOG2E = 1.4426950408889634
BF16 = jnp.bfloat16
F32 = jnp.float32

NT=(((0,),(0,)),((),()))
TN=(((1,),(1,)),((),()))

def plan_tiles(meta, ks, own, load, n_slots, n_blocks, n_row, n_heads):
    for i in range(n_row): load[i]=0
    def level(lv,_):
        cost=n_blocks-lv
        def tile(t,_):
            slot=t//n_blocks; qb=t%n_blocks
            head=meta[0]+slot
            here=head<n_heads
            hd=jnp.minimum(head,n_heads-1)
            n=qb+1-ks[hd,qb]
            mask=jnp.where(slot==0,meta[2],jnp.where(slot==n_slots-1,meta[3],(1<<n_blocks)-1))
            here=jnp.logical_and(here,((mask>>qb)&1)==1)
            @pl.when(cost==n_blocks)
            def _(): own[t]=-1
            @pl.when(jnp.logical_and(here,n==cost))
            def _():
                best=load[0]; who=jnp.int32(0)
                for i in range(1,n_row):
                    less=load[i]<best
                    best=jnp.where(less,load[i],best); who=jnp.where(less,i,who)
                own[t]=who
                load[who]=best+cost
            return 0
        lax.fori_loop(0,n_slots*n_blocks,tile,0)
        return 0
    lax.fori_loop(0,n_blocks,level,0)

def fetch(pieces, whole, sems, row, n_row, width):
    copies=[]
    for i,p in enumerate(pieces):
        at=lax.rem(row+i,n_row)*width
        c=pltpu.make_async_copy(p, whole.at[...,pl.ds(pl.multiple_of(at,width),width)], sems.at[i])
        c.start(); copies.append(c)
    return copies

def fwd_kernel(n_row,n_slots,hd,n_heads,meta,ks,*refs):
    pieces=refs[:n_row]; o_ref,lse_ref,whole,own,load,sems=refs[n_row:]
    S=whole.shape[2]; nb=S//BLK; width=S//n_row
    row=meta[1]
    copies=fetch(pieces,whole,sems,row,n_row,width)
    plan_tiles(meta,ks,own,load,n_slots,nb,n_row,n_heads)
    o_ref[...]=jnp.zeros_like(o_ref)
    for c in copies: c.wait()
    c2=hd**-0.5*LOG2E
    diag=lax.broadcasted_iota(jnp.int32,(BLK,BLK),0)<=lax.broadcasted_iota(jnp.int32,(BLK,BLK),1)
    def tile(t,_):
        @pl.when(own[t]==row)
        def _():
            slot=t//nb; qb=t%nb
            first=ks[meta[0]+slot,qb]
            hs=pl.ds(pl.multiple_of(slot*hd,hd),hd)
            qs=pl.ds(pl.multiple_of(qb*BLK,BLK),BLK)
            q=whole[0,hs,qs]
            def scores(kb_ds):
                return lax.dot_general(whole[1,hs,kb_ds],q,NT,preferred_element_type=jnp.float32)
            s=jnp.where(diag,scores(qs),-1e30)
            m=jnp.max(s,axis=0,keepdims=True)
            p=jnp.exp2((s-m)*c2)
            l=jnp.sum(p,axis=0,keepdims=True)
            acc=jnp.dot(whole[2,hs,qs],p.astype(jnp.bfloat16),preferred_element_type=jnp.float32)
            def step(kb,carry):
                m,l,acc=carry
                kd=pl.ds(pl.multiple_of(kb*BLK,BLK),BLK)
                s=scores(kd)
                mn=jnp.maximum(m,jnp.max(s,axis=0,keepdims=True))
                a=jnp.exp2((m-mn)*c2)
                p=jnp.exp2((s-mn)*c2)
                l=l*a+jnp.sum(p,axis=0,keepdims=True)
                acc=acc*a+jnp.dot(whole[2,hs,kd],p.astype(jnp.bfloat16),preferred_element_type=jnp.float32)
                return mn,l,acc
            m,l,acc=lax.fori_loop(first,qb,step,(m,l,acc))
            o_ref[hs,qs]=(acc/l).astype(jnp.bfloat16)
            lse_ref[pl.ds(slot,1),qs]=m*c2+jnp.log2(l)
        return 0
    lax.fori_loop(0,n_slots*nb,tile,0)

def bwd_kernel(n_row,n_slots,hd,n_heads,meta,ks,*refs):
    pieces=refs[:n_row]; das=refs[n_row:2*n_row]
    o_ref,lse_ref,d_ref,whole,da,acc,own,load,sems,sems2=refs[2*n_row:]
    S=whole.shape[2]; nb=S//BLK; width=S//n_row
    row=meta[1]
    copies=fetch(pieces,whole,sems,row,n_row,width)+fetch(das,da,sems2,row,n_row,width)
    plan_tiles(meta,ks,own,load,n_slots,nb,n_row,n_heads)
    d_ref[0]=jnp.zeros_like(d_ref[0])
    acc[...]=jnp.zeros_like(acc)
    for c in copies: c.wait()
    scale=hd**-0.5; c2=scale*LOG2E
    diag=lax.broadcasted_iota(jnp.int32,(BLK,BLK),0)<=lax.broadcasted_iota(jnp.int32,(BLK,BLK),1)
    def tile(t,_):
        @pl.when(own[t]==row)
        def _():
            slot=t//nb; qb=t%nb
            first=ks[meta[0]+slot,qb]
            hs=pl.ds(pl.multiple_of(slot*hd,hd),hd)
            qs=pl.ds(pl.multiple_of(qb*BLK,BLK),BLK)
            q=whole[0,hs,qs]
            up=da[hs,qs]
            lse=lse_ref[pl.ds(slot,1),qs]
            delta=jnp.sum(up.astype(jnp.float32)*o_ref[hs,qs].astype(jnp.float32),axis=0,keepdims=True)
            def block(kd,masked):
                k=whole[1,hs,kd]
                s=lax.dot_general(k,q,NT,preferred_element_type=jnp.float32)
                p=jnp.exp2(s*c2-lse)
                if masked: p=jnp.where(diag,p,0.0)
                dp=lax.dot_general(whole[2,hs,kd],up,NT,preferred_element_type=jnp.float32)
                ds=(p*(dp-delta)).astype(jnp.bfloat16)
                acc[1,hs,kd]+=lax.dot_general(up,p.astype(jnp.bfloat16),TN,preferred_element_type=jnp.float32)
                acc[0,hs,kd]+=lax.dot_general(q,ds,TN,preferred_element_type=jnp.float32)
                return jnp.dot(k,ds,preferred_element_type=jnp.float32)
            dq=block(qs,True)
            dq=lax.fori_loop(first,qb,lambda kb,dq:dq+block(pl.ds(pl.multiple_of(kb*BLK,BLK),BLK),False),dq)
            d_ref[0,hs,qs]=(dq*scale).astype(jnp.bfloat16)
        return 0
    lax.fori_loop(0,n_slots*nb,tile,0)
    d_ref[1]=(acc[0]*scale).astype(jnp.bfloat16)
    d_ref[2]=acc[1].astype(jnp.bfloat16)

V=pl.BlockSpec(memory_space=pltpu.VMEM); SM=pl.BlockSpec(memory_space=pltpu.SMEM); ANY=pl.BlockSpec(memory_space=pl.ANY)
def attn_fwd(meta,ks,pieces,n_slots,hd):
    n_row=len(pieces); _,H,T=pieces[0].shape; S=T*n_row; nb=S//BLK
    return pl.pallas_call(functools.partial(fwd_kernel,n_row,n_slots,hd,ks.shape[0]),
      out_shape=(jax.ShapeDtypeStruct((H,S),jnp.bfloat16),jax.ShapeDtypeStruct((n_slots,S),jnp.float32)),
      in_specs=[SM,SM]+[ANY]*n_row,out_specs=(V,V),
      scratch_shapes=[pltpu.VMEM((3,H,S),jnp.bfloat16),pltpu.SMEM((n_slots*nb,),jnp.int32),pltpu.SMEM((n_row,),jnp.int32),pltpu.SemaphoreType.DMA((n_row,))],
      compiler_params=pltpu.CompilerParams(vmem_limit_bytes=48*2**20),
      cost_estimate=pl.CostEstimate(flops=4*3*S*S//2*H//2,bytes_accessed=10**7,transcendentals=S*S),
    )(meta,ks,*pieces)
def attn_bwd(meta,ks,pieces,das,o,lse,n_slots,hd):
    n_row=len(pieces); _,H,T=pieces[0].shape; S=T*n_row; nb=S//BLK
    return pl.pallas_call(functools.partial(bwd_kernel,n_row,n_slots,hd,ks.shape[0]),
      out_shape=jax.ShapeDtypeStruct((3,H,S),jnp.bfloat16),
      in_specs=[SM,SM]+[ANY]*(2*n_row)+[V,V],out_specs=V,
      scratch_shapes=[pltpu.VMEM((3,H,S),jnp.bfloat16),pltpu.VMEM((H,S),jnp.bfloat16),pltpu.VMEM((2,H,S),jnp.float32),pltpu.SMEM((n_slots*nb,),jnp.int32),pltpu.SMEM((n_row,),jnp.int32),pltpu.SemaphoreType.DMA((n_row,)),pltpu.SemaphoreType.DMA((n_row,))],
      compiler_params=pltpu.CompilerParams(vmem_limit_bytes=56*2**20),
      cost_estimate=pl.CostEstimate(flops=10*3*S*S//2*H//2,bytes_accessed=10**7,transcendentals=S*S),
    )(meta,ks,*pieces,*das,o,lse)


def dot(a, b):
    return jnp.dot(a, b, preferred_element_type=F32)


def dot_nt(a, b):
    return lax.dot_general(a, b, TN, preferred_element_type=F32)


def dot_tn(a, b):
    return lax.dot_general(a, b, NT, preferred_element_type=F32)


def turn(value, axis, steps):
    size = lax.axis_size(axis)
    if steps % size == 0:
        return value
    return lax.ppermute(value, axis, [(i, (i + steps) % size) for i in range(size)])


def block(value, index, size, axis):
    return lax.dynamic_slice_in_dim(value, index * size, size, axis)


def place(whole, part, index, axis):
    return lax.dynamic_update_slice_in_dim(whole, part, index * part.shape[axis], axis)


def row_gather(value, axis):
    size = lax.axis_size("row")
    if size != 2:
        return lax.all_gather(value, "row", axis=axis, tiled=True)
    other = turn(value, "row", 1)
    low = lax.axis_index("row") == 0
    return jnp.concatenate([jnp.where(low, value, other), jnp.where(low, other, value)], axis)


def row_sum(value, axis):
    size = lax.axis_size("row")
    part = value.shape[axis] // size
    row = lax.axis_index("row")
    total = block(value, row, part, axis).astype(F32)
    for step in range(1, size):
        sent = block(value, (row + step) % size, part, axis).astype(BF16)
        total = total + turn(sent, "row", step).astype(F32)
    return total


def col_sum(value, axis):
    size = lax.axis_size("col")
    part = value.shape[axis] // size
    col = lax.axis_index("col")
    total = block(value, col, part, axis).astype(F32)
    for step in range(1, size):
        sent = block(value, (col + step) % size, part, axis).astype(BF16)
        total = total + turn(sent, "col", step).astype(F32)
    return total


def col_swap(value, split, join):
    size = lax.axis_size("col")
    part = value.shape[split] // size
    col = lax.axis_index("col")
    shape = list(value.shape)
    shape[split] = part
    shape[join] *= size
    whole = jnp.zeros(shape, value.dtype)
    for step in range(size):
        sent = block(value, (col + step) % size, part, split)
        whole = place(whole, turn(sent, "col", step), (col - step) % size, join)
    return whole


def swap_with(value, bit):
    return lax.ppermute(value, "dp", [(i, i ^ bit) for i in range(4)])


def pick(value, index, axis):
    return lax.dynamic_index_in_dim(value, index, axis, keepdims=False)


def dp_sum(value, first):
    if lax.axis_size("dp") != 4:
        return lax.psum(value.astype(BF16), "dp").astype(F32)
    shape = value.shape
    me = lax.axis_index("dp")
    bits = (me % 2, me // 2)
    second = 1 - first
    halves = value.astype(BF16).reshape(2, 2, -1, shape[-1])
    mine, theirs = pick(halves, bits[first], 0), pick(halves, 1 - bits[first], 0)
    half = mine.astype(F32) + swap_with(theirs, 1 << first).astype(F32)
    mine, theirs = pick(half, bits[second], 0), pick(half, 1 - bits[second], 0)
    quarter = mine + swap_with(theirs.astype(BF16), 1 << second).astype(F32)
    quarter = quarter.astype(BF16)
    other = swap_with(quarter, 1 << second)
    low = bits[second] == 0
    half = jnp.stack([jnp.where(low, quarter, other), jnp.where(low, other, quarter)])
    other = swap_with(half, 1 << first)
    low = bits[first] == 0
    whole = jnp.stack([jnp.where(low, half, other), jnp.where(low, other, half)])
    return whole.reshape(shape).astype(F32)


def small_sum(value, axes):
    return lax.psum(value, axes)


class Heads:
    def __init__(self, n_col, width, heads, blocks):
        self.size = n_col * width // heads
        self.firsts = [width * c // self.size for c in range(n_col)]
        lasts = [-(-width * (c + 1) // self.size) for c in range(n_col)]
        self.slots = max(b - a for a, b in zip(self.firsts, lasts))
        self.window = self.slots * self.size
        self.before = [width * c - f * self.size for c, f in enumerate(self.firsts)]
        self.after = [self.window - width - b for b in self.before]
        self.edge = max(self.before + self.after)
        full = (1 << blocks) - 1
        shares = {0: 0, 1: 2, 2: 9, 3: 13, 4: 15}

        def left_share(column):
            part = column % self.size
            return shares[round(4 * part / self.size)] if blocks == 4 else 0

        self.first_mask = [full & ~left_share(b) for b in self.before]
        self.last_mask = []
        for c, f in enumerate(self.firsts):
            end = width * (c + 1)
            begin = (f + self.slots - 1) * self.size
            if begin >= end:
                self.last_mask.append(0)
            elif begin + self.size <= end:
                self.last_mask.append(full)
            else:
                self.last_mask.append(left_share(end - begin))


def widen(value, axis, heads, col):
    size = lax.axis_size("col")
    edge, width = heads.edge, value.shape[axis]
    up = [(i, i + 1) for i in range(size - 1)]
    down = [(i + 1, i) for i in range(size - 1)]
    left = lax.ppermute(lax.slice_in_dim(value, width - edge, width, axis=axis), "col", up)
    right = lax.ppermute(lax.slice_in_dim(value, 0, edge, axis=axis), "col", down)
    wide = jnp.concatenate([left, value, right], axis)
    before = jnp.array(heads.before, jnp.int32)[col]
    return lax.dynamic_slice_in_dim(wide, edge - before, heads.window, axis)


def narrow(value, axis, heads, col, width):
    size = lax.axis_size("col")
    edge = heads.edge
    up = [(i, i + 1) for i in range(size - 1)]
    down = [(i + 1, i) for i in range(size - 1)]
    before = jnp.array(heads.before, jnp.int32)[col]
    shape = list(value.shape)
    shape[axis] = width + 2 * edge
    wide = lax.dynamic_update_slice_in_dim(
        jnp.zeros(shape, value.dtype), value, edge - before, axis
    )
    to_left = lax.slice_in_dim(wide, 0, edge, axis=axis)
    to_right = lax.slice_in_dim(wide, edge + width, width + 2 * edge, axis=axis)
    tail = lax.ppermute(to_left, "col", down)
    front = lax.ppermute(to_right, "col", up)
    pads = [(0, 0)] * value.ndim
    pads[axis] = (0, width - edge)
    own = lax.slice_in_dim(wide, edge, edge + width, axis=axis).astype(F32)
    own = own + jnp.pad(front, pads).astype(F32)
    pads[axis] = (width - edge, 0)
    return own + jnp.pad(tail, pads).astype(F32)


def moments(values):
    mean = jnp.mean(values, axis=0, keepdims=True)
    centred = values - mean
    variance = jnp.mean(centred * centred, axis=0, keepdims=True)
    return mean, lax.rsqrt(variance + EPSILON)


def gelu_parts(u):
    inner = 0.7978845608 * (u + 0.044715 * u * u * u)
    t = jnp.tanh(inner)
    value = 0.5 * u * (1.0 + t)
    slope = 0.5 * (1.0 + t) + 0.5 * u * (1.0 - t * t) * 0.7978845608 * (1.0 + 0.134145 * u * u)
    return value, slope


def body(
    tokens,
    cotangent,
    w_qkv,
    q_bias,
    v_bias,
    w_out,
    out_bias,
    w_up,
    up_bias,
    w_down,
    down_bias,
    ln1_gain,
    ln1_bias,
    ln2_gain,
    ln2_bias,
    key_start,
):
    n_row, n_col = lax.axis_size("row"), lax.axis_size("col")
    row, col = lax.axis_index("row"), lax.axis_index("col")
    seqs, rows, width = tokens.shape
    length = seqs * rows
    depth = width * n_col
    part = length // n_col
    in_rows = w_up.shape[0]
    ff = w_up.shape[1]
    ff_rows = w_down.shape[0]
    ff_part = ff_rows // n_col
    heads = Heads(n_col, width, key_start.shape[0], rows * n_row // BLK)
    size, window = heads.size, heads.window
    firsts = jnp.array(heads.firsts, jnp.int32) * size
    begin = firsts[col]

    x = tokens.reshape(length, width).T
    g = cotangent.reshape(length, width).T

    x_all = lax.all_gather(x, "col", axis=0, tiled=True)
    params = jnp.stack([ln1_gain, ln1_bias, ln2_gain, ln2_bias, out_bias, q_bias, v_bias])
    params = lax.all_gather(params, "col", axis=1, tiled=True)
    gain1, shift1, gain2, shift2, bias_out, bias_q, bias_v = [p[:, None] for p in params]

    w3 = row_gather(widen(w_qkv.transpose(0, 2, 1), 1, heads, col), 2)
    w3 = w3.reshape(3 * window, depth)
    up_all = row_gather(w_up, 0)
    out_all = lax.all_gather(w_out.T, "col", axis=0, tiled=True)
    out_all = row_gather(out_all, 1)
    down_own = w_down.T
    down_part = jnp.zeros((depth, ff_part), BF16)
    for step in range(n_col):
        pairs = []
        for r in range(n_row):
            for c in range(n_col):
                at = r * n_col + (step + c) % n_col
                pairs.append((r * n_col + c, (at % n_row) * n_col + at // n_row))
        sent = block(down_own, (step + col) % n_col, ff_part, 1)
        got = lax.ppermute(sent, ("row", "col"), pairs)
        at = col * n_row + row
        down_part = place(down_part, got, (at % n_col - step) % n_col, 0)
    down_all = row_gather(down_part, 1)

    g_source, unused = lax.optimization_barrier((g, x_all))
    g_all = lax.all_gather(g_source, "col", axis=0, tiled=True)

    x_float = x_all.astype(F32)
    mean1, rstd1 = moments(x_float)
    n1 = ((x_float - mean1) * rstd1 * gain1 + shift1).astype(BF16)
    bias3 = jnp.concatenate(
        [
            lax.dynamic_slice_in_dim(bias_q, begin, window, 0),
            jnp.zeros((window, 1), F32),
            lax.dynamic_slice_in_dim(bias_v, begin, window, 0),
        ]
    )
    qkv = (dot(w3, n1) + bias3).astype(BF16)
    triple = qkv.reshape(3, window, length)
    pieces = [turn(triple, "row", -step) for step in range(n_row)]
    meta = jnp.stack(
        [
            jnp.array(heads.firsts, jnp.int32)[col],
            row,
            jnp.array(heads.first_mask, jnp.int32)[col],
            jnp.array(heads.last_mask, jnp.int32)[col],
        ]
    )
    mixed, norms = attn_fwd(meta, key_start, pieces, heads.slots, size)
    mixed_own = row_sum(mixed, 1).astype(BF16)

    attention = jnp.zeros((depth, part), BF16)
    for step in range(n_col):
        sent = block(mixed_own, (col + step) % n_col, part, 1)
        got = turn(sent, "col", step)
        at = firsts[(col - step) % n_col]
        held = lax.dynamic_slice_in_dim(attention, at, window, 0)
        attention = lax.dynamic_update_slice_in_dim(attention, held + got, at, 0)
    resid = block(x_all, col, part, 1).astype(F32) + (dot(out_all, attention) + bias_out)
    mean2, rstd2 = moments(resid)
    hat2 = (resid - mean2) * rstd2
    n2_own = (hat2 * gain2 + shift2).astype(BF16)

    n2s, gs, hiddens, dus, parts2 = [], [], [], [], []
    summed = jnp.zeros((depth, length), BF16)
    for step in range(n_col):
        at = (col - step) % n_col
        n2 = turn(n2_own, "col", step)
        g_here = block(g_all, at, part, 1)
        u = dot_tn(up_all, n2) + up_bias[:, None]
        value, slope = gelu_parts(u)
        hidden = value.astype(BF16)
        shrunk = dot(down_all, hidden)
        if step == 0:
            shrunk = shrunk + resid
        summed = place(summed, shrunk.astype(BF16), at, 1)
        du = (dot_tn(down_all, g_here) * slope).astype(BF16)
        parts2.append(turn(dot(up_all, du).astype(BF16), "col", -step).astype(F32))
        n2s.append(n2)
        gs.append(g_here)
        hiddens.append(hidden)
        dus.append(du)
    outputs = col_sum(summed, 0) + down_bias[:, None]
    outputs = outputs.astype(BF16)

    dn2 = sum(parts2)
    up2 = dn2 * gain2
    pull2 = jnp.mean(up2, axis=0, keepdims=True)
    lean2 = jnp.mean(up2 * hat2, axis=0, keepdims=True)
    dr = gs[0].astype(F32) + rstd2 * (up2 - pull2 - hat2 * lean2)
    db = dr.astype(BF16)
    da = dot_tn(out_all, db).astype(BF16)
    da_own = jnp.zeros((window, length), BF16)
    for step in range(n_col):
        to = firsts[(col + step) % n_col]
        got = turn(lax.dynamic_slice_in_dim(da, to, window, 0), "col", step)
        da_own = place(da_own, got, (col - step) % n_col, 1)
    da_pieces = [turn(da_own, "row", -step) for step in range(n_row)]
    dqkv = attn_bwd(meta, key_start, pieces, da_pieces, mixed, norms, heads.slots, size)
    dqkv = row_sum(dqkv, 2).astype(BF16).reshape(3 * window, length)

    dn1_part = dot_tn(w3, dqkv).astype(BF16)
    dqkv_float = dqkv.astype(F32)
    weighed = dot(w3, gain1.astype(F32))
    plain = qkv.astype(F32) - (bias3 + dot(w3, shift1))
    stats = jnp.stack(
        [jnp.sum(dqkv_float * weighed, axis=0), jnp.sum(dqkv_float * plain, axis=0)]
    )
    stats = sum(turn(stats, "col", step) for step in range(n_col)) / depth
    dn1 = col_sum(dn1_part, 0)
    hat1 = (x.astype(F32) - mean1) * rstd1
    gain1_own = ln1_gain[:, None]
    dx = rstd1 * (dn1 * gain1_own - stats[0:1] - hat1 * stats[1:2])
    input_grad = (col_swap(db, 0, 1).astype(F32) + dx).astype(BF16)

    n2_all = jnp.concatenate(n2s, 1)
    g_turned = jnp.concatenate(gs, 1)
    hidden_all = jnp.concatenate(hiddens, 1)
    du_all = jnp.concatenate(dus, 1)
    up_grad = dp_sum(row_sum(dot_nt(n2_all, du_all).astype(BF16), 0), 0)
    down_grad = row_sum(dot_nt(g_turned, hidden_all).astype(BF16), 1).astype(BF16)
    down_home = jnp.zeros((width, ff_rows), BF16)
    for step in range(n_col):
        pairs = []
        for r in range(n_row):
            for c in range(n_col):
                at = r * n_col + (step + c) % n_col
                pairs.append(((at % n_row) * n_col + at // n_row, r * n_col + c))
        at = col * n_row + row
        sent = block(down_grad, (at % n_col - step) % n_col, width, 0)
        got = lax.ppermute(sent, ("row", "col"), pairs)
        down_home = place(down_home, got, (step + col) % n_col, 1)
    down_grad = dp_sum(down_home, 1)
    out_grad = dp_sum(col_sum(row_sum(dot_nt(db, attention).astype(BF16), 1).astype(BF16), 0), 0)
    qkv_grad = row_sum(dot_nt(dqkv, n1).astype(BF16).reshape(3, window, depth), 2)
    qkv_grad = dp_sum(narrow(qkv_grad.astype(BF16), 1, heads, col, width), 1)

    spread = jnp.zeros((2, depth), F32)
    dq_dv = jnp.sum(dqkv_float.reshape(3, window, length), axis=2)
    spread = lax.dynamic_update_slice_in_dim(spread, dq_dv[::2], begin, 1)
    everywhere = jnp.stack(
        [
            jnp.sum(db.astype(F32), axis=1),
            jnp.sum(dn2 * hat2, axis=1),
            jnp.sum(dn2, axis=1),
        ]
    )
    early = small_sum(jnp.concatenate([spread, everywhere]), ("dp", "row", "col"))
    early = lax.dynamic_slice_in_dim(early, col * width, width, 1)
    up_bias_grad = small_sum(jnp.sum(du_all.astype(F32), axis=1), ("dp", "row"))
    late = jnp.stack(
        [jnp.sum(g.astype(F32), axis=1), jnp.sum(dn1 * hat1, axis=1), jnp.sum(dn1, axis=1)]
    )
    late = small_sum(late, ("dp", "row"))
    return (
        outputs.T.reshape(tokens.shape),
        input_grad.T.reshape(tokens.shape),
        qkv_grad.transpose(0, 2, 1),
        early[0],
        early[1],
        out_grad.T,
        early[2],
        up_grad,
        up_bias_grad,
        down_grad.T,
        late[0],
        late[1],
        late[2],
        early[3],
        early[4],
    )


def solution(mesh):
    inputs = (
        P("dp", "row", "col"),
        P("dp", "row", "col"),
        P(None, "row", "col"),
        P("col"),
        P("col"),
        P("row", "col"),
        P("col"),
        P("row", "col"),
        P("col"),
        P("row", "col"),
        P("col"),
        P("col"),
        P("col"),
        P("col"),
        P("col"),
        P(),
    )
    return jax.shard_map(
        body, mesh=mesh, in_specs=inputs, out_specs=inputs[:15], check_vma=False
    )
```

```python
import functools

import jax
import jax.numpy as jnp
from jax import lax
from jax.experimental import pallas as pl
from jax.experimental.pallas import tpu as pltpu
from jax.sharding import PartitionSpec as P

BLK = 512
EPSILON = 1e-05
LOG2E = 1.4426950408889634
BF16 = jnp.bfloat16
F32 = jnp.float32

FREE = pl.CostEstimate(flops=0, bytes_accessed=0, transcendentals=0)
ROOM = pltpu.CompilerParams(vmem_limit_bytes=56 * 2**20)

NT=(((0,),(0,)),((),()))
TN=(((1,),(1,)),((),()))

def plan_tiles(meta, ks, own, load, n_slots, n_blocks, n_row, n_heads):
    for i in range(n_row): load[i]=0
    def level(lv,_):
        cost=n_blocks-lv
        def tile(t,_):
            slot=t//n_blocks; qb=t%n_blocks
            head=meta[0]+slot
            here=head<n_heads
            hd=jnp.minimum(head,n_heads-1)
            n=qb+1-ks[hd,qb]
            mask=jnp.where(slot==0,meta[2],jnp.where(slot==n_slots-1,meta[3],(1<<n_blocks)-1))
            here=jnp.logical_and(here,((mask>>qb)&1)==1)
            @pl.when(cost==n_blocks)
            def _(): own[t]=-1
            @pl.when(jnp.logical_and(here,n==cost))
            def _():
                best=load[0]; who=jnp.int32(0)
                for i in range(1,n_row):
                    less=load[i]<best
                    best=jnp.where(less,load[i],best); who=jnp.where(less,i,who)
                own[t]=who
                load[who]=best+cost
            return 0
        lax.fori_loop(0,n_slots*n_blocks,tile,0)
        return 0
    lax.fori_loop(0,n_blocks,level,0)

def fetch(pieces, whole, sems, row, n_row, width):
    copies=[]
    for i,p in enumerate(pieces):
        at=lax.rem(row+i,n_row)*width
        c=pltpu.make_async_copy(p, whole.at[...,pl.ds(pl.multiple_of(at,width),width)], sems.at[i])
        c.start(); copies.append(c)
    return copies

def fwd_kernel(n_row,n_slots,hd,n_heads,meta,ks,*refs):
    pieces=refs[:n_row]; cuts=refs[n_row:2*n_row]; o_ref,lse_ref,whole,own,load,sems=refs[2*n_row:]
    S=whole.shape[2]; nb=S//BLK; width=S//n_row
    row=meta[1]
    copies=fetch(pieces,whole,sems,row,n_row,width)
    plan_tiles(meta,ks,own,load,n_slots,nb,n_row,n_heads)
    o_ref[...]=jnp.zeros_like(o_ref)
    for c in copies: c.wait()
    c2=hd**-0.5*LOG2E
    diag=lax.broadcasted_iota(jnp.int32,(BLK,BLK),0)<=lax.broadcasted_iota(jnp.int32,(BLK,BLK),1)
    def tile(t,_):
        @pl.when(own[t]==row)
        def _():
            slot=t//nb; qb=t%nb
            first=ks[meta[0]+slot,qb]
            hs=pl.ds(pl.multiple_of(slot*hd,hd),hd)
            qs=pl.ds(pl.multiple_of(qb*BLK,BLK),BLK)
            q=whole[0,hs,qs]
            def scores(kb_ds):
                return lax.dot_general(whole[1,hs,kb_ds],q,NT,preferred_element_type=jnp.float32)
            s=jnp.where(diag,scores(qs),-1e30)
            m=jnp.max(s,axis=0,keepdims=True)
            p=jnp.exp2((s-m)*c2)
            l=jnp.sum(p,axis=0,keepdims=True)
            acc=jnp.dot(whole[2,hs,qs],p.astype(jnp.bfloat16),preferred_element_type=jnp.float32)
            def step(kb,carry):
                m,l,acc=carry
                kd=pl.ds(pl.multiple_of(kb*BLK,BLK),BLK)
                s=scores(kd)
                mn=jnp.maximum(m,jnp.max(s,axis=0,keepdims=True))
                a=jnp.exp2((m-mn)*c2)
                p=jnp.exp2((s-mn)*c2)
                l=l*a+jnp.sum(p,axis=0,keepdims=True)
                acc=acc*a+jnp.dot(whole[2,hs,kd],p.astype(jnp.bfloat16),preferred_element_type=jnp.float32)
                return mn,l,acc
            m,l,acc=lax.fori_loop(first,qb,step,(m,l,acc))
            o_ref[hs,qs]=(acc/l).astype(jnp.bfloat16)
            lse_ref[pl.ds(slot,1),qs]=m*c2+jnp.log2(l)
        return 0
    lax.fori_loop(0,n_slots*nb,tile,0)
    for i,cut in enumerate(cuts):
        cut[...]=o_ref[:,pl.ds(pl.multiple_of(lax.rem(row+i,n_row)*width,width),width)]

def bwd_kernel(n_row,n_slots,hd,n_heads,meta,ks,*refs):
    pieces=refs[:n_row]; das=refs[n_row:2*n_row]
    o_ref,lse_ref=refs[2*n_row:2*n_row+2]; cuts=refs[2*n_row+2:3*n_row+2]
    d_ref,whole,da,acc,own,load,sems,sems2=refs[3*n_row+2:]
    S=whole.shape[2]; nb=S//BLK; width=S//n_row
    row=meta[1]
    copies=fetch(pieces,whole,sems,row,n_row,width)+fetch(das,da,sems2,row,n_row,width)
    plan_tiles(meta,ks,own,load,n_slots,nb,n_row,n_heads)
    d_ref[...]=jnp.zeros_like(d_ref)
    acc[...]=jnp.zeros_like(acc)
    for c in copies: c.wait()
    scale=hd**-0.5; c2=scale*LOG2E
    diag=lax.broadcasted_iota(jnp.int32,(BLK,BLK),0)<=lax.broadcasted_iota(jnp.int32,(BLK,BLK),1)
    def tile(t,_):
        @pl.when(own[t]==row)
        def _():
            slot=t//nb; qb=t%nb
            first=ks[meta[0]+slot,qb]
            hs=pl.ds(pl.multiple_of(slot*hd,hd),hd)
            qs=pl.ds(pl.multiple_of(qb*BLK,BLK),BLK)
            q=whole[0,hs,qs]
            up=da[hs,qs]
            lse=lse_ref[pl.ds(slot,1),qs]
            delta=jnp.sum(up.astype(jnp.float32)*o_ref[hs,qs].astype(jnp.float32),axis=0,keepdims=True)
            def block(kd,masked):
                k=whole[1,hs,kd]
                s=lax.dot_general(k,q,NT,preferred_element_type=jnp.float32)
                p=jnp.exp2(s*c2-lse)
                if masked: p=jnp.where(diag,p,0.0)
                dp=lax.dot_general(whole[2,hs,kd],up,NT,preferred_element_type=jnp.float32)
                ds=(p*(dp-delta)).astype(jnp.bfloat16)
                acc[1,hs,kd]+=lax.dot_general(up,p.astype(jnp.bfloat16),TN,preferred_element_type=jnp.float32)
                acc[0,hs,kd]+=lax.dot_general(q,ds,TN,preferred_element_type=jnp.float32)
                return jnp.dot(k,ds,preferred_element_type=jnp.float32)
            dq=block(qs,True)
            dq=lax.fori_loop(first,qb,lambda kb,dq:dq+block(pl.ds(pl.multiple_of(kb*BLK,BLK),BLK),False),dq)
            d_ref[hs,qs]=(dq*scale).astype(jnp.bfloat16)
        return 0
    lax.fori_loop(0,n_slots*nb,tile,0)
    for i,cut in enumerate(cuts):
        at=pl.ds(pl.multiple_of(lax.rem(row+i,n_row)*width,width),width)
        cut[0]=d_ref[:,at]
        cut[1]=(acc[0,:,at]*scale).astype(jnp.bfloat16)
        cut[2]=acc[1,:,at].astype(jnp.bfloat16)

V=pl.BlockSpec(memory_space=pltpu.VMEM); SM=pl.BlockSpec(memory_space=pltpu.SMEM); ANY=pl.BlockSpec(memory_space=pl.ANY)
def attn_fwd(meta,ks,pieces,n_slots,hd):
    n_row=len(pieces); _,H,T=pieces[0].shape; S=T*n_row; nb=S//BLK
    return pl.pallas_call(functools.partial(fwd_kernel,n_row,n_slots,hd,ks.shape[0]),
      out_shape=[jax.ShapeDtypeStruct((H,T),jnp.bfloat16)]*n_row+[jax.ShapeDtypeStruct((H,S),jnp.bfloat16),jax.ShapeDtypeStruct((n_slots,S),jnp.float32)],
      in_specs=[SM,SM]+[ANY]*n_row,out_specs=[V]*(n_row+2),
      scratch_shapes=[pltpu.VMEM((3,H,S),jnp.bfloat16),pltpu.SMEM((n_slots*nb,),jnp.int32),pltpu.SMEM((n_row,),jnp.int32),pltpu.SemaphoreType.DMA((n_row,))],
      compiler_params=pltpu.CompilerParams(vmem_limit_bytes=48*2**20),
      cost_estimate=FREE,
    )(meta,ks,*pieces)
def attn_bwd(meta,ks,pieces,das,o,lse,n_slots,hd):
    n_row=len(pieces); _,H,T=pieces[0].shape; S=T*n_row; nb=S//BLK
    return pl.pallas_call(functools.partial(bwd_kernel,n_row,n_slots,hd,ks.shape[0]),
      out_shape=[jax.ShapeDtypeStruct((3,H,T),jnp.bfloat16)]*n_row,
      in_specs=[SM,SM]+[ANY]*(2*n_row)+[V,V],out_specs=[V]*n_row,
      scratch_shapes=[pltpu.VMEM((H,S),jnp.bfloat16),pltpu.VMEM((3,H,S),jnp.bfloat16),pltpu.VMEM((H,S),jnp.bfloat16),pltpu.VMEM((2,H,S),jnp.float32),pltpu.SMEM((n_slots*nb,),jnp.int32),pltpu.SMEM((n_row,),jnp.int32),pltpu.SemaphoreType.DMA((n_row,)),pltpu.SemaphoreType.DMA((n_row,))],
      compiler_params=pltpu.CompilerParams(vmem_limit_bytes=56*2**20),
      cost_estimate=FREE,
    )(meta,ks,*pieces,*das,o,lse)


def rows_of(total, most):
    for rows in range(min(total, most) // 16 * 16, 0, -16):
        if total % rows == 0:
            return rows
    return total


def by_rows(i, *refs):
    return (i, 0)


def whole_block(i, *refs):
    return (0, 0)


def product_kernel(a_ref, b_ref, bias_ref, o_ref):
    o_ref[...] = (
        jnp.dot(a_ref[...], b_ref[...], preferred_element_type=F32) + bias_ref[...]
    ).astype(o_ref.dtype)


def product(a, b, bias):
    rows = rows_of(a.shape[0], 448)
    return pl.pallas_call(
        product_kernel,
        out_shape=jax.ShapeDtypeStruct((a.shape[0], b.shape[1]), BF16),
        grid=(a.shape[0] // rows,),
        in_specs=[
            pl.BlockSpec((rows, a.shape[1]), by_rows),
            pl.BlockSpec(b.shape, whole_block),
            pl.BlockSpec((rows, 1), by_rows),
        ],
        out_specs=pl.BlockSpec((rows, b.shape[1]), by_rows),
        compiler_params=ROOM,
        cost_estimate=FREE,
    )(a, b, bias)


def split_product(parts, b, row, bias, dtype):
    n = len(parts)
    total, depth = parts[0].shape
    width = b.shape[1]
    rows = rows_of(total, 400)

    def kernel(row_ref, b_ref, bias_ref, *refs):
        out = bias_ref[...] + jnp.zeros((rows, width), F32)
        for i in range(n):
            at = pl.multiple_of(lax.rem(row_ref[0] + i, n) * depth, 8)
            out = out + jnp.dot(refs[i][...], b_ref[pl.ds(at, depth), :], preferred_element_type=F32)
        refs[n][...] = out.astype(dtype)

    return pl.pallas_call(
        kernel,
        out_shape=jax.ShapeDtypeStruct((total, width), dtype),
        grid=(total // rows,),
        in_specs=[SM, pl.BlockSpec(b.shape, whole_block), pl.BlockSpec((rows, 1), by_rows)]
        + [pl.BlockSpec((rows, depth), by_rows)] * n,
        out_specs=pl.BlockSpec((rows, width), by_rows),
        compiler_params=ROOM,
        cost_estimate=FREE,
    )(row, b, bias, *parts)


def split_product_tn(parts, b, row):
    n = len(parts)
    depth = parts[0].shape[1]
    total, width = b.shape
    rows = rows_of(total, 400)
    steps = total // rows

    def kernel(row_ref, b_ref, *refs):
        o_ref, acc = refs[n:]

        @pl.when(pl.program_id(0) == 0)
        def start():
            acc[...] = jnp.zeros_like(acc)

        for i in range(n):
            at = pl.multiple_of(lax.rem(row_ref[0] + i, n) * depth, 8)
            acc[pl.ds(at, depth), :] += lax.dot_general(
                refs[i][...], b_ref[...], NT, preferred_element_type=F32
            )

        @pl.when(pl.program_id(0) == steps - 1)
        def end():
            o_ref[...] = acc[...].astype(BF16)

    return pl.pallas_call(
        kernel,
        out_shape=jax.ShapeDtypeStruct((n * depth, width), BF16),
        grid=(steps,),
        in_specs=[SM, pl.BlockSpec((rows, width), by_rows)]
        + [pl.BlockSpec((rows, depth), by_rows)] * n,
        out_specs=pl.BlockSpec((n * depth, width), whole_block),
        scratch_shapes=[pltpu.VMEM((n * depth, width), F32)],
        compiler_params=ROOM,
        cost_estimate=FREE,
    )(row, b, *parts)


def norm_product_tn(a, b, normed, gain, shift, scale):
    rows = rows_of(a.shape[0], 448)
    steps = a.shape[0] // rows
    depth, tokens = a.shape[1], b.shape[1]
    cut = rows_of(depth, 400)

    def kernel(a_ref, b_ref, n_ref, g_ref, s_ref, c_ref, o_ref, t_ref, f_ref, acc):
        @pl.when(pl.program_id(0) == 0)
        def start():
            acc[...] = lax.dot_general(a_ref[...], b_ref[...], NT, preferred_element_type=F32)

        @pl.when(pl.program_id(0) > 0)
        def more():
            acc[...] += lax.dot_general(a_ref[...], b_ref[...], NT, preferred_element_type=F32)

        @pl.when(pl.program_id(0) == steps - 1)
        def end():
            t_ref[...] = jnp.zeros_like(t_ref)
            for first in range(0, depth, cut):
                at = pl.ds(first, cut)
                p = acc[at, :]
                scaled = p * g_ref[at, :]
                o_ref[at, :] = (scaled * c_ref[...]).astype(BF16)
                moved = p * (n_ref[at, :].astype(F32) - s_ref[at, :])
                t_ref[0:1, :] += jnp.sum(scaled, axis=0, keepdims=True)
                t_ref[1:2, :] += jnp.sum(moved, axis=0, keepdims=True)
                f_ref[at, 0:1] = jnp.sum(moved, axis=1, keepdims=True)
                f_ref[at, 1:2] = jnp.sum(p, axis=1, keepdims=True)

    return pl.pallas_call(
        kernel,
        out_shape=[
            jax.ShapeDtypeStruct((depth, tokens), BF16),
            jax.ShapeDtypeStruct((2, tokens), F32),
            jax.ShapeDtypeStruct((depth, 2), F32),
        ],
        grid=(steps,),
        in_specs=[
            pl.BlockSpec((rows, depth), by_rows),
            pl.BlockSpec((rows, tokens), by_rows),
            pl.BlockSpec((depth, tokens), whole_block),
            pl.BlockSpec((depth, 1), whole_block),
            pl.BlockSpec((depth, 1), whole_block),
            pl.BlockSpec((1, tokens), whole_block),
        ],
        out_specs=[
            pl.BlockSpec((depth, tokens), whole_block),
            pl.BlockSpec((2, tokens), whole_block),
            pl.BlockSpec((depth, 2), whole_block),
        ],
        scratch_shapes=[pltpu.VMEM((depth, tokens), F32)],
        compiler_params=ROOM,
        cost_estimate=FREE,
    )(a, b, normed, gain, shift, scale)


def token_product(a, b, index, parts, of_a):
    rows_a = a.shape[0] // (parts if of_a else 1)
    rows_b = b.shape[0] // (1 if of_a else parts)
    rows = rows_of(rows_a, 448)
    steps = rows_a // rows

    def kernel(index_ref, a_ref, b_ref, o_ref):
        o_ref[...] = lax.dot_general(
            a_ref[...], b_ref[...], TN, preferred_element_type=F32
        ).astype(BF16)

    if of_a:
        a_map, b_map = (lambda i, r: (r[0] * steps + i, 0)), whole_block
    else:
        a_map, b_map = by_rows, (lambda i, r: (r[0], 0))
    return pl.pallas_call(
        kernel,
        out_shape=jax.ShapeDtypeStruct((rows_a, rows_b), BF16),
        grid_spec=pltpu.PrefetchScalarGridSpec(
            num_scalar_prefetch=1,
            grid=(steps,),
            in_specs=[
                pl.BlockSpec((rows, a.shape[1]), a_map),
                pl.BlockSpec((rows_b, b.shape[1]), b_map),
            ],
            out_specs=pl.BlockSpec((rows, rows_b), by_rows),
        ),
        compiler_params=ROOM,
        cost_estimate=FREE,
    )(index, a, b)


def gelu_parts(u):
    inner = 0.7978845608 * (u + 0.044715 * u * u * u)
    t = jnp.tanh(inner)
    value = 0.5 * u * (1.0 + t)
    slope = 0.5 * (1.0 + t) + 0.5 * u * (1.0 - t * t) * 0.7978845608 * (1.0 + 0.134145 * u * u)
    return value, slope


def hidden_layer(up, down, n, bias, n2, g, row):
    ff, depth = up.shape
    tokens = n2.shape[1]
    rows = rows_of(ff // n, 400)
    cuts = ff // n // rows
    steps = ff // rows

    def kernel(row_ref, up_ref, down_ref, bias_ref, n_ref, g_ref, h_ref, d_ref, p_ref, acc):
        step = pl.program_id(0)
        u = jnp.dot(up_ref[...], n_ref[...], preferred_element_type=F32) + bias_ref[...]
        value, slope = gelu_parts(u)
        h_ref[...] = value.astype(BF16)
        dh = jnp.dot(down_ref[...], g_ref[...], preferred_element_type=F32)
        du = (dh * slope).astype(BF16)
        d_ref[...] = du

        @pl.when(step == 0)
        def start():
            acc[...] = lax.dot_general(up_ref[...], du, NT, preferred_element_type=F32)

        @pl.when(step > 0)
        def more():
            acc[...] += lax.dot_general(up_ref[...], du, NT, preferred_element_type=F32)

        @pl.when(step == steps - 1)
        def end():
            p_ref[...] = acc[...].astype(BF16)

    mine = lambda i, r: (lax.rem(r[0] * cuts + i, steps), 0)
    full = lambda i, r: (0, 0)
    return pl.pallas_call(
        kernel,
        out_shape=[
            jax.ShapeDtypeStruct((ff, tokens), BF16),
            jax.ShapeDtypeStruct((ff, tokens), BF16),
            jax.ShapeDtypeStruct((depth, tokens), BF16),
        ],
        grid_spec=pltpu.PrefetchScalarGridSpec(
            num_scalar_prefetch=1,
            grid=(steps,),
            in_specs=[
                pl.BlockSpec((rows, depth), mine),
                pl.BlockSpec((rows, depth), lambda i, r: (i, 0)),
                pl.BlockSpec((rows, 1), mine),
                pl.BlockSpec((depth, tokens), full),
                pl.BlockSpec((depth, tokens), full),
            ],
            out_specs=[
                pl.BlockSpec((rows, tokens), mine),
                pl.BlockSpec((rows, tokens), mine),
                pl.BlockSpec((depth, tokens), full),
            ],
            scratch_shapes=[pltpu.VMEM((depth, tokens), F32)],
        ),
        compiler_params=ROOM,
        cost_estimate=FREE,
    )(row, up, down, bias, n2, g)


def gate(values, others):
    def kernel(*refs):
        pass

    out = pl.pallas_call(
        kernel,
        out_shape=[jax.ShapeDtypeStruct(v.shape, v.dtype) for v in values],
        in_specs=[ANY] * (len(values) + len(others)),
        out_specs=[ANY] * len(values),
        input_output_aliases={i: i for i in range(len(values))},
        cost_estimate=FREE,
    )(*values, *others)
    return list(out)


def turn(value, axis, steps):
    size = lax.axis_size(axis)
    if steps % size == 0:
        return value
    return lax.ppermute(value, axis, [(i, (i + steps) % size) for i in range(size)])


def block(value, index, size, axis):
    return lax.dynamic_slice_in_dim(value, index * size, size, axis)


def row_sum(parts):
    total = parts[0].astype(F32)
    for step in range(1, len(parts)):
        total = total + turn(parts[step], "row", step).astype(F32)
    return total


def swap_with(value, bit):
    return lax.ppermute(value, "dp", [(i, i ^ bit) for i in range(4)])


def pick(value, index, axis=0):
    return lax.dynamic_index_in_dim(value, index, axis, keepdims=False)


def dot(a, b):
    return jnp.dot(a, b, preferred_element_type=F32)


def ordered(parts, base, sign):
    size = len(parts)
    stacked = jnp.stack(parts)
    return [pick(stacked, (sign * (j - base)) % size) for j in range(size)]


class Shares:
    def __init__(self, rows):
        self.rows = rows
        self.size = -(-rows // 64) * 16
        self.starts = [(rows - self.size) * s // 48 * 16 for s in range(3)] + [rows - self.size]
        ends = self.starts[1:] + [rows]
        self.lengths = [b - a for a, b in zip(self.starts, ends)]

    def take(self, value, share, axis):
        start = jnp.array(self.starts, jnp.int32)[share]
        return lax.dynamic_slice_in_dim(value, start, self.size, axis)

    def join(self, parts, me, axis):
        stacked = jnp.stack(parts)
        laid = [
            lax.slice_in_dim(pick(stacked, me ^ s), 0, self.lengths[s], axis=axis)
            for s in range(4)
        ]
        return jnp.concatenate(laid, axis)


def assemble(parts, shares, me):
    n, wide = parts[0].shape[0], parts[0].shape[2]

    def kernel(me_ref, *refs):
        o_ref, sems = refs[-2:]
        for act in ("start", "wait"):
            for m in range(4):
                for s in range(4):

                    @pl.when(me_ref[0] ^ m == s)
                    def move():
                        rows = pl.ds(0, shares.lengths[s])
                        to = pl.ds(shares.starts[s], shares.lengths[s])
                        pairs = [(refs[m].at[:, rows], o_ref.at[:, to])]
                        if m == 3:
                            low, high = pl.ds(0, n // 2), pl.ds(n // 2, n // 2)
                            pairs = [
                                (refs[3].at[:, rows], o_ref.at[low, to]),
                                (refs[4].at[:, rows], o_ref.at[high, to]),
                            ]
                        for k, (source, target) in enumerate(pairs):
                            copy = pltpu.make_async_copy(source, target, sems.at[m + k])
                            getattr(copy, act)()

    return pl.pallas_call(
        kernel,
        out_shape=jax.ShapeDtypeStruct((n, shares.rows, wide), parts[0].dtype),
        in_specs=[SM] + [ANY] * 5,
        out_specs=V,
        scratch_shapes=[pltpu.SemaphoreType.DMA((5,))],
        compiler_params=ROOM,
        cost_estimate=FREE,
    )(me, *parts)


def small_sum(value, axes):
    for axis in axes:
        size = lax.axis_size(axis)
        if size & (size - 1):
            value = lax.psum(value, axis)
            continue
        bit = 1
        while bit < size:
            value = value + lax.ppermute(value, axis, [(i, i ^ bit) for i in range(size)])
            bit *= 2
    return value


def go_up(value, first, last):
    return lax.ppermute(value, "col", [(i, i + 1) for i in range(first, last + 1)])


def go_down(value, first, last):
    return lax.ppermute(value, "col", [(i, i - 1) for i in range(first, last + 1)])


def row_join(parts, axis):
    row = lax.axis_index("row")
    if len(parts) == 2:
        low = row == 0
        parts = [jnp.where(low, parts[0], parts[1]), jnp.where(low, parts[1], parts[0])]
    else:
        parts = ordered(parts, row, 1)
    return jnp.concatenate(parts, axis)


def swap_all(value):
    return [swap_with(value, 1), swap_with(value, 2), swap_with(value, 3)]


class Heads:
    def __init__(self, n_col, width, heads, blocks):
        self.size = n_col * width // heads
        self.firsts = [width * c // self.size for c in range(n_col)]
        lasts = [-(-width * (c + 1) // self.size) for c in range(n_col)]
        self.slots = max(b - a for a, b in zip(self.firsts, lasts))
        self.window = self.slots * self.size
        self.before = [width * c - f * self.size for c, f in enumerate(self.firsts)]
        self.after = [self.window - width - b for b in self.before]
        self.edge = max(self.before + self.after)
        full = (1 << blocks) - 1
        shares = {0: 0, 1: 2, 2: 9, 3: 13, 4: 15}

        def left_share(column):
            part = column % self.size
            return shares[round(4 * part / self.size)] if blocks == 4 else 0

        self.first_mask = [full & ~left_share(b) for b in self.before]
        self.last_mask = []
        for c, f in enumerate(self.firsts):
            end = width * (c + 1)
            begin = (f + self.slots - 1) * self.size
            if begin >= end:
                self.last_mask.append(0)
            elif begin + self.size <= end:
                self.last_mask.append(full)
            else:
                self.last_mask.append(left_share(end - begin))


def edges(value, axis, heads):
    n = lax.axis_size("col")
    edge, width = heads.edge, value.shape[axis]
    left = go_up(lax.slice_in_dim(value, width - edge, width, axis=axis), 0, n - 2)
    right = go_down(lax.slice_in_dim(value, 0, edge, axis=axis), 1, n - 1)
    return left, right


def widen(value, left, right, axis, heads, col):
    wide = jnp.concatenate([left, value, right], axis)
    before = jnp.array(heads.before, jnp.int32)[col]
    return lax.dynamic_slice_in_dim(wide, heads.edge - before, heads.window, axis)


def narrow_edges(value, axis, heads, col, width):
    n = lax.axis_size("col")
    edge = heads.edge
    before = jnp.array(heads.before, jnp.int32)[col]
    shape = list(value.shape)
    shape[axis] = width + 2 * edge
    wide = lax.dynamic_update_slice_in_dim(
        jnp.zeros(shape, value.dtype), value, edge - before, axis
    )
    tail = go_down(lax.slice_in_dim(wide, 0, edge, axis=axis), 1, n - 1)
    front = go_up(lax.slice_in_dim(wide, edge + width, width + 2 * edge, axis=axis), 0, n - 2)
    return wide, front, tail


def narrow(wide, front, tail, axis, heads, width):
    edge = heads.edge
    pads = [(0, 0)] * wide.ndim
    pads[axis] = (0, width - edge)
    own = lax.slice_in_dim(wide, edge, edge + width, axis=axis).astype(F32)
    own = own + jnp.pad(front, pads).astype(F32)
    pads[axis] = (width - edge, 0)
    return own + jnp.pad(tail, pads).astype(F32)


def moments(values):
    mean = jnp.mean(values, axis=0, keepdims=True)
    centred = values - mean
    variance = jnp.mean(centred * centred, axis=0, keepdims=True)
    return mean, lax.rsqrt(variance + EPSILON)


def body(
    tokens,
    cotangent,
    w_qkv,
    q_bias,
    v_bias,
    w_out,
    out_bias,
    w_up,
    up_bias,
    w_down,
    down_bias,
    ln1_gain,
    ln1_bias,
    ln2_gain,
    ln2_bias,
    key_start,
):
    n_row, n_col = lax.axis_size("row"), lax.axis_size("col")
    row, col = lax.axis_index("row"), lax.axis_index("col")
    seqs, rows, width = tokens.shape
    length = seqs * rows
    depth = width * n_col
    part = length // n_col
    in_rows = w_up.shape[0]
    ff = w_up.shape[1]
    ff_rows = w_down.shape[0]
    ff_part = ff_rows // n_col
    heads = Heads(n_col, width, key_start.shape[0], rows * n_row // BLK)
    size, window = heads.size, heads.window
    firsts = jnp.array(heads.firsts, jnp.int32) * size
    begin = firsts[col]

    shares = Shares(width)
    dp = lax.axis_index("dp")
    row_at = row[None].astype(jnp.int32)
    col_at = col[None].astype(jnp.int32)
    other_rows = [((row + i) % n_row)[None].astype(jnp.int32) for i in range(n_row)]


    x = tokens.reshape(length, width).T
    g = cotangent.reshape(length, width).T
    place_in = col * n_row + row

    def between_owners(value_of, back):
        got = []
        for step in range(n_col):
            pairs = []
            for r in range(n_row):
                for c in range(n_col):
                    to = r * n_col + (c - step) % n_col
                    here, there = r * n_col + c, (to % n_row) * n_col + to // n_row
                    pairs.append((there, here) if back else (here, there))
            got.append(lax.ppermute(value_of(step), ("row", "col"), pairs))
        return got

    x_all = lax.all_gather(x, "col", axis=0, tiled=True)
    wq = w_qkv.transpose(0, 2, 1)
    w3_own = widen(wq, *edges(wq, 1, heads), 1, heads, col)
    w3_parts = [w3_own] + [turn(w3_own, "row", -step) for step in range(1, n_row)]
    w3 = row_join(w3_parts, 2).reshape(3 * window, depth)
    params = jnp.stack([ln1_gain, ln1_bias, ln2_gain, ln2_bias, out_bias, q_bias, v_bias])
    params = [turn(params, "col", step) for step in range(n_col)]
    params = jnp.concatenate(ordered(params, col, -1), 1)
    gain1, shift1, gain2, shift2, bias_out, bias_q, bias_v = [p[:, None] for p in params]
    bias3 = jnp.concatenate(
        [
            lax.dynamic_slice_in_dim(bias_q, begin, window, 0),
            jnp.zeros((window, 1), F32),
            lax.dynamic_slice_in_dim(bias_v, begin, window, 0),
        ]
    )
    up_parts = [w_up] + [turn(w_up, "row", -step) for step in range(1, n_row)]
    up_turned = row_join(up_parts, 0).T
    out_own = shares.take(w_out.T, dp, 0)
    down_own = shares.take(w_down.T, dp, 0)
    x_all, g, out_own, down_own, w3 = gate([x_all, g, out_own, down_own, w3], [up_turned, bias3])

    moved_out = [out_own] + [turn(out_own, "col", -step) for step in range(1, n_col)]
    moved_down = between_owners(
        lambda step: block(down_own, (col - step) % n_col, ff_part, 1), False
    )
    x_float = x_all.astype(F32)
    mean1, rstd1 = moments(x_float)
    n1 = ((x_float - mean1) * rstd1 * gain1 + shift1).astype(BF16)
    triple = product(w3, n1, bias3).reshape(3, window, length)
    triple, g, *rest = gate([triple, g] + moved_out[1:] + moved_down, [])
    moved_out = jnp.stack(ordered(moved_out[:1] + rest[: n_col - 1], col, 1))
    moved_down = jnp.stack(ordered(rest[n_col - 1 :], place_in, 1))

    g_all = lax.all_gather(g, "col", axis=0, tiled=True)
    pieces = [triple] + [turn(triple, "row", -step) for step in range(1, n_row)]
    near_out = [swap_with(moved_out, 1), swap_with(moved_out, 2)]
    *pieces, near_x, near_y, moved_down = gate(pieces[1:] + near_out + [moved_down], [])
    pieces, near_out = [triple] + pieces, [near_x, near_y]

    half = n_col // 2

    def to_diagonal(near):
        return [swap_with(near[0][:half], 2), swap_with(near[1][half:], 1)]

    far_out = to_diagonal(near_out)
    near_down = [swap_with(moved_down, 1), swap_with(moved_down, 2)]
    meta = jnp.stack(
        [
            jnp.array(heads.firsts, jnp.int32)[col],
            row,
            jnp.array(heads.first_mask, jnp.int32)[col],
            jnp.array(heads.last_mask, jnp.int32)[col],
        ]
    )
    *cuts, mixed, norms = attn_fwd(meta, key_start, pieces, heads.slots, size)
    *cuts, a, b, c, d = gate(list(cuts) + far_out + near_down, [])
    far_out, near_down = [a, b], [c, d]

    dp_at = dp[None].astype(jnp.int32)
    far_down = to_diagonal(near_down)
    mixed_own = row_sum(cuts).astype(BF16)
    out_weights = assemble([moved_out] + near_out + far_out, shares, dp_at)
    mixed_own, out_weights, g_all, *far_down = gate(
        [mixed_own, out_weights, g_all] + far_down, []
    )

    got = [
        turn(block(mixed_own, (col + step) % n_col, part, 1), "col", step) for step in range(n_col)
    ]
    out_weights = [turn(out_weights, "row", -step) for step in range(n_row)]
    down_weights = assemble([moved_down] + near_down + far_down, shares, dp_at)
    *rest, down_weights = gate(got[1:] + out_weights[1:] + [down_weights], [])
    got = got[:1] + rest[: n_col - 1]
    out_weights = out_weights[:1] + rest[n_col - 1 :]
    out_weights = [w.reshape(depth, in_rows) for w in out_weights]

    down_weights = [turn(down_weights, "row", -step) for step in range(n_row)]
    got = ordered(got, col, -1)
    lapped = [heads.firsts[j] * size for j in range(n_col)]
    attention = sum(
        jnp.pad(piece, ((at, depth - at - window), (0, 0))) for piece, at in zip(got, lapped)
    )
    branch = split_product(out_weights, attention, row_at, bias_out, F32)
    resid = block(x_all, col, part, 1).astype(F32) + branch
    mean2, rstd2 = moments(resid)
    hat2 = (resid - mean2) * rstd2
    n2_own = (hat2 * gain2 + shift2).astype(BF16)
    n2_own, *rest = gate([n2_own] + down_weights[1:], [hat2])
    down_weights = down_weights[:1] + rest
    down_weights = [w.reshape(depth, ff_part) for w in down_weights]

    n2_all = lax.all_gather(n2_own, "col", axis=1, tiled=True)
    down_turned = jnp.concatenate([w.T for w in down_weights])
    g_sums = jnp.sum(g.astype(F32), axis=1)
    n2_all, down_turned = gate([n2_all, down_turned], [g_sums])

    hidden_all, du_all, part2 = hidden_layer(
        up_turned, down_turned, n_row, up_bias[:, None], n2_all, g_all, row_at
    )
    part2, hidden_all, du_all = gate([part2, hidden_all, du_all], [])

    dn2 = lax.psum_scatter(part2, "col", scatter_dimension=1, tiled=True)
    up_grad = [token_product(n2_all, du_all, r, n_row, True) for r in other_rows[::-1]][::-1]
    up_grad = row_sum(up_grad).astype(BF16)
    down_grad = [token_product(g_all, hidden_all, r, n_row, False) for r in other_rows[::-1]][::-1]
    down_grad = [d.reshape(n_col, width, ff_part) for d in down_grad]
    down_grad = row_sum(down_grad).astype(BF16)
    no_bias = jnp.zeros((depth, 1), F32)
    shrunk = split_product(down_weights, hidden_all, row_at, no_bias, BF16)
    own_sum = block(shrunk, col, part, 1).astype(F32) + resid
    shrunk = lax.dynamic_update_slice_in_dim(shrunk, own_sum.astype(BF16), col * part, 1)
    du_sums = jnp.sum(du_all.astype(F32), axis=1)
    up_rows = width if in_rows % width == 0 else in_rows
    up_shares = Shares(up_rows)
    up_grad = up_grad.reshape(in_rows // up_rows, up_rows, ff)
    dn2, up_grad, down_grad, shrunk = gate([dn2, up_grad, down_grad, shrunk], [du_sums])

    dn2 = dn2.astype(F32)
    up2 = dn2 * gain2
    pull2 = jnp.mean(up2, axis=0, keepdims=True)
    lean2 = jnp.mean(up2 * hat2, axis=0, keepdims=True)
    dr = block(g_all, col, part, 1).astype(F32) + rstd2 * (up2 - pull2 - hat2 * lean2)
    db = dr.astype(BF16)
    da = split_product_tn(out_weights, db, row_at)
    sums2 = jnp.stack(
        [
            jnp.sum(db.astype(F32), axis=1),
            jnp.sum(dn2 * hat2, axis=1),
            jnp.sum(dn2, axis=1),
        ]
    )
    da, db, shrunk, up_grad, down_grad = gate([da, db, shrunk, up_grad, down_grad], [sums2])

    outputs = lax.psum_scatter(shrunk, "col", scatter_dimension=0, tiled=True)
    got = []
    for step in range(n_col):
        to = firsts[(col + step) % n_col]
        got.append(turn(lax.dynamic_slice_in_dim(da, to, window, 0), "col", step))

    def first_sums(value, cut, bit):
        near = swap_with(cut.take(value, dp ^ bit, 1), bit)
        return [near, swap_with(cut.take(value, dp ^ 3, 1), bit)]

    def relay(value, far, cut, bit):
        sent = cut.take(value, dp ^ (3 - bit), 1).astype(F32) + far.astype(F32)
        return swap_with(sent.astype(BF16), 3 - bit)

    def share_sum(value, cut, near, relayed):
        own = cut.take(value, dp, 1).astype(F32)
        return (own + near.astype(F32) + relayed.astype(F32)).astype(BF16)

    up_first = first_sums(up_grad, up_shares, 1)
    down_first = first_sums(down_grad, shares, 2)
    out_grad = [token_product(db, attention, r, n_row, False) for r in other_rows[::-1]][::-1]
    out_grad = [o.reshape(n_col, width, in_rows) for o in out_grad]
    rest = gate(got[1:] + out_grad + up_first + down_first, [])
    got, rest = got[:1] + rest[: n_col - 1], rest[n_col - 1 :]
    out_grad, up_first, down_first = rest[:n_row], rest[n_row : n_row + 2], rest[n_row + 2 :]

    da_own = jnp.concatenate(ordered(got, col, -1), 1)
    da_pieces = [da_own] + [turn(da_own, "row", -step) for step in range(1, n_row)]
    up_relay = relay(up_grad, up_first[1], up_shares, 1)
    down_relay = relay(down_grad, down_first[1], shares, 2)
    out_grad = row_sum(out_grad).astype(BF16)
    *rest, out_grad, up_relay, down_relay = gate(
        da_pieces[1:] + [out_grad, up_relay, down_relay], []
    )
    da_pieces = [da_own] + rest

    out_first = first_sums(out_grad, shares, 1)
    dqkv = attn_bwd(meta, key_start, pieces, da_pieces, mixed, norms, heads.slots, size)
    *dqkv, outputs, down_relay, a, b = gate(list(dqkv) + [outputs, down_relay] + out_first, [])
    out_first = [a, b]

    down_share = share_sum(down_grad, shares, down_first[0], down_relay)
    down_home = between_owners(lambda step: pick(down_share, (place_in + step) % n_col), True)
    out_relay = relay(out_grad, out_first[1], shares, 1)
    dqkv = row_sum(dqkv).astype(BF16).reshape(3 * window, length)
    dqkv, out_relay, up_relay, *down_home = gate([dqkv, out_relay, up_relay] + down_home, [])

    out_share = share_sum(out_grad, shares, out_first[0], out_relay)
    out_home = [turn(pick(out_share, (col + step) % n_col), "col", step) for step in range(n_col)]
    up_share = share_sum(up_grad, up_shares, up_first[0], up_relay)
    up_near = [swap_with(up_share, 1), swap_with(up_share, 2)]
    dn1, stats, norm1 = norm_product_tn(w3, dqkv, n1, gain1, shift1, rstd1)
    riding = block(dn1, col, part, 1).astype(F32) + dr
    dn1 = lax.dynamic_update_slice_in_dim(dn1, riding.astype(BF16), col * part, 1)
    dn1, dqkv, stats, norm1, *rest = gate([dn1, dqkv, stats, norm1] + out_home[1:] + up_near, [])
    out_home, up_near = out_home[:1] + rest[: n_col - 1], rest[n_col - 1 :]

    dx = lax.psum_scatter(dn1, "col", scatter_dimension=0, tiled=True)
    qkv_parts = [token_product(dqkv, n1, r, n_row, False) for r in other_rows[::-1]][::-1]
    qkv_parts = [q.reshape(3, window, in_rows) for q in qkv_parts]
    qkv_grad = row_sum(qkv_parts).astype(BF16)
    up_half = up_share.shape[1] // 2 // 16 * 16
    up_far = [swap_with(up_near[0][:, :up_half], 2), swap_with(up_near[1][:, up_half:], 1)]
    out_home = sum(o.astype(F32) for o in out_home).astype(BF16)
    homes = jnp.stack([out_home] + ordered(down_home, col, -1))
    homes_near = [swap_with(homes, 1), swap_with(homes, 2)]
    stats = sum(turn(stats, "col", step) for step in range(n_col)) / depth
    dq_dv = jnp.sum(dqkv.astype(F32), axis=1).reshape(3, window)
    sums = lax.dynamic_update_slice_in_dim(jnp.zeros((2, depth), F32), dq_dv[::2], begin, 1)
    sums = jnp.concatenate([sums, (norm1[:, :1] / gain1).T, norm1[:, 1:].T, sums2]).reshape(-1)
    small = jnp.concatenate([sums, du_sums, g_sums])[None]
    small = small_sum(small, ("row",))
    outputs = (outputs.astype(F32) + down_bias[:, None]).astype(BF16)
    qkv_grad, small, *rest = gate([qkv_grad, small] + up_far + homes_near, [stats, outputs])
    up_far, homes_near = rest[:2], rest[2:]

    wide, front, tail = narrow_edges(qkv_grad, 1, heads, col, width)
    homes_far = [swap_with(homes_near[0][:2], 2), swap_with(homes_near[1][2:], 1)]
    small = small_sum(small, ("dp",))[0]
    up_grad = up_shares.join(
        [up_share] + up_near + [jnp.concatenate(up_far, 1)], dp, 1
    ).astype(F32)
    up_grad = up_grad.reshape(in_rows, ff)
    front, tail, small, *homes_far = gate([front, tail, small] + homes_far, [up_grad])

    qkv_grad = narrow(wide, front, tail, 1, heads, width).astype(BF16)
    qkv_got = [swap_with(shares.take(qkv_grad, dp ^ m, 1), m) for m in (1, 2, 3)]
    sums, local = small[: 7 * depth].reshape(7, depth), small[7 * depth :]
    sums = small_sum(sums, ("col",))
    sums = lax.dynamic_slice_in_dim(sums, col * width, width, 1)
    homes = shares.join(
        [homes] + homes_near + [jnp.concatenate(homes_far)], dp, 1
    ).astype(F32)
    out_grad = homes[0]
    down_grad = jnp.concatenate([homes[1 + j] for j in range(n_col)], 1)
    qkv_got = gate(qkv_got, [out_grad, down_grad, sums])

    qkv_share = shares.take(qkv_grad, dp, 1).astype(F32)
    qkv_share = (qkv_share + sum(q.astype(F32) for q in qkv_got)).astype(BF16)
    qkv_all = swap_all(qkv_share)
    hat1 = (x.astype(F32) - mean1) * rstd1
    input_grad = (dx.astype(F32) - rstd1 * (stats[0:1] + hat1 * stats[1:2])).astype(BF16)
    qkv_grad = shares.join([qkv_share] + qkv_all, dp, 1).astype(F32)
    return (
        outputs.T.reshape(tokens.shape),
        input_grad.T.reshape(tokens.shape),
        qkv_grad.transpose(0, 2, 1),
        sums[0],
        sums[1],
        out_grad.T,
        sums[4],
        up_grad,
        local[:ff],
        down_grad.T,
        local[ff:],
        sums[2],
        sums[3],
        sums[5],
        sums[6],
    )


def solution(mesh):
    inputs = (
        P("dp", "row", "col"),
        P("dp", "row", "col"),
        P(None, "row", "col"),
        P("col"),
        P("col"),
        P("row", "col"),
        P("col"),
        P("row", "col"),
        P("col"),
        P("row", "col"),
        P("col"),
        P("col"),
        P("col"),
        P("col"),
        P("col"),
        P(),
    )
    return jax.shard_map(
        body, mesh=mesh, in_specs=inputs, out_specs=inputs[:15], check_vma=False
    )
```

```python
import functools

import jax
import jax.numpy as jnp
from jax import lax
from jax.experimental import pallas as pl
from jax.experimental.pallas import tpu as pltpu
from jax.sharding import PartitionSpec as P

BLK = 512
EPSILON = 1e-05
LOG2E = 1.4426950408889634
BF16 = jnp.bfloat16
F32 = jnp.float32

FREE = pl.CostEstimate(flops=0, bytes_accessed=0, transcendentals=0)
ROOM = pltpu.CompilerParams(vmem_limit_bytes=56 * 2**20)

NT=(((0,),(0,)),((),()))
TN=(((1,),(1,)),((),()))

def plan_tiles(meta, ks, own, load, n_slots, n_blocks, n_row, n_heads):
    for i in range(n_row): load[i]=0
    def level(lv,_):
        cost=n_blocks-lv
        def tile(t,_):
            slot=t//n_blocks; qb=t%n_blocks
            head=meta[0]+slot
            here=head<n_heads
            hd=jnp.minimum(head,n_heads-1)
            n=qb+1-ks[hd,qb]
            mask=jnp.where(slot==0,meta[2],jnp.where(slot==n_slots-1,meta[3],(1<<n_blocks)-1))
            here=jnp.logical_and(here,((mask>>qb)&1)==1)
            @pl.when(cost==n_blocks)
            def _(): own[t]=-1
            @pl.when(jnp.logical_and(here,n==cost))
            def _():
                best=load[0]; who=jnp.int32(0)
                for i in range(1,n_row):
                    less=load[i]<best
                    best=jnp.where(less,load[i],best); who=jnp.where(less,i,who)
                own[t]=who
                load[who]=best+cost
            return 0
        lax.fori_loop(0,n_slots*n_blocks,tile,0)
        return 0
    lax.fori_loop(0,n_blocks,level,0)

def fetch(pieces, whole, sems, row, n_row, width):
    copies=[]
    for i,p in enumerate(pieces):
        at=lax.rem(row+i,n_row)*width
        c=pltpu.make_async_copy(p, whole.at[...,pl.ds(pl.multiple_of(at,width),width)], sems.at[i])
        c.start(); copies.append(c)
    return copies

def fwd_kernel(n_row,n_slots,hd,n_heads,meta,ks,*refs):
    pieces=refs[:n_row]; cuts=refs[n_row:2*n_row]; o_ref,lse_ref,whole,own,load,sems=refs[2*n_row:]
    S=whole.shape[2]; nb=S//BLK; width=S//n_row
    row=meta[1]
    copies=fetch(pieces,whole,sems,row,n_row,width)
    plan_tiles(meta,ks,own,load,n_slots,nb,n_row,n_heads)
    o_ref[...]=jnp.zeros_like(o_ref)
    for c in copies: c.wait()
    c2=hd**-0.5*LOG2E
    diag=lax.broadcasted_iota(jnp.int32,(BLK,BLK),0)<=lax.broadcasted_iota(jnp.int32,(BLK,BLK),1)
    def tile(t,_):
        @pl.when(own[t]==row)
        def _():
            slot=t//nb; qb=t%nb
            first=ks[meta[0]+slot,qb]
            hs=pl.ds(pl.multiple_of(slot*hd,hd),hd)
            qs=pl.ds(pl.multiple_of(qb*BLK,BLK),BLK)
            q=whole[0,hs,qs]
            def scores(kb_ds):
                return lax.dot_general(whole[1,hs,kb_ds],q,NT,preferred_element_type=jnp.float32)
            s=jnp.where(diag,scores(qs),-1e30)
            m=jnp.max(s,axis=0,keepdims=True)
            p=jnp.exp2((s-m)*c2)
            l=jnp.sum(p,axis=0,keepdims=True)
            acc=jnp.dot(whole[2,hs,qs],p.astype(jnp.bfloat16),preferred_element_type=jnp.float32)
            def step(kb,carry):
                m,l,acc=carry
                kd=pl.ds(pl.multiple_of(kb*BLK,BLK),BLK)
                s=scores(kd)
                mn=jnp.maximum(m,jnp.max(s,axis=0,keepdims=True))
                a=jnp.exp2((m-mn)*c2)
                p=jnp.exp2((s-mn)*c2)
                l=l*a+jnp.sum(p,axis=0,keepdims=True)
                acc=acc*a+jnp.dot(whole[2,hs,kd],p.astype(jnp.bfloat16),preferred_element_type=jnp.float32)
                return mn,l,acc
            m,l,acc=lax.fori_loop(first,qb,step,(m,l,acc))
            o_ref[hs,qs]=(acc/l).astype(jnp.bfloat16)
            lse_ref[pl.ds(slot,1),qs]=m*c2+jnp.log2(l)
        return 0
    lax.fori_loop(0,n_slots*nb,tile,0)
    for i,cut in enumerate(cuts):
        cut[...]=o_ref[:,pl.ds(pl.multiple_of(lax.rem(row+i,n_row)*width,width),width)]

def bwd_kernel(n_row,n_slots,hd,n_heads,meta,ks,*refs):
    pieces=refs[:n_row]; das=refs[n_row:2*n_row]
    o_ref,lse_ref=refs[2*n_row:2*n_row+2]; cuts=refs[2*n_row+2:3*n_row+2]
    d_ref,whole,da,acc,own,load,sems,sems2=refs[3*n_row+2:]
    S=whole.shape[2]; nb=S//BLK; width=S//n_row
    row=meta[1]
    copies=fetch(pieces,whole,sems,row,n_row,width)+fetch(das,da,sems2,row,n_row,width)
    plan_tiles(meta,ks,own,load,n_slots,nb,n_row,n_heads)
    d_ref[...]=jnp.zeros_like(d_ref)
    acc[...]=jnp.zeros_like(acc)
    for c in copies: c.wait()
    scale=hd**-0.5; c2=scale*LOG2E
    diag=lax.broadcasted_iota(jnp.int32,(BLK,BLK),0)<=lax.broadcasted_iota(jnp.int32,(BLK,BLK),1)
    def tile(t,_):
        @pl.when(own[t]==row)
        def _():
            slot=t//nb; qb=t%nb
            first=ks[meta[0]+slot,qb]
            hs=pl.ds(pl.multiple_of(slot*hd,hd),hd)
            qs=pl.ds(pl.multiple_of(qb*BLK,BLK),BLK)
            q=whole[0,hs,qs]
            up=da[hs,qs]
            lse=lse_ref[pl.ds(slot,1),qs]
            delta=jnp.sum(up.astype(jnp.float32)*o_ref[hs,qs].astype(jnp.float32),axis=0,keepdims=True)
            def block(kd,masked):
                k=whole[1,hs,kd]
                s=lax.dot_general(k,q,NT,preferred_element_type=jnp.float32)
                p=jnp.exp2(s*c2-lse)
                if masked: p=jnp.where(diag,p,0.0)
                dp=lax.dot_general(whole[2,hs,kd],up,NT,preferred_element_type=jnp.float32)
                ds=(p*(dp-delta)).astype(jnp.bfloat16)
                acc[1,hs,kd]+=lax.dot_general(up,p.astype(jnp.bfloat16),TN,preferred_element_type=jnp.float32)
                acc[0,hs,kd]+=lax.dot_general(q,ds,TN,preferred_element_type=jnp.float32)
                return jnp.dot(k,ds,preferred_element_type=jnp.float32)
            dq=block(qs,True)
            dq=lax.fori_loop(first,qb,lambda kb,dq:dq+block(pl.ds(pl.multiple_of(kb*BLK,BLK),BLK),False),dq)
            d_ref[hs,qs]=(dq*scale).astype(jnp.bfloat16)
        return 0
    lax.fori_loop(0,n_slots*nb,tile,0)
    for i,cut in enumerate(cuts):
        at=pl.ds(pl.multiple_of(lax.rem(row+i,n_row)*width,width),width)
        cut[0]=d_ref[:,at]
        cut[1]=(acc[0,:,at]*scale).astype(jnp.bfloat16)
        cut[2]=acc[1,:,at].astype(jnp.bfloat16)

V=pl.BlockSpec(memory_space=pltpu.VMEM); SM=pl.BlockSpec(memory_space=pltpu.SMEM); ANY=pl.BlockSpec(memory_space=pl.ANY)
def attn_fwd(meta,ks,pieces,n_slots,hd):
    n_row=len(pieces); _,H,T=pieces[0].shape; S=T*n_row; nb=S//BLK
    return pl.pallas_call(functools.partial(fwd_kernel,n_row,n_slots,hd,ks.shape[0]),
      out_shape=[jax.ShapeDtypeStruct((H,T),jnp.bfloat16)]*n_row+[jax.ShapeDtypeStruct((H,S),jnp.bfloat16),jax.ShapeDtypeStruct((n_slots,S),jnp.float32)],
      in_specs=[SM,SM]+[ANY]*n_row,out_specs=[V]*(n_row+2),
      scratch_shapes=[pltpu.VMEM((3,H,S),jnp.bfloat16),pltpu.SMEM((n_slots*nb,),jnp.int32),pltpu.SMEM((n_row,),jnp.int32),pltpu.SemaphoreType.DMA((n_row,))],
      compiler_params=pltpu.CompilerParams(vmem_limit_bytes=48*2**20),
      cost_estimate=FREE,
    )(meta,ks,*pieces)
def attn_bwd(meta,ks,pieces,das,o,lse,n_slots,hd):
    n_row=len(pieces); _,H,T=pieces[0].shape; S=T*n_row; nb=S//BLK
    return pl.pallas_call(functools.partial(bwd_kernel,n_row,n_slots,hd,ks.shape[0]),
      out_shape=[jax.ShapeDtypeStruct((3,H,T),jnp.bfloat16)]*n_row,
      in_specs=[SM,SM]+[ANY]*(2*n_row)+[V,V],out_specs=[V]*n_row,
      scratch_shapes=[pltpu.VMEM((H,S),jnp.bfloat16),pltpu.VMEM((3,H,S),jnp.bfloat16),pltpu.VMEM((H,S),jnp.bfloat16),pltpu.VMEM((2,H,S),jnp.float32),pltpu.SMEM((n_slots*nb,),jnp.int32),pltpu.SMEM((n_row,),jnp.int32),pltpu.SemaphoreType.DMA((n_row,)),pltpu.SemaphoreType.DMA((n_row,))],
      compiler_params=pltpu.CompilerParams(vmem_limit_bytes=56*2**20),
      cost_estimate=FREE,
    )(meta,ks,*pieces,*das,o,lse)


def rows_of(total, most):
    for rows in range(min(total, most) // 16 * 16, 0, -16):
        if total % rows == 0:
            return rows
    return total


def by_rows(i, *refs):
    return (i, 0)


def whole_block(i, *refs):
    return (0, 0)


def product_kernel(a_ref, b_ref, bias_ref, o_ref):
    o_ref[...] = (
        jnp.dot(a_ref[...], b_ref[...], preferred_element_type=F32) + bias_ref[...]
    ).astype(o_ref.dtype)


def product(a, b, bias):
    rows = rows_of(a.shape[0], 448)
    return pl.pallas_call(
        product_kernel,
        out_shape=jax.ShapeDtypeStruct((a.shape[0], b.shape[1]), BF16),
        grid=(a.shape[0] // rows,),
        in_specs=[
            pl.BlockSpec((rows, a.shape[1]), by_rows),
            pl.BlockSpec(b.shape, whole_block),
            pl.BlockSpec((rows, 1), by_rows),
        ],
        out_specs=pl.BlockSpec((rows, b.shape[1]), by_rows),
        compiler_params=ROOM,
        cost_estimate=FREE,
    )(a, b, bias)


def split_product(parts, b, row, columns, which, dtype):
    n = len(parts)
    total, depth = parts[0].shape
    width = b.shape[1]
    rows = rows_of(total, 400)

    def kernel(row_ref, b_ref, bias_ref, *refs):
        out = bias_ref[:, which : which + 1] + jnp.zeros((rows, width), F32)
        for i in range(n):
            at = pl.multiple_of(lax.rem(row_ref[0] + i, n) * depth, 8)
            out = out + jnp.dot(refs[i][...], b_ref[pl.ds(at, depth), :], preferred_element_type=F32)
        refs[n][...] = out.astype(dtype)

    return pl.pallas_call(
        kernel,
        out_shape=jax.ShapeDtypeStruct((total, width), dtype),
        grid=(total // rows,),
        in_specs=[
            SM,
            pl.BlockSpec(b.shape, whole_block),
            pl.BlockSpec((rows, columns.shape[1]), by_rows),
        ]
        + [pl.BlockSpec((rows, depth), by_rows)] * n,
        out_specs=pl.BlockSpec((rows, width), by_rows),
        compiler_params=ROOM,
        cost_estimate=FREE,
    )(row, b, columns, *parts)


def split_product_tn(parts, b, row):
    n = len(parts)
    depth = parts[0].shape[1]
    total, width = b.shape
    rows = rows_of(total, 400)
    steps = total // rows

    def kernel(row_ref, b_ref, *refs):
        o_ref, acc = refs[n:]

        @pl.when(pl.program_id(0) == 0)
        def start():
            acc[...] = jnp.zeros_like(acc)

        for i in range(n):
            at = pl.multiple_of(lax.rem(row_ref[0] + i, n) * depth, 8)
            acc[pl.ds(at, depth), :] += lax.dot_general(
                refs[i][...], b_ref[...], NT, preferred_element_type=F32
            )

        @pl.when(pl.program_id(0) == steps - 1)
        def end():
            o_ref[...] = acc[...].astype(BF16)

    return pl.pallas_call(
        kernel,
        out_shape=jax.ShapeDtypeStruct((n * depth, width), BF16),
        grid=(steps,),
        in_specs=[SM, pl.BlockSpec((rows, width), by_rows)]
        + [pl.BlockSpec((rows, depth), by_rows)] * n,
        out_specs=pl.BlockSpec((n * depth, width), whole_block),
        scratch_shapes=[pltpu.VMEM((n * depth, width), F32)],
        compiler_params=ROOM,
        cost_estimate=FREE,
    )(row, b, *parts)


def norm_product_tn(a, b, normed, columns, scale, riding, col, n_col):
    rows = rows_of(a.shape[0], 448)
    steps = a.shape[0] // rows
    depth, tokens = a.shape[1], b.shape[1]
    cut, part = depth // n_col, tokens // n_col

    def kernel(col_ref, a_ref, b_ref, n_ref, g_ref, c_ref, r_ref, o_ref, f_ref, acc):
        @pl.when(pl.program_id(0) == 0)
        def start():
            acc[...] = lax.dot_general(a_ref[...], b_ref[...], NT, preferred_element_type=F32)

        @pl.when(pl.program_id(0) > 0)
        def more():
            acc[...] += lax.dot_general(a_ref[...], b_ref[...], NT, preferred_element_type=F32)

        @pl.when(pl.program_id(0) == steps - 1)
        def end():
            first = jnp.zeros((1, tokens), F32)
            second = jnp.zeros((1, tokens), F32)
            for j in range(n_col):
                at = pl.ds(j * cut, cut)
                p = acc[at, :]
                scaled = p * g_ref[at, 0:1]
                o_ref[j, 0:cut, :] = (scaled * c_ref[...]).astype(BF16)
                moved = p * (n_ref[at, :].astype(F32) - g_ref[at, 1:2])
                first += jnp.sum(scaled, axis=0, keepdims=True)
                second += jnp.sum(moved, axis=0, keepdims=True)
                f_ref[at, 0:1] = jnp.sum(moved, axis=1, keepdims=True)
                f_ref[at, 1:2] = jnp.sum(p, axis=1, keepdims=True)
                for c in range(n_col):

                    @pl.when(col_ref[0] == c)
                    def ride():
                        here = slice(c * part, (c + 1) * part)
                        own = scaled[:, here] * c_ref[:, here] + r_ref[at, :]
                        o_ref[j, 0:cut, here] = own.astype(BF16)

            lines = []
            for line in (first, second):
                high = line.astype(BF16).astype(F32)
                lines += [high, line - high]
            lines = jnp.concatenate(lines + [jnp.zeros((12, tokens), F32)]).astype(BF16)
            for j in range(n_col):
                o_ref[j, cut : cut + 16, :] = lines

    return pl.pallas_call(
        kernel,
        out_shape=[
            jax.ShapeDtypeStruct((n_col, cut + 16, tokens), BF16),
            jax.ShapeDtypeStruct((depth, 2), F32),
        ],
        grid=(steps,),
        in_specs=[
            SM,
            pl.BlockSpec((rows, depth), by_rows),
            pl.BlockSpec((rows, tokens), by_rows),
            pl.BlockSpec((depth, tokens), whole_block),
            pl.BlockSpec(columns.shape, whole_block),
            pl.BlockSpec((1, tokens), whole_block),
            pl.BlockSpec((depth, part), whole_block),
        ],
        out_specs=[
            pl.BlockSpec((n_col, cut + 16, tokens), lambda i: (0, 0, 0)),
            pl.BlockSpec((depth, 2), whole_block),
        ],
        scratch_shapes=[pltpu.VMEM((depth, tokens), F32)],
        compiler_params=ROOM,
        cost_estimate=FREE,
    )(col, a, b, normed, columns, scale, riding)


def token_product(a, b, index, parts, of_a):
    rows_a = a.shape[0] // (parts if of_a else 1)
    rows_b = b.shape[0] // (1 if of_a else parts)
    rows = rows_of(rows_a, 448)
    steps = rows_a // rows

    def kernel(index_ref, a_ref, b_ref, o_ref):
        o_ref[...] = lax.dot_general(
            a_ref[...], b_ref[...], TN, preferred_element_type=F32
        ).astype(BF16)

    if of_a:
        a_map, b_map = (lambda i, r: (r[0] * steps + i, 0)), whole_block
    else:
        a_map, b_map = by_rows, (lambda i, r: (r[0], 0))
    return pl.pallas_call(
        kernel,
        out_shape=jax.ShapeDtypeStruct((rows_a, rows_b), BF16),
        grid_spec=pltpu.PrefetchScalarGridSpec(
            num_scalar_prefetch=1,
            grid=(steps,),
            in_specs=[
                pl.BlockSpec((rows, a.shape[1]), a_map),
                pl.BlockSpec((rows_b, b.shape[1]), b_map),
            ],
            out_specs=pl.BlockSpec((rows, rows_b), by_rows),
        ),
        compiler_params=ROOM,
        cost_estimate=FREE,
    )(index, a, b)


def gelu_parts(u):
    inner = 0.7978845608 * (u + 0.044715 * u * u * u)
    t = jnp.tanh(inner)
    value = 0.5 * u * (1.0 + t)
    slope = 0.5 * (1.0 + t) + 0.5 * u * (1.0 - t * t) * 0.7978845608 * (1.0 + 0.134145 * u * u)
    return value, slope


def hidden_layer(up, down, n, bias, n2, g, row):
    ff, depth = up.shape
    tokens = n2.shape[1]
    rows = rows_of(ff // n, 400)
    cuts = ff // n // rows
    steps = ff // rows

    def kernel(row_ref, up_ref, down_ref, bias_ref, n_ref, g_ref, h_ref, d_ref, p_ref, acc):
        step = pl.program_id(0)
        u = jnp.dot(up_ref[...], n_ref[...], preferred_element_type=F32) + bias_ref[...]
        value, slope = gelu_parts(u)
        h_ref[...] = value.astype(BF16)
        dh = jnp.dot(down_ref[...], g_ref[...], preferred_element_type=F32)
        du = (dh * slope).astype(BF16)
        d_ref[...] = du

        @pl.when(step == 0)
        def start():
            acc[...] = lax.dot_general(up_ref[...], du, NT, preferred_element_type=F32)

        @pl.when(step > 0)
        def more():
            acc[...] += lax.dot_general(up_ref[...], du, NT, preferred_element_type=F32)

        @pl.when(step == steps - 1)
        def end():
            p_ref[...] = acc[...].astype(BF16)

    mine = lambda i, r: (lax.rem(r[0] * cuts + i, steps), 0)
    full = lambda i, r: (0, 0)
    return pl.pallas_call(
        kernel,
        out_shape=[
            jax.ShapeDtypeStruct((ff, tokens), BF16),
            jax.ShapeDtypeStruct((ff, tokens), BF16),
            jax.ShapeDtypeStruct((depth, tokens), BF16),
        ],
        grid_spec=pltpu.PrefetchScalarGridSpec(
            num_scalar_prefetch=1,
            grid=(steps,),
            in_specs=[
                pl.BlockSpec((rows, depth), mine),
                pl.BlockSpec((rows, depth), lambda i, r: (i, 0)),
                pl.BlockSpec((rows, 1), mine),
                pl.BlockSpec((depth, tokens), full),
                pl.BlockSpec((depth, tokens), full),
            ],
            out_specs=[
                pl.BlockSpec((rows, tokens), mine),
                pl.BlockSpec((rows, tokens), mine),
                pl.BlockSpec((depth, tokens), full),
            ],
            scratch_shapes=[pltpu.VMEM((depth, tokens), F32)],
        ),
        compiler_params=ROOM,
        cost_estimate=FREE,
    )(row, up, down, bias, n2, g)


def turned(parts):
    n = len(parts)
    depth, wide = parts[0].shape

    def kernel(*refs):
        o_ref = refs[n]
        for i in range(n):
            for first in range(0, wide, 256):
                size = min(256, wide - first)
                at = lax.broadcasted_iota(jnp.int32, (size, size), 0)
                ones = (at == lax.broadcasted_iota(jnp.int32, (size, size), 1)).astype(BF16)
                cut = refs[i][:, first : first + size]
                out = lax.dot_general(ones, cut, TN, preferred_element_type=F32)
                o_ref[i * wide + first : i * wide + first + size, :] = out.astype(BF16)

    return pl.pallas_call(
        kernel,
        out_shape=jax.ShapeDtypeStruct((n * wide, depth), BF16),
        in_specs=[V] * n,
        out_specs=V,
        compiler_params=ROOM,
        cost_estimate=FREE,
    )(*parts)


def gate(values, others):
    def kernel(*refs):
        pass

    out = pl.pallas_call(
        kernel,
        out_shape=[jax.ShapeDtypeStruct(v.shape, v.dtype) for v in values],
        in_specs=[ANY] * (len(values) + len(others)),
        out_specs=[ANY] * len(values),
        input_output_aliases={i: i for i in range(len(values))},
        cost_estimate=FREE,
    )(*values, *others)
    return list(out)


def turn(value, axis, steps):
    size = lax.axis_size(axis)
    if steps % size == 0:
        return value
    return lax.ppermute(value, axis, [(i, (i + steps) % size) for i in range(size)])


def block(value, index, size, axis):
    return lax.dynamic_slice_in_dim(value, index * size, size, axis)


def row_sum(parts):
    total = parts[0].astype(F32)
    for step in range(1, len(parts)):
        total = total + turn(parts[step], "row", step).astype(F32)
    return total


def swap_with(value, bit):
    return lax.ppermute(value, "dp", [(i, i ^ bit) for i in range(4)])


def pick(value, index, axis=0):
    return lax.dynamic_index_in_dim(value, index, axis, keepdims=False)


def dot(a, b):
    return jnp.dot(a, b, preferred_element_type=F32)


def ordered(parts, base, sign):
    size = len(parts)
    stacked = jnp.stack(parts)
    return [pick(stacked, (sign * (j - base)) % size) for j in range(size)]


class Shares:
    def __init__(self, rows):
        self.rows = rows
        self.size = -(-rows // 64) * 16
        self.starts = [(rows - self.size) * s // 48 * 16 for s in range(3)] + [rows - self.size]
        ends = self.starts[1:] + [rows]
        self.lengths = [b - a for a, b in zip(self.starts, ends)]

    def take(self, value, share, axis):
        start = jnp.array(self.starts, jnp.int32)[share]
        return lax.dynamic_slice_in_dim(value, start, self.size, axis)

    def join(self, parts, me, axis):
        stacked = jnp.stack(parts)
        laid = [
            lax.slice_in_dim(pick(stacked, me ^ s), 0, self.lengths[s], axis=axis)
            for s in range(4)
        ]
        return jnp.concatenate(laid, axis)


def assemble(parts, shares, me):
    n, wide = parts[0].shape[0], parts[0].shape[2]

    def kernel(me_ref, *refs):
        o_ref, sems = refs[-2:]
        for act in ("start", "wait"):
            for m in range(4):
                for s in range(4):

                    @pl.when(me_ref[0] ^ m == s)
                    def move():
                        rows = pl.ds(0, shares.lengths[s])
                        to = pl.ds(shares.starts[s], shares.lengths[s])
                        pairs = [(refs[m].at[:, rows], o_ref.at[:, to])]
                        if m == 3 and len(parts) == 5:
                            low, high = pl.ds(0, n // 2), pl.ds(n // 2, n // 2)
                            pairs = [
                                (refs[3].at[:, rows], o_ref.at[low, to]),
                                (refs[4].at[:, rows], o_ref.at[high, to]),
                            ]
                        for k, (source, target) in enumerate(pairs):
                            copy = pltpu.make_async_copy(source, target, sems.at[m + k])
                            getattr(copy, act)()

    return pl.pallas_call(
        kernel,
        out_shape=jax.ShapeDtypeStruct((n, shares.rows, wide), parts[0].dtype),
        in_specs=[SM] + [ANY] * len(parts),
        out_specs=V,
        scratch_shapes=[pltpu.SemaphoreType.DMA((5,))],
        compiler_params=ROOM,
        cost_estimate=FREE,
    )(me, *parts)


def small_sum(value, axes):
    for axis in axes:
        size = lax.axis_size(axis)
        if size & (size - 1):
            value = lax.psum(value, axis)
            continue
        bit = 1
        while bit < size:
            value = value + lax.ppermute(value, axis, [(i, i ^ bit) for i in range(size)])
            bit *= 2
    return value


def go_up(value, first, last):
    return lax.ppermute(value, "col", [(i, i + 1) for i in range(first, last + 1)])


def go_down(value, first, last):
    return lax.ppermute(value, "col", [(i, i - 1) for i in range(first, last + 1)])


def row_join(parts, axis):
    row = lax.axis_index("row")
    if len(parts) == 2:
        low = row == 0
        parts = [jnp.where(low, parts[0], parts[1]), jnp.where(low, parts[1], parts[0])]
    else:
        parts = ordered(parts, row, 1)
    return jnp.concatenate(parts, axis)


def swap_all(value):
    return [swap_with(value, 1), swap_with(value, 2), swap_with(value, 3)]


class Heads:
    def __init__(self, n_col, width, heads, blocks):
        self.size = n_col * width // heads
        self.firsts = [width * c // self.size for c in range(n_col)]
        lasts = [-(-width * (c + 1) // self.size) for c in range(n_col)]
        self.slots = max(b - a for a, b in zip(self.firsts, lasts))
        self.window = self.slots * self.size
        self.before = [width * c - f * self.size for c, f in enumerate(self.firsts)]
        self.after = [self.window - width - b for b in self.before]
        self.edge = max(self.before + self.after)
        full = (1 << blocks) - 1
        shares = {0: 0, 1: 2, 2: 9, 3: 13, 4: 15}

        def left_share(column):
            part = column % self.size
            return shares[round(4 * part / self.size)] if blocks == 4 else 0

        self.first_mask = [full & ~left_share(b) for b in self.before]
        self.last_mask = []
        for c, f in enumerate(self.firsts):
            end = width * (c + 1)
            begin = (f + self.slots - 1) * self.size
            if begin >= end:
                self.last_mask.append(0)
            elif begin + self.size <= end:
                self.last_mask.append(full)
            else:
                self.last_mask.append(left_share(end - begin))


def edges(value, axis, heads):
    n = lax.axis_size("col")
    edge, width = heads.edge, value.shape[axis]
    left = go_up(lax.slice_in_dim(value, width - edge, width, axis=axis), 0, n - 2)
    right = go_down(lax.slice_in_dim(value, 0, edge, axis=axis), 1, n - 1)
    return left, right


def widen(value, left, right, axis, heads, col):
    wide = jnp.concatenate([left, value, right], axis)
    before = jnp.array(heads.before, jnp.int32)[col]
    return lax.dynamic_slice_in_dim(wide, heads.edge - before, heads.window, axis)


def narrow_edges(value, axis, heads, col, width):
    n = lax.axis_size("col")
    edge = heads.edge
    before = jnp.array(heads.before, jnp.int32)[col]
    shape = list(value.shape)
    shape[axis] = width + 2 * edge
    wide = lax.dynamic_update_slice_in_dim(
        jnp.zeros(shape, value.dtype), value, edge - before, axis
    )
    tail = go_down(lax.slice_in_dim(wide, 0, edge, axis=axis), 1, n - 1)
    front = go_up(lax.slice_in_dim(wide, edge + width, width + 2 * edge, axis=axis), 0, n - 2)
    return wide, front, tail


def narrow(wide, front, tail, axis, heads, width):
    edge = heads.edge
    pads = [(0, 0)] * wide.ndim
    pads[axis] = (0, width - edge)
    own = lax.slice_in_dim(wide, edge, edge + width, axis=axis).astype(F32)
    own = own + jnp.pad(front, pads).astype(F32)
    pads[axis] = (width - edge, 0)
    return own + jnp.pad(tail, pads).astype(F32)


def moments(values):
    mean = jnp.mean(values, axis=0, keepdims=True)
    centred = values - mean
    variance = jnp.mean(centred * centred, axis=0, keepdims=True)
    return mean, lax.rsqrt(variance + EPSILON)


def body(
    tokens,
    cotangent,
    w_qkv,
    q_bias,
    v_bias,
    w_out,
    out_bias,
    w_up,
    up_bias,
    w_down,
    down_bias,
    ln1_gain,
    ln1_bias,
    ln2_gain,
    ln2_bias,
    key_start,
):
    n_row, n_col = lax.axis_size("row"), lax.axis_size("col")
    row, col = lax.axis_index("row"), lax.axis_index("col")
    seqs, rows, width = tokens.shape
    length = seqs * rows
    depth = width * n_col
    part = length // n_col
    in_rows = w_up.shape[0]
    ff = w_up.shape[1]
    ff_rows = w_down.shape[0]
    ff_part = ff_rows // n_col
    heads = Heads(n_col, width, key_start.shape[0], rows * n_row // BLK)
    size, window = heads.size, heads.window
    firsts = jnp.array(heads.firsts, jnp.int32) * size
    begin = firsts[col]

    shares = Shares(width)
    dp = lax.axis_index("dp")
    row_at = row[None].astype(jnp.int32)
    col_at = col[None].astype(jnp.int32)
    other_rows = [((row + i) % n_row)[None].astype(jnp.int32) for i in range(n_row)]


    x = tokens.reshape(length, width).T
    g = cotangent.reshape(length, width).T
    place_in = col * n_row + row
    half = n_col // 2

    def between_owners(value_of, steps, back):
        got = []
        for step in steps:
            pairs = []
            for r in range(n_row):
                for c in range(n_col):
                    to = r * n_col + (c - step) % n_col
                    here, there = r * n_col + c, (to % n_row) * n_col + to // n_row
                    pairs.append((there, here) if back else (here, there))
            got.append(lax.ppermute(value_of(step), ("row", "col"), pairs))
        return got

    x_all = lax.all_gather(x, "col", axis=0, tiled=True)
    wq = w_qkv.transpose(0, 2, 1)
    w3_own = widen(wq, *edges(wq, 1, heads), 1, heads, col)
    w3_parts = [w3_own] + [turn(w3_own, "row", -step) for step in range(1, n_row)]
    w3 = row_join(w3_parts, 2).reshape(3 * window, depth)
    params = jnp.stack([ln1_gain, ln1_bias, ln2_gain, ln2_bias, out_bias, q_bias, v_bias])
    params = [turn(params, "col", step) for step in range(n_col)]
    params = jnp.concatenate(ordered(params, col, -1), 1)
    gain1, shift1, gain2, shift2, bias_out, bias_q, bias_v = [p[:, None] for p in params]
    bias3 = jnp.concatenate(
        [
            lax.dynamic_slice_in_dim(bias_q, begin, window, 0),
            jnp.zeros((window, 1), F32),
            lax.dynamic_slice_in_dim(bias_v, begin, window, 0),
        ]
    )
    columns = jnp.concatenate([gain1, shift1, bias_out, jnp.zeros((depth, 1), F32)], 1)
    meta = jnp.stack(
        [
            jnp.array(heads.firsts, jnp.int32)[col],
            row,
            jnp.array(heads.first_mask, jnp.int32)[col],
            jnp.array(heads.last_mask, jnp.int32)[col],
        ]
    )
    up_parts = [w_up] + [turn(w_up, "row", -step) for step in range(1, n_row)]
    up_turned = row_join(up_parts, 0).T
    out_own = shares.take(w_out.T, dp, 0)
    down_own = shares.take(w_down.T, dp, 0)
    x_all, g, out_own, down_own, w3, meta, columns, bias3 = gate(
        [x_all, g, out_own, down_own, w3, meta, columns, bias3], [up_turned]
    )

    g_all = lax.all_gather(g, "col", axis=0, tiled=True)
    moved_out = [out_own] + [turn(out_own, "col", -step) for step in range(1, n_col)]
    x_float = x_all.astype(F32)
    mean1, rstd1 = moments(x_float)
    n1 = ((x_float - mean1) * rstd1 * gain1 + shift1).astype(BF16)
    triple = product(w3, n1, bias3).reshape(3, window, length)
    triple, *rest = gate([triple] + moved_out[1:], [])
    moved_out = moved_out[:1] + rest

    pieces = [triple] + [turn(triple, "row", -step) for step in range(1, n_row)]
    moved_out = jnp.stack(ordered(moved_out, col, 1))
    moved_out, *rest = gate([moved_out] + pieces[1:], [])
    pieces = pieces[:1] + rest

    near_out = [swap_with(moved_out, 1), swap_with(moved_out, 2)]
    *cuts, mixed, norms = attn_fwd(meta, key_start, pieces, heads.slots, size)
    *cuts, near_x, near_y, g_all = gate(list(cuts) + near_out + [g_all], [])

    half = n_col // 2
    far_out = [swap_with(near_x[:half], 2), swap_with(near_y[half:], 1)]
    mixed_own = row_sum(cuts).astype(BF16)
    mixed_own, *far_out = gate([mixed_own] + far_out, [])

    dp_at = dp[None].astype(jnp.int32)
    got = [
        turn(block(mixed_own, (col + step) % n_col, part, 1), "col", step) for step in range(n_col)
    ]
    out_weights = assemble([moved_out, near_x, near_y] + far_out, shares, dp_at)
    out_weights = [out_weights] + [turn(out_weights, "row", -step) for step in range(1, n_row)]
    down_own, *rest = gate([down_own] + got[1:] + out_weights[1:], [])
    got = got[:1] + rest[: n_col - 1]
    out_weights = out_weights[:1] + rest[n_col - 1 :]
    out_weights = [w.reshape(depth, in_rows) for w in out_weights]

    moved_down = between_owners(
        lambda step: block(down_own, (col - step) % n_col, ff_part, 1), range(n_col), False
    )
    got = ordered(got, col, -1)
    lapped = [heads.firsts[j] * size for j in range(n_col)]
    attention = sum(
        jnp.pad(piece, ((at, depth - at - window), (0, 0))) for piece, at in zip(got, lapped)
    )
    branch = split_product(out_weights, attention, row_at, columns, 2, F32)
    resid = block(x_all, col, part, 1).astype(F32) + branch
    mean2, rstd2 = moments(resid)
    hat2 = (resid - mean2) * rstd2
    n2_own = (hat2 * gain2 + shift2).astype(BF16)
    n2_own, g, *moved_down = gate([n2_own, g] + moved_down, [hat2])

    n2_all = lax.all_gather(n2_own, "col", axis=1, tiled=True)
    moved_down = jnp.stack(ordered(moved_down, place_in, 1))
    down_weights = assemble([moved_down] + swap_all(moved_down), shares, dp_at)
    down_weights = [turn(down_weights, "row", -step) for step in range(n_row)]
    down_weights = [w.reshape(depth, ff_part) for w in down_weights]
    down_turned = turned(down_weights)
    g_sums = jnp.sum(g.astype(F32), axis=1)
    n2_all, down_turned = gate([n2_all, down_turned], [g_sums])

    hidden_all, du_all, part2 = hidden_layer(
        up_turned, down_turned, n_row, up_bias[:, None], n2_all, g_all, row_at
    )
    part2, hidden_all, du_all = gate([part2, hidden_all, du_all], [])

    dn2 = lax.psum_scatter(part2, "col", scatter_dimension=1, tiled=True)
    up_grad = [token_product(n2_all, du_all, r, n_row, True) for r in other_rows[::-1]][::-1]
    down_grad = [token_product(g_all, hidden_all, r, n_row, False) for r in other_rows[::-1]][::-1]
    down_grad = [d.reshape(n_col, width, ff_part) for d in down_grad]
    up_grad = up_grad[:1] + [turn(p, "row", i) for i, p in enumerate(up_grad) if i]
    down_grad = down_grad[:1] + [turn(p, "row", i) for i, p in enumerate(down_grad) if i]
    hidden_all, *rest = gate([hidden_all] + up_grad + down_grad, [])
    up_grad, down_grad = rest[:n_row], rest[n_row:]

    up_grad = sum(p.astype(F32) for p in up_grad).astype(BF16)
    down_grad = sum(p.astype(F32) for p in down_grad).astype(BF16)
    up_rows = width if in_rows % width == 0 else in_rows
    up_shares = Shares(up_rows)
    up_grad = up_grad.reshape(in_rows // up_rows, up_rows, ff)

    def first_sum(value, cut, bit):
        sent = [cut.take(value, dp ^ bit, 1), cut.take(value, dp ^ 3, 1)]
        return swap_with(jnp.stack(sent), bit)

    def relay(value, first, cut, bit):
        sent = cut.take(value, dp ^ (3 - bit), 1).astype(F32) + first[1].astype(F32)
        return swap_with(sent.astype(BF16), 3 - bit)

    def share_sum(value, cut, first, relayed):
        own = cut.take(value, dp, 1).astype(F32)
        return (own + first[0].astype(F32) + relayed.astype(F32)).astype(BF16)

    up_first = first_sum(up_grad, up_shares, 1)
    down_first = first_sum(down_grad, shares, 2)
    shrunk = split_product(down_weights, hidden_all, row_at, columns, 3, BF16)
    own_sum = block(shrunk, col, part, 1).astype(F32) + resid
    shrunk = lax.dynamic_update_slice_in_dim(shrunk, own_sum.astype(BF16), col * part, 1)
    du_sums = jnp.sum(du_all.astype(F32), axis=1)
    dn2, shrunk = gate([dn2, shrunk], [du_sums])

    dn2 = dn2.astype(F32)
    up2 = dn2 * gain2
    pull2 = jnp.mean(up2, axis=0, keepdims=True)
    lean2 = jnp.mean(up2 * hat2, axis=0, keepdims=True)
    dr = block(g_all, col, part, 1).astype(F32) + rstd2 * (up2 - pull2 - hat2 * lean2)
    db = dr.astype(BF16)
    da = split_product_tn(out_weights, db, row_at)
    sums2 = jnp.stack(
        [
            jnp.sum(db.astype(F32), axis=1),
            jnp.sum(dn2 * hat2, axis=1),
            jnp.sum(dn2, axis=1),
        ]
    )
    da, db, shrunk, up_first, down_first = gate([da, db, shrunk, up_first, down_first], [sums2])

    got = []
    for step in range(n_col):
        to = firsts[(col + step) % n_col]
        got.append(turn(lax.dynamic_slice_in_dim(da, to, window, 0), "col", step))
    up_relay = relay(up_grad, up_first, up_shares, 1)
    down_relay = relay(down_grad, down_first, shares, 2)
    out_grad = [token_product(db, attention, r, n_row, False) for r in other_rows[::-1]][::-1]
    out_grad = [o.reshape(n_col, width, in_rows) for o in out_grad]
    rest = gate(got[1:] + out_grad + [up_relay, down_relay, shrunk], [])
    got, rest = got[:1] + rest[: n_col - 1], rest[n_col - 1 :]
    out_grad, (up_relay, down_relay, shrunk) = rest[:n_row], rest[n_row:]

    outputs = lax.psum_scatter(shrunk, "col", scatter_dimension=0, tiled=True)
    da_own = jnp.concatenate(ordered(got, col, -1), 1)
    da_pieces = [da_own] + [turn(da_own, "row", -step) for step in range(1, n_row)]
    out_grad = row_sum(out_grad).astype(BF16)
    up_share = share_sum(up_grad, up_shares, up_first, up_relay)
    down_share = share_sum(down_grad, shares, down_first, down_relay)
    out_cuts = [(out_grad[:half], 1), (out_grad[half:], 2)]
    out_sent = [
        jnp.stack([shares.take(v, dp ^ bit, 1), shares.take(v, dp ^ 3, 1)]) for v, bit in out_cuts
    ]
    *rest, up_share, down_share = gate(da_pieces[1:] + out_sent + [up_share, down_share], [])
    da_pieces, out_sent = [da_own] + rest[: n_row - 1], rest[n_row - 1 :]

    out_first = [swap_with(v, bit) for v, (_, bit) in zip(out_sent, out_cuts)]
    up_near = [swap_with(up_share, 1), swap_with(up_share, 2)]
    dqkv = attn_bwd(meta, key_start, pieces, da_pieces, mixed, norms, heads.slots, size)
    *rest, down_share = gate(list(dqkv) + up_near + out_first + [down_share], [])
    dqkv, up_near, out_first = rest[:n_row], rest[n_row : n_row + 2], rest[n_row + 2 :]

    down_home = between_owners(
        lambda step: pick(down_share, (place_in + step) % n_col), range(n_col), True
    )
    dqkv = row_sum(dqkv).astype(BF16).reshape(3 * window, length)
    *rest, dqkv, outputs = gate(down_home + out_first + up_near + [dqkv, outputs], [])
    down_home, out_first, up_near = rest[:n_col], rest[n_col : n_col + 2], rest[n_col + 2 :]

    homes = jnp.stack(ordered(down_home, col, -1))
    homes_near = [swap_with(homes, 1), swap_with(homes, 2)]
    out_relay = [relay(v, f, shares, bit) for (v, bit), f in zip(out_cuts, out_first)]
    qkv_parts = [token_product(dqkv, n1, r, n_row, False) for r in other_rows[::-1]][::-1]
    qkv_parts = [q.reshape(3, window, in_rows) for q in qkv_parts]
    qkv_grad = row_sum(qkv_parts).astype(BF16)
    dqkv, qkv_grad, *rest = gate([dqkv, qkv_grad] + out_relay + homes_near, [])
    out_relay, homes_near = rest[:2], rest[2:]

    out_share = [
        share_sum(v, shares, f, r) for (v, _), f, r in zip(out_cuts, out_first, out_relay)
    ]
    out_home = lax.psum_scatter(
        jnp.concatenate(out_share), "col", scatter_dimension=0, tiled=True
    )
    wide, front, tail = narrow_edges(qkv_grad, 1, heads, col, width)
    homes_far = swap_with(homes_near[0], 2)
    up_far = swap_with(up_near[1], 1)
    dn1, norm1 = norm_product_tn(w3, dqkv, n1, columns, rstd1, dr, col_at, n_col)
    dn1, front, tail, dqkv, out_home, homes_far, up_far, outputs = gate(
        [dn1, front, tail, dqkv, out_home, homes_far, up_far, outputs], [norm1]
    )

    dx = lax.psum_scatter(dn1, "col", scatter_dimension=0, tiled=True)
    qkv_grad = narrow(wide, front, tail, 1, heads, width).astype(BF16)
    qkv_got = [swap_with(shares.take(qkv_grad, dp ^ m, 1), m) for m in (1, 2, 3)]
    out_near = [swap_with(out_home, 1), swap_with(out_home, 2)]
    dq_dv = jnp.sum(dqkv.astype(F32), axis=1).reshape(3, window)
    sums = lax.dynamic_update_slice_in_dim(jnp.zeros((2, depth), F32), dq_dv[::2], begin, 1)
    sums = jnp.concatenate([sums, (norm1[:, :1] / gain1).T, norm1[:, 1:].T, sums2]).reshape(-1)
    small = jnp.concatenate([sums, du_sums, g_sums])[None]
    small, outputs, up_far, homes_far, *rest = gate(
        [small, outputs, up_far, homes_far] + out_near + qkv_got, []
    )
    out_near, qkv_got = rest[:2], rest[2:]

    qkv_share = shares.take(qkv_grad, dp, 1).astype(F32)
    qkv_share = (qkv_share + sum(q.astype(F32) for q in qkv_got)).astype(BF16)
    qkv_all = swap_all(qkv_share)
    out_far = swap_with(out_near[0], 2)
    small = small_sum(small, ("row",))[0]
    sums, local = small[: 7 * depth].reshape(7, depth), small[7 * depth :]
    sums = small_sum(sums, ("col",))
    sums = lax.dynamic_slice_in_dim(sums, col * width, width, 1)
    small = jnp.concatenate([sums.reshape(-1), local])[None]
    small = small_sum(small, ("dp",))[0]
    sums, local = small[: 7 * width].reshape(7, width), small[7 * width :]
    up_grad = up_shares.join([up_share] + up_near + [up_far], dp, 1).astype(F32)
    up_grad = up_grad.reshape(in_rows, ff)
    homes = shares.join([homes] + homes_near + [homes_far], dp, 1).astype(F32)
    down_grad = jnp.concatenate([homes[j] for j in range(n_col)], 1)
    outputs = (outputs.astype(F32) + down_bias[:, None]).astype(BF16)
    hat1 = (x.astype(F32) - mean1) * rstd1
    dx = dx.reshape(width + 16, length)
    lines = dx[width : width + 4].astype(F32)
    lines = (lines[0::2] + lines[1::2]) / depth
    input_grad = dx[:width].astype(F32) - rstd1 * (lines[0:1] + hat1 * lines[1:2])
    input_grad = input_grad.astype(BF16)
    out_far, *qkv_all = gate(
        [out_far] + qkv_all, [sums, local, up_grad, down_grad, outputs, input_grad]
    )

    out_grad = shares.join([out_home] + out_near + [out_far], dp, 1).astype(F32)[0]
    qkv_grad = shares.join([qkv_share] + qkv_all, dp, 1).astype(F32)
    return (
        outputs.T.reshape(tokens.shape),
        input_grad.T.reshape(tokens.shape),
        qkv_grad.transpose(0, 2, 1),
        sums[0],
        sums[1],
        out_grad.T,
        sums[4],
        up_grad,
        local[:ff],
        down_grad.T,
        local[ff:],
        sums[2],
        sums[3],
        sums[5],
        sums[6],
    )


def solution(mesh):
    inputs = (
        P("dp", "row", "col"),
        P("dp", "row", "col"),
        P(None, "row", "col"),
        P("col"),
        P("col"),
        P("row", "col"),
        P("col"),
        P("row", "col"),
        P("col"),
        P("row", "col"),
        P("col"),
        P("col"),
        P("col"),
        P("col"),
        P("col"),
        P(),
    )
    return jax.shard_map(
        body, mesh=mesh, in_specs=inputs, out_specs=inputs[:15], check_vma=False
    )
```

```python
import functools

import jax
import jax.numpy as jnp
from jax import lax
from jax.experimental import pallas as pl
from jax.experimental.pallas import tpu as pltpu
from jax.sharding import PartitionSpec as P

BLK = 512
EPSILON = 1e-05
LOG2E = 1.4426950408889634
BF16 = jnp.bfloat16
F32 = jnp.float32

FREE = pl.CostEstimate(flops=0, bytes_accessed=0, transcendentals=0)
ROOM = pltpu.CompilerParams(vmem_limit_bytes=56 * 2**20)

NT=(((0,),(0,)),((),()))
TN=(((1,),(1,)),((),()))

def plan_tiles(meta, ks, own, load, n_slots, n_blocks, n_row, n_heads):
    for i in range(n_row): load[i]=0
    def level(lv,_):
        cost=n_blocks-lv
        def tile(t,_):
            slot=t//n_blocks; qb=t%n_blocks
            head=meta[0]+slot
            here=head<n_heads
            hd=jnp.minimum(head,n_heads-1)
            n=qb+1-ks[hd,qb]
            mask=jnp.where(slot==0,meta[2],jnp.where(slot==n_slots-1,meta[3],(1<<n_blocks)-1))
            here=jnp.logical_and(here,((mask>>qb)&1)==1)
            @pl.when(cost==n_blocks)
            def _(): own[t]=-1
            @pl.when(jnp.logical_and(here,n==cost))
            def _():
                best=load[0]; who=jnp.int32(0)
                for i in range(1,n_row):
                    less=load[i]<best
                    best=jnp.where(less,load[i],best); who=jnp.where(less,i,who)
                own[t]=who
                load[who]=best+cost
            return 0
        lax.fori_loop(0,n_slots*n_blocks,tile,0)
        return 0
    lax.fori_loop(0,n_blocks,level,0)

def fetch(pieces, whole, sems, row, n_row, width):
    copies=[]
    for i,p in enumerate(pieces):
        at=lax.rem(row+i,n_row)*width
        c=pltpu.make_async_copy(p, whole.at[...,pl.ds(pl.multiple_of(at,width),width)], sems.at[i])
        c.start(); copies.append(c)
    return copies

def fwd_kernel(n_row,n_slots,hd,n_heads,meta,ks,*refs):
    pieces=refs[:n_row]; cuts=refs[n_row:2*n_row]; o_ref,lse_ref,whole,own,load,sems=refs[2*n_row:]
    S=whole.shape[2]; nb=S//BLK; width=S//n_row
    row=meta[1]
    copies=fetch(pieces,whole,sems,row,n_row,width)
    plan_tiles(meta,ks,own,load,n_slots,nb,n_row,n_heads)
    o_ref[...]=jnp.zeros_like(o_ref)
    for c in copies: c.wait()
    c2=hd**-0.5*LOG2E
    diag=lax.broadcasted_iota(jnp.int32,(BLK,BLK),0)<=lax.broadcasted_iota(jnp.int32,(BLK,BLK),1)
    def tile(t,_):
        @pl.when(own[t]==row)
        def _():
            slot=t//nb; qb=t%nb
            first=ks[meta[0]+slot,qb]
            hs=pl.ds(pl.multiple_of(slot*hd,hd),hd)
            qs=pl.ds(pl.multiple_of(qb*BLK,BLK),BLK)
            q=whole[0,hs,qs]
            def scores(kb_ds):
                return lax.dot_general(whole[1,hs,kb_ds],q,NT,preferred_element_type=jnp.float32)
            s=jnp.where(diag,scores(qs),-1e30)
            m=jnp.max(s,axis=0,keepdims=True)
            p=jnp.exp2((s-m)*c2)
            l=jnp.sum(p,axis=0,keepdims=True)
            acc=jnp.dot(whole[2,hs,qs],p.astype(jnp.bfloat16),preferred_element_type=jnp.float32)
            def step(kb,carry):
                m,l,acc=carry
                kd=pl.ds(pl.multiple_of(kb*BLK,BLK),BLK)
                s=scores(kd)
                mn=jnp.maximum(m,jnp.max(s,axis=0,keepdims=True))
                a=jnp.exp2((m-mn)*c2)
                p=jnp.exp2((s-mn)*c2)
                l=l*a+jnp.sum(p,axis=0,keepdims=True)
                acc=acc*a+jnp.dot(whole[2,hs,kd],p.astype(jnp.bfloat16),preferred_element_type=jnp.float32)
                return mn,l,acc
            m,l,acc=lax.fori_loop(first,qb,step,(m,l,acc))
            o_ref[hs,qs]=(acc/l).astype(jnp.bfloat16)
            lse_ref[pl.ds(slot,1),qs]=m*c2+jnp.log2(l)
        return 0
    lax.fori_loop(0,n_slots*nb,tile,0)
    for i,cut in enumerate(cuts):
        cut[...]=o_ref[:,pl.ds(pl.multiple_of(lax.rem(row+i,n_row)*width,width),width)]

def bwd_kernel(n_row,n_slots,hd,n_heads,meta,ks,*refs):
    pieces=refs[:n_row]; das=refs[n_row:2*n_row]
    o_ref,lse_ref=refs[2*n_row:2*n_row+2]; cuts=refs[2*n_row+2:3*n_row+2]
    d_ref,whole,da,acc,own,load,sems,sems2=refs[3*n_row+2:]
    S=whole.shape[2]; nb=S//BLK; width=S//n_row
    row=meta[1]
    copies=fetch(pieces,whole,sems,row,n_row,width)+fetch(das,da,sems2,row,n_row,width)
    plan_tiles(meta,ks,own,load,n_slots,nb,n_row,n_heads)
    d_ref[...]=jnp.zeros_like(d_ref)
    acc[...]=jnp.zeros_like(acc)
    for c in copies: c.wait()
    scale=hd**-0.5; c2=scale*LOG2E
    diag=lax.broadcasted_iota(jnp.int32,(BLK,BLK),0)<=lax.broadcasted_iota(jnp.int32,(BLK,BLK),1)
    def tile(t,_):
        @pl.when(own[t]==row)
        def _():
            slot=t//nb; qb=t%nb
            first=ks[meta[0]+slot,qb]
            hs=pl.ds(pl.multiple_of(slot*hd,hd),hd)
            qs=pl.ds(pl.multiple_of(qb*BLK,BLK),BLK)
            q=whole[0,hs,qs]
            up=da[hs,qs]
            lse=lse_ref[pl.ds(slot,1),qs]
            delta=jnp.sum(up.astype(jnp.float32)*o_ref[hs,qs].astype(jnp.float32),axis=0,keepdims=True)
            def block(kd,masked):
                k=whole[1,hs,kd]
                s=lax.dot_general(k,q,NT,preferred_element_type=jnp.float32)
                p=jnp.exp2(s*c2-lse)
                if masked: p=jnp.where(diag,p,0.0)
                dp=lax.dot_general(whole[2,hs,kd],up,NT,preferred_element_type=jnp.float32)
                ds=(p*(dp-delta)).astype(jnp.bfloat16)
                acc[1,hs,kd]+=lax.dot_general(up,p.astype(jnp.bfloat16),TN,preferred_element_type=jnp.float32)
                acc[0,hs,kd]+=lax.dot_general(q,ds,TN,preferred_element_type=jnp.float32)
                return jnp.dot(k,ds,preferred_element_type=jnp.float32)
            dq=block(qs,True)
            dq=lax.fori_loop(first,qb,lambda kb,dq:dq+block(pl.ds(pl.multiple_of(kb*BLK,BLK),BLK),False),dq)
            d_ref[hs,qs]=(dq*scale).astype(jnp.bfloat16)
        return 0
    lax.fori_loop(0,n_slots*nb,tile,0)
    for i,cut in enumerate(cuts):
        at=pl.ds(pl.multiple_of(lax.rem(row+i,n_row)*width,width),width)
        cut[0]=d_ref[:,at]
        cut[1]=(acc[0,:,at]*scale).astype(jnp.bfloat16)
        cut[2]=acc[1,:,at].astype(jnp.bfloat16)

V=pl.BlockSpec(memory_space=pltpu.VMEM); SM=pl.BlockSpec(memory_space=pltpu.SMEM); ANY=pl.BlockSpec(memory_space=pl.ANY)
def attn_fwd(meta,ks,pieces,n_slots,hd):
    n_row=len(pieces); _,H,T=pieces[0].shape; S=T*n_row; nb=S//BLK
    return pl.pallas_call(functools.partial(fwd_kernel,n_row,n_slots,hd,ks.shape[0]),
      out_shape=[jax.ShapeDtypeStruct((H,T),jnp.bfloat16)]*n_row+[jax.ShapeDtypeStruct((H,S),jnp.bfloat16),jax.ShapeDtypeStruct((n_slots,S),jnp.float32)],
      in_specs=[SM,SM]+[ANY]*n_row,out_specs=[V]*(n_row+2),
      scratch_shapes=[pltpu.VMEM((3,H,S),jnp.bfloat16),pltpu.SMEM((n_slots*nb,),jnp.int32),pltpu.SMEM((n_row,),jnp.int32),pltpu.SemaphoreType.DMA((n_row,))],
      compiler_params=pltpu.CompilerParams(vmem_limit_bytes=48*2**20),
      cost_estimate=FREE,
    )(meta,ks,*pieces)
def attn_bwd(meta,ks,pieces,das,o,lse,n_slots,hd):
    n_row=len(pieces); _,H,T=pieces[0].shape; S=T*n_row; nb=S//BLK
    return pl.pallas_call(functools.partial(bwd_kernel,n_row,n_slots,hd,ks.shape[0]),
      out_shape=[jax.ShapeDtypeStruct((3,H,T),jnp.bfloat16)]*n_row,
      in_specs=[SM,SM]+[ANY]*(2*n_row)+[V,V],out_specs=[V]*n_row,
      scratch_shapes=[pltpu.VMEM((H,S),jnp.bfloat16),pltpu.VMEM((3,H,S),jnp.bfloat16),pltpu.VMEM((H,S),jnp.bfloat16),pltpu.VMEM((2,H,S),jnp.float32),pltpu.SMEM((n_slots*nb,),jnp.int32),pltpu.SMEM((n_row,),jnp.int32),pltpu.SemaphoreType.DMA((n_row,)),pltpu.SemaphoreType.DMA((n_row,))],
      compiler_params=pltpu.CompilerParams(vmem_limit_bytes=56*2**20),
      cost_estimate=FREE,
    )(meta,ks,*pieces,*das,o,lse)


def rows_of(total, most):
    for rows in range(min(total, most) // 16 * 16, 0, -16):
        if total % rows == 0:
            return rows
    return total


def by_rows(i, *refs):
    return (i, 0)


def whole_block(i, *refs):
    return (0, 0)


def product_kernel(a_ref, b_ref, bias_ref, o_ref):
    o_ref[...] = (
        jnp.dot(a_ref[...], b_ref[...], preferred_element_type=F32) + bias_ref[...]
    ).astype(o_ref.dtype)


def product(a, b, bias):
    rows = rows_of(a.shape[0], 448)
    return pl.pallas_call(
        product_kernel,
        out_shape=jax.ShapeDtypeStruct((a.shape[0], b.shape[1]), BF16),
        grid=(a.shape[0] // rows,),
        in_specs=[
            pl.BlockSpec((rows, a.shape[1]), by_rows),
            pl.BlockSpec(b.shape, whole_block),
            pl.BlockSpec((rows, 1), by_rows),
        ],
        out_specs=pl.BlockSpec((rows, b.shape[1]), by_rows),
        compiler_params=ROOM,
        cost_estimate=FREE,
    )(a, b, bias)


def split_product(parts, b, row, columns, which, dtype):
    n = len(parts)
    total, depth = parts[0].shape
    width = b.shape[1]
    rows = rows_of(total, 400)

    def kernel(row_ref, b_ref, bias_ref, *refs):
        out = bias_ref[:, which : which + 1] + jnp.zeros((rows, width), F32)
        for i in range(n):
            at = pl.multiple_of(lax.rem(row_ref[0] + i, n) * depth, 8)
            out = out + jnp.dot(refs[i][...], b_ref[pl.ds(at, depth), :], preferred_element_type=F32)
        refs[n][...] = out.astype(dtype)

    return pl.pallas_call(
        kernel,
        out_shape=jax.ShapeDtypeStruct((total, width), dtype),
        grid=(total // rows,),
        in_specs=[
            SM,
            pl.BlockSpec(b.shape, whole_block),
            pl.BlockSpec((rows, columns.shape[1]), by_rows),
        ]
        + [pl.BlockSpec((rows, depth), by_rows)] * n,
        out_specs=pl.BlockSpec((rows, width), by_rows),
        compiler_params=ROOM,
        cost_estimate=FREE,
    )(row, b, columns, *parts)


def split_product_tn(parts, b, row):
    n = len(parts)
    depth = parts[0].shape[1]
    total, width = b.shape
    rows = rows_of(total, 400)
    steps = total // rows

    def kernel(row_ref, b_ref, *refs):
        o_ref, acc = refs[n:]

        @pl.when(pl.program_id(0) == 0)
        def start():
            acc[...] = jnp.zeros_like(acc)

        for i in range(n):
            at = pl.multiple_of(lax.rem(row_ref[0] + i, n) * depth, 8)
            acc[pl.ds(at, depth), :] += lax.dot_general(
                refs[i][...], b_ref[...], NT, preferred_element_type=F32
            )

        @pl.when(pl.program_id(0) == steps - 1)
        def end():
            o_ref[...] = acc[...].astype(BF16)

    return pl.pallas_call(
        kernel,
        out_shape=jax.ShapeDtypeStruct((n * depth, width), BF16),
        grid=(steps,),
        in_specs=[SM, pl.BlockSpec((rows, width), by_rows)]
        + [pl.BlockSpec((rows, depth), by_rows)] * n,
        out_specs=pl.BlockSpec((n * depth, width), whole_block),
        scratch_shapes=[pltpu.VMEM((n * depth, width), F32)],
        compiler_params=ROOM,
        cost_estimate=FREE,
    )(row, b, *parts)


def norm_product_tn(a, b, normed, columns, scale, riding, col, n_col):
    rows = rows_of(a.shape[0], 448)
    steps = a.shape[0] // rows
    depth, tokens = a.shape[1], b.shape[1]
    cut, part = depth // n_col, tokens // n_col

    def kernel(col_ref, a_ref, b_ref, n_ref, g_ref, c_ref, r_ref, o_ref, f_ref, acc):
        @pl.when(pl.program_id(0) == 0)
        def start():
            acc[...] = lax.dot_general(a_ref[...], b_ref[...], NT, preferred_element_type=F32)

        @pl.when(pl.program_id(0) > 0)
        def more():
            acc[...] += lax.dot_general(a_ref[...], b_ref[...], NT, preferred_element_type=F32)

        @pl.when(pl.program_id(0) == steps - 1)
        def end():
            first = jnp.zeros((1, tokens), F32)
            second = jnp.zeros((1, tokens), F32)
            for j in range(n_col):
                at = pl.ds(j * cut, cut)
                p = acc[at, :]
                scaled = p * g_ref[at, 0:1]
                o_ref[j, 0:cut, :] = (scaled * c_ref[...]).astype(BF16)
                moved = p * (n_ref[at, :].astype(F32) - g_ref[at, 1:2])
                first += jnp.sum(scaled, axis=0, keepdims=True)
                second += jnp.sum(moved, axis=0, keepdims=True)
                f_ref[at, 0:1] = jnp.sum(moved, axis=1, keepdims=True) / g_ref[at, 0:1]
                f_ref[at, 1:2] = jnp.sum(p, axis=1, keepdims=True)
                for c in range(n_col):

                    @pl.when(col_ref[0] == c)
                    def ride():
                        here = slice(c * part, (c + 1) * part)
                        own = scaled[:, here] * c_ref[:, here] + r_ref[at, :]
                        o_ref[j, 0:cut, here] = own.astype(BF16)

            lines = []
            for line in (first, second):
                high = line.astype(BF16).astype(F32)
                lines += [high, line - high]
            lines = jnp.concatenate(lines + [jnp.zeros((12, tokens), F32)]).astype(BF16)
            for j in range(n_col):
                o_ref[j, cut : cut + 16, :] = lines

    return pl.pallas_call(
        kernel,
        out_shape=[
            jax.ShapeDtypeStruct((n_col, cut + 16, tokens), BF16),
            jax.ShapeDtypeStruct((depth, 2), F32),
        ],
        grid=(steps,),
        in_specs=[
            SM,
            pl.BlockSpec((rows, depth), by_rows),
            pl.BlockSpec((rows, tokens), by_rows),
            pl.BlockSpec((depth, tokens), whole_block),
            pl.BlockSpec(columns.shape, whole_block),
            pl.BlockSpec((1, tokens), whole_block),
            pl.BlockSpec((depth, part), whole_block),
        ],
        out_specs=[
            pl.BlockSpec((n_col, cut + 16, tokens), lambda i: (0, 0, 0)),
            pl.BlockSpec((depth, 2), whole_block),
        ],
        scratch_shapes=[pltpu.VMEM((depth, tokens), F32)],
        compiler_params=ROOM,
        cost_estimate=FREE,
    )(col, a, b, normed, columns, scale, riding)


def token_product(a, b, index, parts, of_a):
    rows_a = a.shape[0] // (parts if of_a else 1)
    rows_b = b.shape[0] // (1 if of_a else parts)
    rows = rows_of(rows_a, 448)
    steps = rows_a // rows

    def kernel(index_ref, a_ref, b_ref, o_ref):
        o_ref[...] = lax.dot_general(
            a_ref[...], b_ref[...], TN, preferred_element_type=F32
        ).astype(BF16)

    if of_a:
        a_map, b_map = (lambda i, r: (r[0] * steps + i, 0)), whole_block
    else:
        a_map, b_map = by_rows, (lambda i, r: (r[0], 0))
    return pl.pallas_call(
        kernel,
        out_shape=jax.ShapeDtypeStruct((rows_a, rows_b), BF16),
        grid_spec=pltpu.PrefetchScalarGridSpec(
            num_scalar_prefetch=1,
            grid=(steps,),
            in_specs=[
                pl.BlockSpec((rows, a.shape[1]), a_map),
                pl.BlockSpec((rows_b, b.shape[1]), b_map),
            ],
            out_specs=pl.BlockSpec((rows, rows_b), by_rows),
        ),
        compiler_params=ROOM,
        cost_estimate=FREE,
    )(index, a, b)


def gelu_parts(u):
    inner = 0.7978845608 * (u + 0.044715 * u * u * u)
    t = jnp.tanh(inner)
    value = 0.5 * u * (1.0 + t)
    slope = 0.5 * (1.0 + t) + 0.5 * u * (1.0 - t * t) * 0.7978845608 * (1.0 + 0.134145 * u * u)
    return value, slope


def hidden_layer(up, down, n, bias, n2, g, row):
    ff, depth = up.shape
    tokens = n2.shape[1]
    rows = rows_of(ff // n, 400)
    cuts = ff // n // rows
    steps = ff // rows

    def kernel(row_ref, up_ref, down_ref, bias_ref, n_ref, g_ref, h_ref, d_ref, p_ref, s_ref, acc):
        step = pl.program_id(0)
        u = jnp.dot(up_ref[...], n_ref[...], preferred_element_type=F32) + bias_ref[...]
        value, slope = gelu_parts(u)
        h_ref[...] = value.astype(BF16)
        dh = jnp.dot(down_ref[...], g_ref[...], preferred_element_type=F32)
        du = (dh * slope).astype(BF16)
        d_ref[...] = du
        s_ref[...] = jnp.sum(du.astype(F32), axis=1, keepdims=True)

        @pl.when(step == 0)
        def start():
            acc[...] = lax.dot_general(up_ref[...], du, NT, preferred_element_type=F32)

        @pl.when(step > 0)
        def more():
            acc[...] += lax.dot_general(up_ref[...], du, NT, preferred_element_type=F32)

        @pl.when(step == steps - 1)
        def end():
            p_ref[...] = acc[...].astype(BF16)

    mine = lambda i, r: (lax.rem(r[0] * cuts + i, steps), 0)
    full = lambda i, r: (0, 0)
    return pl.pallas_call(
        kernel,
        out_shape=[
            jax.ShapeDtypeStruct((ff, tokens), BF16),
            jax.ShapeDtypeStruct((ff, tokens), BF16),
            jax.ShapeDtypeStruct((depth, tokens), BF16),
            jax.ShapeDtypeStruct((ff, 1), F32),
        ],
        grid_spec=pltpu.PrefetchScalarGridSpec(
            num_scalar_prefetch=1,
            grid=(steps,),
            in_specs=[
                pl.BlockSpec((rows, depth), mine),
                pl.BlockSpec((rows, depth), lambda i, r: (i, 0)),
                pl.BlockSpec((rows, 1), mine),
                pl.BlockSpec((depth, tokens), full),
                pl.BlockSpec((depth, tokens), full),
            ],
            out_specs=[
                pl.BlockSpec((rows, tokens), mine),
                pl.BlockSpec((rows, tokens), mine),
                pl.BlockSpec((depth, tokens), full),
                pl.BlockSpec((rows, 1), mine),
            ],
            scratch_shapes=[pltpu.VMEM((depth, tokens), F32)],
        ),
        compiler_params=ROOM,
        cost_estimate=FREE,
    )(row, up, down, bias, n2, g)


def turned(parts):
    n = len(parts)
    depth, wide = parts[0].shape

    def kernel(*refs):
        o_ref = refs[n]
        for i in range(n):
            for first in range(0, wide, 256):
                size = min(256, wide - first)
                at = lax.broadcasted_iota(jnp.int32, (size, size), 0)
                ones = (at == lax.broadcasted_iota(jnp.int32, (size, size), 1)).astype(BF16)
                cut = refs[i][:, first : first + size]
                out = lax.dot_general(ones, cut, TN, preferred_element_type=F32)
                o_ref[i * wide + first : i * wide + first + size, :] = out.astype(BF16)

    return pl.pallas_call(
        kernel,
        out_shape=jax.ShapeDtypeStruct((n * wide, depth), BF16),
        in_specs=[V] * n,
        out_specs=V,
        compiler_params=ROOM,
        cost_estimate=FREE,
    )(*parts)


def gate(values, others):
    def kernel(*refs):
        pass

    out = pl.pallas_call(
        kernel,
        out_shape=[jax.ShapeDtypeStruct(v.shape, v.dtype) for v in values],
        in_specs=[ANY] * (len(values) + len(others)),
        out_specs=[ANY] * len(values),
        input_output_aliases={i: i for i in range(len(values))},
        cost_estimate=FREE,
    )(*values, *others)
    return list(out)


def turn(value, axis, steps):
    size = lax.axis_size(axis)
    if steps % size == 0:
        return value
    return lax.ppermute(value, axis, [(i, (i + steps) % size) for i in range(size)])


def block(value, index, size, axis):
    return lax.dynamic_slice_in_dim(value, index * size, size, axis)


def row_sum(parts):
    total = parts[0].astype(F32)
    for step in range(1, len(parts)):
        total = total + turn(parts[step], "row", step).astype(F32)
    return total


def swap_with(value, bit):
    return lax.ppermute(value, "dp", [(i, i ^ bit) for i in range(4)])


def pick(value, index, axis=0):
    return lax.dynamic_index_in_dim(value, index, axis, keepdims=False)


def dot(a, b):
    return jnp.dot(a, b, preferred_element_type=F32)


def ordered(parts, base, sign):
    size = len(parts)
    stacked = jnp.stack(parts)
    return [pick(stacked, (sign * (j - base)) % size) for j in range(size)]


class Shares:
    def __init__(self, rows, tile):
        self.rows = rows
        self.size = -(-rows // (4 * tile)) * tile
        self.starts = [(rows - self.size) * s // (3 * tile) * tile for s in range(3)]
        self.starts.append(rows - self.size)
        ends = self.starts[1:] + [rows]
        self.lengths = [b - a for a, b in zip(self.starts, ends)]

    def take(self, value, share, axis):
        start = jnp.array(self.starts, jnp.int32)[share]
        return lax.dynamic_slice_in_dim(value, start, self.size, axis)

    def lay(self, parts, axis):
        return jnp.concatenate(
            [lax.slice_in_dim(p, 0, n, axis=axis) for p, n in zip(parts, self.lengths)], axis
        )

    def join(self, parts, me, axis):
        odd, high = me % 2 == 1, me // 2 == 1
        picked = [
            jnp.where(
                high,
                jnp.where(odd, parts[3 ^ s], parts[2 ^ s]),
                jnp.where(odd, parts[1 ^ s], parts[s]),
            )
            for s in range(4)
        ]
        return self.lay(picked, axis)


def assemble(parts, shares, me):
    n, wide = parts[0].shape[0], parts[0].shape[2]

    def kernel(me_ref, *refs):
        o_ref, sems = refs[-2:]
        for act in ("start", "wait"):
            for m in range(4):
                for s in range(4):

                    @pl.when(me_ref[0] ^ m == s)
                    def move():
                        rows = pl.ds(0, shares.lengths[s])
                        to = pl.ds(shares.starts[s], shares.lengths[s])
                        pairs = [(refs[m].at[:, rows], o_ref.at[:, to])]
                        if m == 3 and len(parts) == 5:
                            low, high = pl.ds(0, n // 2), pl.ds(n // 2, n // 2)
                            pairs = [
                                (refs[3].at[:, rows], o_ref.at[low, to]),
                                (refs[4].at[:, rows], o_ref.at[high, to]),
                            ]
                        for k, (source, target) in enumerate(pairs):
                            copy = pltpu.make_async_copy(source, target, sems.at[m + k])
                            getattr(copy, act)()

    return pl.pallas_call(
        kernel,
        out_shape=jax.ShapeDtypeStruct((n, shares.rows, wide), parts[0].dtype),
        in_specs=[SM] + [ANY] * len(parts),
        out_specs=V,
        scratch_shapes=[pltpu.SemaphoreType.DMA((5,))],
        compiler_params=ROOM,
        cost_estimate=FREE,
    )(me, *parts)


def small_sum(value, axes):
    for axis in axes:
        size = lax.axis_size(axis)
        if size & (size - 1):
            value = lax.psum(value, axis)
            continue
        bit = 1
        while bit < size:
            value = value + lax.ppermute(value, axis, [(i, i ^ bit) for i in range(size)])
            bit *= 2
    return value


def go_up(value, first, last):
    return lax.ppermute(value, "col", [(i, i + 1) for i in range(first, last + 1)])


def go_down(value, first, last):
    return lax.ppermute(value, "col", [(i, i - 1) for i in range(first, last + 1)])


def row_join(parts, axis):
    row = lax.axis_index("row")
    if len(parts) == 2:
        low = row == 0
        parts = [jnp.where(low, parts[0], parts[1]), jnp.where(low, parts[1], parts[0])]
    else:
        parts = ordered(parts, row, 1)
    return jnp.concatenate(parts, axis)


def swap_all(value):
    return [swap_with(value, 1), swap_with(value, 2), swap_with(value, 3)]


class Heads:
    def __init__(self, n_col, width, heads, blocks):
        self.size = n_col * width // heads
        self.firsts = [width * c // self.size for c in range(n_col)]
        lasts = [-(-width * (c + 1) // self.size) for c in range(n_col)]
        self.slots = max(b - a for a, b in zip(self.firsts, lasts))
        self.window = self.slots * self.size
        self.before = [width * c - f * self.size for c, f in enumerate(self.firsts)]
        self.after = [self.window - width - b for b in self.before]
        self.edge = max(self.before + self.after)
        full = (1 << blocks) - 1
        shares = {0: 0, 1: 2, 2: 9, 3: 13, 4: 15}

        def left_share(column):
            part = column % self.size
            return shares[round(4 * part / self.size)] if blocks == 4 else 0

        self.first_mask = [full & ~left_share(b) for b in self.before]
        self.last_mask = []
        for c, f in enumerate(self.firsts):
            end = width * (c + 1)
            begin = (f + self.slots - 1) * self.size
            if begin >= end:
                self.last_mask.append(0)
            elif begin + self.size <= end:
                self.last_mask.append(full)
            else:
                self.last_mask.append(left_share(end - begin))


def edges(value, axis, heads):
    n = lax.axis_size("col")
    edge, width = heads.edge, value.shape[axis]
    left = go_up(lax.slice_in_dim(value, width - edge, width, axis=axis), 0, n - 2)
    right = go_down(lax.slice_in_dim(value, 0, edge, axis=axis), 1, n - 1)
    return left, right


def widen(value, left, right, axis, heads, col):
    wide = jnp.concatenate([left, value, right], axis)
    before = jnp.array(heads.before, jnp.int32)[col]
    return lax.dynamic_slice_in_dim(wide, heads.edge - before, heads.window, axis)


def narrow_cuts(value, axis, heads, col, width):
    edge = heads.edge
    before = jnp.array(heads.before, jnp.int32)[col]
    shape = list(value.shape)
    shape[axis] = width + 2 * edge
    wide = lax.dynamic_update_slice_in_dim(
        jnp.zeros(shape, value.dtype), value, edge - before, axis
    )
    to_left = lax.slice_in_dim(wide, 0, edge, axis=axis)
    to_right = lax.slice_in_dim(wide, edge + width, width + 2 * edge, axis=axis)
    return wide, to_left, to_right


def narrow(wide, front, tail, axis, heads, width):
    edge = heads.edge
    pads = [(0, 0)] * wide.ndim
    pads[axis] = (0, width - edge)
    own = lax.slice_in_dim(wide, edge, edge + width, axis=axis).astype(F32)
    own = own + jnp.pad(front, pads).astype(F32)
    pads[axis] = (width - edge, 0)
    return own + jnp.pad(tail, pads).astype(F32)


def moments(values):
    mean = jnp.mean(values, axis=0, keepdims=True)
    centred = values - mean
    variance = jnp.mean(centred * centred, axis=0, keepdims=True)
    return mean, lax.rsqrt(variance + EPSILON)


def body(
    tokens,
    cotangent,
    w_qkv,
    q_bias,
    v_bias,
    w_out,
    out_bias,
    w_up,
    up_bias,
    w_down,
    down_bias,
    ln1_gain,
    ln1_bias,
    ln2_gain,
    ln2_bias,
    key_start,
):
    n_row, n_col = lax.axis_size("row"), lax.axis_size("col")
    row, col = lax.axis_index("row"), lax.axis_index("col")
    seqs, rows, width = tokens.shape
    length = seqs * rows
    depth = width * n_col
    part = length // n_col
    in_rows = w_up.shape[0]
    ff = w_up.shape[1]
    ff_rows = w_down.shape[0]
    ff_part = ff_rows // n_col
    heads = Heads(n_col, width, key_start.shape[0], rows * n_row // BLK)
    size, window = heads.size, heads.window
    firsts = jnp.array(heads.firsts, jnp.int32) * size
    begin = firsts[col]

    shares = Shares(width, 16)
    dp = lax.axis_index("dp")
    row_at = row[None].astype(jnp.int32)
    col_at = col[None].astype(jnp.int32)
    other_rows = [((row + i) % n_row)[None].astype(jnp.int32) for i in range(n_row)]


    x = tokens.reshape(length, width).T
    g = cotangent.reshape(length, width).T
    place_in = col * n_row + row
    half = n_col // 2

    def between_owners(value_of, steps, back):
        got = []
        for step in steps:
            pairs = []
            for r in range(n_row):
                for c in range(n_col):
                    to = r * n_col + (c - step) % n_col
                    here, there = r * n_col + c, (to % n_row) * n_col + to // n_row
                    pairs.append((there, here) if back else (here, there))
            got.append(lax.ppermute(value_of(step), ("row", "col"), pairs))
        return got

    x_all = lax.all_gather(x, "col", axis=0, tiled=True)
    wq = w_qkv.transpose(0, 2, 1)
    w3_own = widen(wq, *edges(wq, 1, heads), 1, heads, col)
    w3_parts = [w3_own] + [turn(w3_own, "row", -step) for step in range(1, n_row)]
    w3 = row_join(w3_parts, 2).reshape(3 * window, depth)
    params = jnp.stack([ln1_gain, ln1_bias, ln2_gain, ln2_bias, out_bias, q_bias, v_bias])
    params = [turn(params, "col", step) for step in range(n_col)]
    params = jnp.concatenate(ordered(params, col, -1), 1)
    gain1, shift1, gain2, shift2, bias_out, bias_q, bias_v = [p[:, None] for p in params]
    bias3 = jnp.concatenate(
        [
            lax.dynamic_slice_in_dim(bias_q, begin, window, 0),
            jnp.zeros((window, 1), F32),
            lax.dynamic_slice_in_dim(bias_v, begin, window, 0),
        ]
    )
    columns = jnp.concatenate([gain1, shift1, bias_out, jnp.zeros((depth, 1), F32)], 1)
    meta = jnp.stack(
        [
            jnp.array(heads.firsts, jnp.int32)[col],
            row,
            jnp.array(heads.first_mask, jnp.int32)[col],
            jnp.array(heads.last_mask, jnp.int32)[col],
        ]
    )
    up_parts = [w_up] + [turn(w_up, "row", -step) for step in range(1, n_row)]
    up_turned = row_join(up_parts, 0).T
    out_own = shares.take(w_out.T, dp, 0)
    down_own = shares.take(w_down.T, dp, 0)
    x_all, g, out_own, down_own, w3, meta, columns, bias3 = gate(
        [x_all, g, out_own, down_own, w3, meta, columns, bias3], [up_turned]
    )

    g_all = lax.all_gather(g, "col", axis=0, tiled=True)
    moved_out = [out_own] + [turn(out_own, "col", -step) for step in range(1, n_col)]
    x_float = x_all.astype(F32)
    mean1, rstd1 = moments(x_float)
    n1 = ((x_float - mean1) * rstd1 * gain1 + shift1).astype(BF16)
    triple = product(w3, n1, bias3).reshape(3, window, length)
    triple, *rest = gate([triple] + moved_out[1:], [])
    moved_out = moved_out[:1] + rest

    pieces = [triple] + [turn(triple, "row", -step) for step in range(1, n_row)]
    moved_out = jnp.stack(ordered(moved_out, col, 1))
    moved_out, *rest = gate([moved_out] + pieces[1:], [])
    pieces = pieces[:1] + rest

    near_out = [swap_with(moved_out, 1), swap_with(moved_out, 2)]
    *cuts, mixed, norms = attn_fwd(meta, key_start, pieces, heads.slots, size)
    far_cuts = [near_out[0][:half], near_out[1][half:]]
    *cuts, near_x, near_y, far_x, far_y, g_all, down_own = gate(
        list(cuts) + near_out + far_cuts + [g_all, down_own], []
    )

    def move_down(step):
        return block(down_own, (col - step) % n_col, ff_part, 1)

    far_out = [swap_with(far_x, 2), swap_with(far_y, 1)]
    moved_down = between_owners(move_down, range(half), False)
    mixed_own = row_sum(cuts).astype(BF16)
    mixed_own, *rest = gate([mixed_own] + moved_down + far_out, [])
    moved_down, far_out = rest[:half], rest[half:]

    dp_at = dp[None].astype(jnp.int32)
    got = [
        turn(block(mixed_own, (col + step) % n_col, part, 1), "col", step) for step in range(n_col)
    ]
    out_weights = assemble([moved_out, near_x, near_y] + far_out, shares, dp_at)
    out_weights = [out_weights] + [turn(out_weights, "row", -step) for step in range(1, n_row)]
    down_own, *rest = gate([down_own] + got[1:] + out_weights[1:], [])
    got = got[:1] + rest[: n_col - 1]
    out_weights = out_weights[:1] + rest[n_col - 1 :]
    out_weights = [w.reshape(depth, in_rows) for w in out_weights]

    moved_down = moved_down + between_owners(move_down, range(half, n_col), False)
    got = ordered(got, col, -1)
    lapped = [heads.firsts[j] * size for j in range(n_col)]
    attention = sum(
        jnp.pad(piece, ((at, depth - at - window), (0, 0))) for piece, at in zip(got, lapped)
    )
    branch = split_product(out_weights, attention, row_at, columns, 2, F32)
    resid = block(x_all, col, part, 1).astype(F32) + branch
    mean2, rstd2 = moments(resid)
    hat2 = (resid - mean2) * rstd2
    n2_own = (hat2 * gain2 + shift2).astype(BF16)
    moved_down = jnp.stack(ordered(moved_down, place_in, 1))
    n2_own, g, moved_down = gate([n2_own, g, moved_down], [hat2])

    n2_all = lax.all_gather(n2_own, "col", axis=1, tiled=True)
    down_weights = assemble([moved_down] + swap_all(moved_down), shares, dp_at)
    down_weights = [turn(down_weights, "row", -step) for step in range(n_row)]
    down_weights = [w.reshape(depth, ff_part) for w in down_weights]
    down_turned = turned(down_weights)
    g_sums = jnp.sum(g.astype(F32), axis=1)
    n2_all, down_turned = gate([n2_all, down_turned], [g_sums])

    hidden_all, du_all, part2, du_sums = hidden_layer(
        up_turned, down_turned, n_row, up_bias[:, None], n2_all, g_all, row_at
    )
    part2, hidden_all, du_all = gate([part2, hidden_all, du_all], [])

    def relay_cut(value, far, cut, bit):
        return (cut.take(value, dp ^ (3 - bit), 1).astype(F32) + far.astype(F32)).astype(BF16)

    def share_sum(value, cut, near, relayed):
        own = cut.take(value, dp, 1).astype(F32)
        return (own + near.astype(F32) + relayed.astype(F32)).astype(BF16)

    def up_product(r):
        return token_product(n2_all, du_all, r, n_row, True)

    def down_product(r):
        return token_product(g_all, hidden_all, r, n_row, False).reshape(n_col, width, ff_part)

    dn2 = lax.psum_scatter(part2, "col", scatter_dimension=1, tiled=True)
    up_grad = [up_product(r) for r in other_rows[1:]]
    n2_all, hidden_all, *up_grad = gate([n2_all, hidden_all] + up_grad, [])

    up_grad = [turn(p, "row", i + 1) for i, p in enumerate(up_grad)]
    up_grad = [up_product(other_rows[0])] + up_grad
    down_grad = [down_product(r) for r in other_rows[1:]]
    hidden_all, *rest = gate([hidden_all] + up_grad + down_grad, [])
    up_grad, down_grad = rest[:n_row], rest[n_row:]
    up_rows = width if in_rows % width == 0 else in_rows
    up_shares, fine = Shares(up_rows, 8), Shares(width, 8)
    up_grad = sum(p.astype(F32) for p in up_grad).astype(BF16)
    up_grad = up_grad.reshape(in_rows // up_rows, up_rows, ff)
    up_far = up_shares.take(up_grad, dp ^ 3, 1)
    up_far, hidden_all, *down_grad = gate([up_far, hidden_all] + down_grad, [])

    up_far = swap_with(up_far, 1)
    down_grad = [turn(p, "row", i + 1) for i, p in enumerate(down_grad)]
    down_grad = [down_product(other_rows[0])] + down_grad
    hidden_all, *down_grad = gate([hidden_all] + down_grad, [])
    down_grad = sum(p.astype(F32) for p in down_grad).astype(BF16)
    down_far = fine.take(down_grad, dp ^ 3, 1)
    down_far, hidden_all = gate([down_far, hidden_all], [])

    down_far = swap_with(down_far, 2)
    up_near = up_shares.take(up_grad, dp ^ 1, 1)
    down_near = fine.take(down_grad, dp ^ 2, 1)
    du_row = du_sums[:, 0]
    shrunk = split_product(down_weights, hidden_all, row_at, columns, 3, BF16)
    own_sum = block(shrunk, col, part, 1).astype(F32) + resid
    shrunk = lax.dynamic_update_slice_in_dim(shrunk, own_sum.astype(BF16), col * part, 1)
    dn2, shrunk, up_far, down_far, up_near, down_near, du_row = gate(
        [dn2, shrunk, up_far, down_far, up_near, down_near, du_row], []
    )

    dn2 = dn2.astype(F32)
    up2 = dn2 * gain2
    pull2 = jnp.mean(up2, axis=0, keepdims=True)
    lean2 = jnp.mean(up2 * hat2, axis=0, keepdims=True)
    dr = block(g_all, col, part, 1).astype(F32) + rstd2 * (up2 - pull2 - hat2 * lean2)
    db = dr.astype(BF16)
    da = split_product_tn(out_weights, db, row_at)
    sums2 = jnp.stack(
        [
            jnp.sum(db.astype(F32), axis=1),
            jnp.sum(dn2 * hat2, axis=1),
            jnp.sum(dn2, axis=1),
        ]
    )
    early = jnp.concatenate([sums2.reshape(-1), du_row, g_sums])
    da_cuts = [
        lax.dynamic_slice_in_dim(da, firsts[(col + step) % n_col], window, 0)
        for step in range(n_col)
    ]
    up_near = swap_with(up_near, 1)
    down_near = swap_with(down_near, 2)
    up_relay = relay_cut(up_grad, up_far, up_shares, 1)
    down_relay = relay_cut(down_grad, down_far, fine, 2)
    db, shrunk, up_near, down_near, up_relay, down_relay, *da_cuts = gate(
        [db, shrunk, up_near, down_near, up_relay, down_relay] + da_cuts, [early]
    )

    got = [turn(cut, "col", step) for step, cut in enumerate(da_cuts)]
    up_relay = swap_with(up_relay, 2)
    down_relay = swap_with(down_relay, 1)
    out_grad = [token_product(db, attention, r, n_row, False) for r in other_rows[::-1]][::-1]
    out_grad = [o.reshape(n_col, width, in_rows) for o in out_grad]
    rest = gate(got[1:] + out_grad + [up_relay, down_relay, shrunk], [])
    got, rest = got[:1] + rest[: n_col - 1], rest[n_col - 1 :]
    out_grad, (up_relay, down_relay, shrunk) = rest[:n_row], rest[n_row:]

    outputs = lax.psum_scatter(shrunk, "col", scatter_dimension=0, tiled=True)
    da_own = jnp.concatenate(ordered(got, col, -1), 1)
    da_pieces = [da_own] + [turn(da_own, "row", -step) for step in range(1, n_row)]
    out_grad = row_sum(out_grad).astype(BF16)
    up_share = share_sum(up_grad, up_shares, up_near, up_relay)
    down_share = share_sum(down_grad, fine, down_near, down_relay)
    out_sent = jnp.stack([fine.take(out_grad, dp ^ 1, 1), fine.take(out_grad, dp ^ 3, 1)])
    *rest, out_sent, up_share, down_share = gate(
        da_pieces[1:] + [out_sent, up_share, down_share], []
    )
    da_pieces = [da_own] + rest

    out_first = swap_with(out_sent, 1)
    up_y = swap_with(up_share, 2)

    def move_home(step):
        return pick(down_share, (place_in + step) % n_col)

    down_home = between_owners(move_home, range(n_col - 1), True)
    dqkv = attn_bwd(meta, key_start, pieces, da_pieces, mixed, norms, heads.slots, size)
    *rest, out_first, up_y, up_share, down_share = gate(
        list(dqkv) + down_home + [out_first, up_y, up_share, down_share], []
    )
    dqkv, down_home = rest[:n_row], rest[n_row:]
    out_near, out_far = out_first[0], out_first[1]
    out_relay = relay_cut(out_grad, out_far, fine, 1)

    out_relay = swap_with(out_relay, 2)
    up_x = swap_with(up_share, 1)
    down_home = down_home + between_owners(move_home, range(n_col - 1, n_col), True)
    dqkv = row_sum(dqkv).astype(BF16).reshape(3 * window, length)
    homes = jnp.stack(ordered(down_home, col, -1))
    out_share = share_sum(out_grad, fine, out_near, out_relay)
    dqkv, homes, outputs, up_x, out_share = gate([dqkv, homes, outputs, up_x, out_share], [])

    homes_near = [swap_with(homes, 1), swap_with(homes, 2)]
    qkv_parts = [token_product(dqkv, n1, r, n_row, False) for r in other_rows[::-1]][::-1]
    qkv_parts = [q.reshape(3, window, in_rows) for q in qkv_parts]
    qkv_grad = row_sum(qkv_parts).astype(BF16)
    wide, to_left, to_right = narrow_cuts(qkv_grad, 1, heads, col, width)
    dqkv, wide, to_left, to_right, out_share, up_y, *homes_near = gate(
        [dqkv, wide, to_left, to_right, out_share, up_y] + homes_near, []
    )

    out_home = lax.psum_scatter(out_share, "col", scatter_dimension=0, tiled=True)
    tail, front = go_down(to_left, 1, n_col - 1), go_up(to_right, 0, n_col - 2)
    homes_far = swap_with(homes_near[1], 1)
    up_far = swap_with(up_x, 2)
    dn1, norm1 = norm_product_tn(w3, dqkv, n1, columns, rstd1, dr, col_at, n_col)
    qkv_grad = narrow(wide, front, tail, 1, heads, width).astype(BF16)
    qkv_sent = [fine.take(qkv_grad, dp ^ m, 1) for m in (1, 2, 3)]
    dn1, dqkv, homes_far, up_far, out_home, *qkv_sent = gate(
        [dn1, dqkv, homes_far, up_far, out_home] + qkv_sent, [norm1]
    )

    dx = lax.psum_scatter(dn1, "col", scatter_dimension=0, tiled=True)
    qkv_got = [swap_with(v, m) for v, m in zip(qkv_sent, (1, 2, 3))]
    out_all = [swap_with(out_home, 1), swap_with(out_home, 2)]
    homes, homes_far, norm1, outputs, dqkv = gate(
        [homes, homes_far, norm1, outputs, dqkv], qkv_sent
    )
    homes = fine.join([homes] + homes_near + [homes_far], dp, 1).astype(F32)
    down_grad = jnp.concatenate([homes[j] for j in range(n_col)], 1)
    outputs = (outputs.astype(F32) + down_bias[:, None]).astype(BF16)
    dq_dv = jnp.sum(dqkv.astype(F32), axis=1).reshape(3, window)
    sums = lax.dynamic_update_slice_in_dim(jnp.zeros((2, depth), F32), dq_dv[::2], begin, 1)
    small = jnp.concatenate([sums.reshape(-1), norm1.T.reshape(-1), early])[None]
    small = small_sum(small, ("row",))[0]
    sums, local = small[: 7 * depth].reshape(7, depth), small[7 * depth :]
    sums = small_sum(sums, ("col",))
    sums = lax.dynamic_slice_in_dim(sums, col * width, width, 1)
    small = jnp.concatenate([sums.reshape(-1), local])[None]
    qkv_share = fine.take(qkv_grad, dp, 1).astype(F32)
    qkv_share = (qkv_share + sum(q.astype(F32) for q in qkv_got)).astype(BF16)
    small, up_far, qkv_share, *out_all = gate(
        [small, up_far, qkv_share] + out_all, [down_grad, outputs]
    )

    qkv_all = swap_all(qkv_share)
    out_all.append(swap_with(out_all[0], 2))
    small = small_sum(small, ("dp",))[0]
    sums, local = small[: 7 * width].reshape(7, width), small[7 * width :]
    up_grad = up_shares.join([up_share, up_x, up_y, up_far], dp, 1).astype(F32)
    up_grad = up_grad.reshape(in_rows, ff)
    hat1 = (x.astype(F32) - mean1) * rstd1
    dx = dx.reshape(width + 16, length)
    lines = dx[width : width + 4].astype(F32)
    lines = (lines[0::2] + lines[1::2]) / depth
    input_grad = dx[:width].astype(F32) - rstd1 * (lines[0:1] + hat1 * lines[1:2])
    input_grad = input_grad.astype(BF16)
    *out_all, a, b, c = gate(out_all + qkv_all, [sums, local, up_grad, input_grad])

    out_grad = fine.join([out_home] + out_all, dp, 1).astype(F32)[0]
    qkv_grad = fine.join([qkv_share, a, b, c], dp, 1).astype(F32)
    return (
        outputs.T.reshape(tokens.shape),
        input_grad.T.reshape(tokens.shape),
        qkv_grad.transpose(0, 2, 1),
        sums[0],
        sums[1],
        out_grad.T,
        sums[4],
        up_grad,
        local[:ff],
        down_grad.T,
        local[ff:],
        sums[2],
        sums[3],
        sums[5],
        sums[6],
    )


def solution(mesh):
    inputs = (
        P("dp", "row", "col"),
        P("dp", "row", "col"),
        P(None, "row", "col"),
        P("col"),
        P("col"),
        P("row", "col"),
        P("col"),
        P("row", "col"),
        P("col"),
        P("row", "col"),
        P("col"),
        P("col"),
        P("col"),
        P("col"),
        P("col"),
        P(),
    )
    return jax.shard_map(
        body, mesh=mesh, in_specs=inputs, out_specs=inputs[:15], check_vma=False
    )
```

```python
import functools

import jax
import jax.numpy as jnp
from jax import lax
from jax.experimental import pallas as pl
from jax.experimental.pallas import tpu as pltpu
from jax.sharding import PartitionSpec as P

BLK = 512
EPSILON = 1e-05
LOG2E = 1.4426950408889634
BF16 = jnp.bfloat16
F32 = jnp.float32

FREE = pl.CostEstimate(flops=0, bytes_accessed=0, transcendentals=0)
ROOM = pltpu.CompilerParams(vmem_limit_bytes=56 * 2**20)

NT=(((0,),(0,)),((),()))
TN=(((1,),(1,)),((),()))

def plan_tiles(meta, ks, own, load, n_slots, n_blocks, n_row, n_heads):
    for i in range(n_row): load[i]=0
    def level(lv,_):
        cost=n_blocks-lv
        def tile(t,_):
            slot=t//n_blocks; qb=t%n_blocks
            head=meta[0]+slot
            here=head<n_heads
            hd=jnp.minimum(head,n_heads-1)
            n=qb+1-ks[hd,qb]
            mask=jnp.where(slot==0,meta[2],jnp.where(slot==n_slots-1,meta[3],(1<<n_blocks)-1))
            here=jnp.logical_and(here,((mask>>qb)&1)==1)
            @pl.when(cost==n_blocks)
            def _(): own[t]=-1
            @pl.when(jnp.logical_and(here,n==cost))
            def _():
                best=load[0]; who=jnp.int32(0)
                for i in range(1,n_row):
                    less=load[i]<best
                    best=jnp.where(less,load[i],best); who=jnp.where(less,i,who)
                own[t]=who
                load[who]=best+cost
            return 0
        lax.fori_loop(0,n_slots*n_blocks,tile,0)
        return 0
    lax.fori_loop(0,n_blocks,level,0)

def fetch(pieces, whole, sems, row, n_row, width):
    copies=[]
    for i,p in enumerate(pieces):
        at=lax.rem(row+i,n_row)*width
        c=pltpu.make_async_copy(p, whole.at[...,pl.ds(pl.multiple_of(at,width),width)], sems.at[i])
        c.start(); copies.append(c)
    return copies

def fwd_kernel(n_row,n_slots,hd,n_heads,meta,ks,*refs):
    pieces=refs[:n_row]; cuts=refs[n_row:2*n_row]; o_ref,lse_ref,whole,own,load,sems=refs[2*n_row:]
    S=whole.shape[2]; nb=S//BLK; width=S//n_row
    row=meta[1]
    copies=fetch(pieces,whole,sems,row,n_row,width)
    plan_tiles(meta,ks,own,load,n_slots,nb,n_row,n_heads)
    o_ref[...]=jnp.zeros_like(o_ref)
    for c in copies: c.wait()
    c2=hd**-0.5*LOG2E
    diag=lax.broadcasted_iota(jnp.int32,(BLK,BLK),0)<=lax.broadcasted_iota(jnp.int32,(BLK,BLK),1)
    def tile(t,_):
        @pl.when(own[t]==row)
        def _():
            slot=t//nb; qb=t%nb
            first=ks[meta[0]+slot,qb]
            hs=pl.ds(pl.multiple_of(slot*hd,hd),hd)
            qs=pl.ds(pl.multiple_of(qb*BLK,BLK),BLK)
            q=whole[0,hs,qs]
            def scores(kb_ds):
                return lax.dot_general(whole[1,hs,kb_ds],q,NT,preferred_element_type=jnp.float32)
            s=jnp.where(diag,scores(qs),-1e30)
            m=jnp.max(s,axis=0,keepdims=True)
            p=jnp.exp2((s-m)*c2)
            l=jnp.sum(p,axis=0,keepdims=True)
            acc=jnp.dot(whole[2,hs,qs],p.astype(jnp.bfloat16),preferred_element_type=jnp.float32)
            def step(kb,carry):
                m,l,acc=carry
                kd=pl.ds(pl.multiple_of(kb*BLK,BLK),BLK)
                s=scores(kd)
                mn=jnp.maximum(m,jnp.max(s,axis=0,keepdims=True))
                a=jnp.exp2((m-mn)*c2)
                p=jnp.exp2((s-mn)*c2)
                l=l*a+jnp.sum(p,axis=0,keepdims=True)
                acc=acc*a+jnp.dot(whole[2,hs,kd],p.astype(jnp.bfloat16),preferred_element_type=jnp.float32)
                return mn,l,acc
            m,l,acc=lax.fori_loop(first,qb,step,(m,l,acc))
            o_ref[hs,qs]=(acc/l).astype(jnp.bfloat16)
            lse_ref[pl.ds(slot,1),qs]=m*c2+jnp.log2(l)
        return 0
    lax.fori_loop(0,n_slots*nb,tile,0)
    for i,cut in enumerate(cuts):
        cut[...]=o_ref[:,pl.ds(pl.multiple_of(lax.rem(row+i,n_row)*width,width),width)]

def bwd_kernel(n_row,n_slots,hd,n_heads,meta,ks,*refs):
    pieces=refs[:n_row]; das=refs[n_row:2*n_row]
    o_ref,lse_ref=refs[2*n_row:2*n_row+2]; cuts=refs[2*n_row+2:3*n_row+2]
    d_ref,whole,da,acc,own,load,sems,sems2=refs[3*n_row+2:]
    S=whole.shape[2]; nb=S//BLK; width=S//n_row
    row=meta[1]
    copies=fetch(pieces,whole,sems,row,n_row,width)+fetch(das,da,sems2,row,n_row,width)
    plan_tiles(meta,ks,own,load,n_slots,nb,n_row,n_heads)
    d_ref[...]=jnp.zeros_like(d_ref)
    acc[...]=jnp.zeros_like(acc)
    for c in copies: c.wait()
    scale=hd**-0.5; c2=scale*LOG2E
    diag=lax.broadcasted_iota(jnp.int32,(BLK,BLK),0)<=lax.broadcasted_iota(jnp.int32,(BLK,BLK),1)
    def tile(t,_):
        @pl.when(own[t]==row)
        def _():
            slot=t//nb; qb=t%nb
            first=ks[meta[0]+slot,qb]
            hs=pl.ds(pl.multiple_of(slot*hd,hd),hd)
            qs=pl.ds(pl.multiple_of(qb*BLK,BLK),BLK)
            q=whole[0,hs,qs]
            up=da[hs,qs]
            lse=lse_ref[pl.ds(slot,1),qs]
            delta=jnp.sum(up.astype(jnp.float32)*o_ref[hs,qs].astype(jnp.float32),axis=0,keepdims=True)
            def block(kd,masked):
                k=whole[1,hs,kd]
                s=lax.dot_general(k,q,NT,preferred_element_type=jnp.float32)
                p=jnp.exp2(s*c2-lse)
                if masked: p=jnp.where(diag,p,0.0)
                dp=lax.dot_general(whole[2,hs,kd],up,NT,preferred_element_type=jnp.float32)
                ds=(p*(dp-delta)).astype(jnp.bfloat16)
                acc[1,hs,kd]+=lax.dot_general(up,p.astype(jnp.bfloat16),TN,preferred_element_type=jnp.float32)
                acc[0,hs,kd]+=lax.dot_general(q,ds,TN,preferred_element_type=jnp.float32)
                return jnp.dot(k,ds,preferred_element_type=jnp.float32)
            dq=block(qs,True)
            dq=lax.fori_loop(first,qb,lambda kb,dq:dq+block(pl.ds(pl.multiple_of(kb*BLK,BLK),BLK),False),dq)
            d_ref[hs,qs]=(dq*scale).astype(jnp.bfloat16)
        return 0
    lax.fori_loop(0,n_slots*nb,tile,0)
    for i,cut in enumerate(cuts):
        at=pl.ds(pl.multiple_of(lax.rem(row+i,n_row)*width,width),width)
        cut[0]=d_ref[:,at]
        cut[1]=(acc[0,:,at]*scale).astype(jnp.bfloat16)
        cut[2]=acc[1,:,at].astype(jnp.bfloat16)

V=pl.BlockSpec(memory_space=pltpu.VMEM); SM=pl.BlockSpec(memory_space=pltpu.SMEM); ANY=pl.BlockSpec(memory_space=pl.ANY)
def attn_fwd(meta,ks,pieces,n_slots,hd):
    n_row=len(pieces); _,H,T=pieces[0].shape; S=T*n_row; nb=S//BLK
    return pl.pallas_call(functools.partial(fwd_kernel,n_row,n_slots,hd,ks.shape[0]),
      out_shape=[jax.ShapeDtypeStruct((H,T),jnp.bfloat16)]*n_row+[jax.ShapeDtypeStruct((H,S),jnp.bfloat16),jax.ShapeDtypeStruct((n_slots,S),jnp.float32)],
      in_specs=[SM,SM]+[ANY]*n_row,out_specs=[V]*(n_row+2),
      scratch_shapes=[pltpu.VMEM((3,H,S),jnp.bfloat16),pltpu.SMEM((n_slots*nb,),jnp.int32),pltpu.SMEM((n_row,),jnp.int32),pltpu.SemaphoreType.DMA((n_row,))],
      compiler_params=pltpu.CompilerParams(vmem_limit_bytes=48*2**20),
      cost_estimate=FREE,
    )(meta,ks,*pieces)
def attn_bwd(meta,ks,pieces,das,o,lse,n_slots,hd):
    n_row=len(pieces); _,H,T=pieces[0].shape; S=T*n_row; nb=S//BLK
    return pl.pallas_call(functools.partial(bwd_kernel,n_row,n_slots,hd,ks.shape[0]),
      out_shape=[jax.ShapeDtypeStruct((3,H,T),jnp.bfloat16)]*n_row,
      in_specs=[SM,SM]+[ANY]*(2*n_row)+[V,V],out_specs=[V]*n_row,
      scratch_shapes=[pltpu.VMEM((H,S),jnp.bfloat16),pltpu.VMEM((3,H,S),jnp.bfloat16),pltpu.VMEM((H,S),jnp.bfloat16),pltpu.VMEM((2,H,S),jnp.float32),pltpu.SMEM((n_slots*nb,),jnp.int32),pltpu.SMEM((n_row,),jnp.int32),pltpu.SemaphoreType.DMA((n_row,)),pltpu.SemaphoreType.DMA((n_row,))],
      compiler_params=pltpu.CompilerParams(vmem_limit_bytes=56*2**20),
      cost_estimate=FREE,
    )(meta,ks,*pieces,*das,o,lse)


def rows_of(total, most):
    for rows in range(min(total, most) // 16 * 16, 0, -16):
        if total % rows == 0:
            return rows
    return total


def by_rows(i, *refs):
    return (i, 0)


def whole_block(i, *refs):
    return (0, 0)


def product_kernel(a_ref, b_ref, bias_ref, o_ref):
    o_ref[...] = (
        jnp.dot(a_ref[...], b_ref[...], preferred_element_type=F32) + bias_ref[...]
    ).astype(o_ref.dtype)


def product(a, b, bias):
    rows = rows_of(a.shape[0], 448)
    return pl.pallas_call(
        product_kernel,
        out_shape=jax.ShapeDtypeStruct((a.shape[0], b.shape[1]), BF16),
        grid=(a.shape[0] // rows,),
        in_specs=[
            pl.BlockSpec((rows, a.shape[1]), by_rows),
            pl.BlockSpec(b.shape, whole_block),
            pl.BlockSpec((rows, 1), by_rows),
        ],
        out_specs=pl.BlockSpec((rows, b.shape[1]), by_rows),
        compiler_params=ROOM,
        cost_estimate=FREE,
    )(a, b, bias)


def split_product(parts, b, row, columns, which, dtype):
    n = len(parts)
    total, depth = parts[0].shape
    width = b.shape[1]
    rows = rows_of(total, 400)

    def kernel(row_ref, b_ref, bias_ref, *refs):
        out = bias_ref[:, which : which + 1] + jnp.zeros((rows, width), F32)
        for i in range(n):
            at = pl.multiple_of(lax.rem(row_ref[0] + i, n) * depth, 8)
            out = out + jnp.dot(refs[i][...], b_ref[pl.ds(at, depth), :], preferred_element_type=F32)
        refs[n][...] = out.astype(dtype)

    return pl.pallas_call(
        kernel,
        out_shape=jax.ShapeDtypeStruct((total, width), dtype),
        grid=(total // rows,),
        in_specs=[
            SM,
            pl.BlockSpec(b.shape, whole_block),
            pl.BlockSpec((rows, columns.shape[1]), by_rows),
        ]
        + [pl.BlockSpec((rows, depth), by_rows)] * n,
        out_specs=pl.BlockSpec((rows, width), by_rows),
        compiler_params=ROOM,
        cost_estimate=FREE,
    )(row, b, columns, *parts)


def mixed_norm(parts, b, row, columns, x):
    n = len(parts)
    total, depth = parts[0].shape
    width = b.shape[1]
    rows = rows_of(total, 400)
    steps = total // rows

    def kernel(row_ref, b_ref, c_ref, x_ref, *refs):
        o_ref, hat_ref, norm_ref, scale_ref = refs[n:]
        step = pl.program_id(0)
        at = pl.ds(pl.multiple_of(step * rows, 8), rows)
        out = c_ref[at, 2:3] + x_ref[...].astype(F32)
        for i in range(n):
            here = pl.multiple_of(lax.rem(row_ref[0] + i, n) * depth, 8)
            out = out + jnp.dot(
                refs[i][...], b_ref[pl.ds(here, depth), :], preferred_element_type=F32
            )
        o_ref[at, :] = out

        @pl.when(step == steps - 1)
        def end():
            mean = jnp.sum(o_ref[...], axis=0, keepdims=True) / total
            centred = o_ref[...] - mean
            scale = lax.rsqrt(jnp.sum(centred * centred, axis=0, keepdims=True) / total + EPSILON)
            hat = centred * scale
            hat_ref[...] = hat
            norm_ref[...] = (hat * c_ref[:, 3:4] + c_ref[:, 4:5]).astype(BF16)
            scale_ref[...] = scale

    return pl.pallas_call(
        kernel,
        out_shape=[
            jax.ShapeDtypeStruct((total, width), F32),
            jax.ShapeDtypeStruct((total, width), F32),
            jax.ShapeDtypeStruct((total, width), BF16),
            jax.ShapeDtypeStruct((1, width), F32),
        ],
        grid=(steps,),
        in_specs=[
            SM,
            pl.BlockSpec(b.shape, whole_block),
            pl.BlockSpec(columns.shape, whole_block),
            pl.BlockSpec((rows, width), by_rows),
        ]
        + [pl.BlockSpec((rows, depth), by_rows)] * n,
        out_specs=[
            pl.BlockSpec((total, width), whole_block),
            pl.BlockSpec((total, width), whole_block),
            pl.BlockSpec((total, width), whole_block),
            pl.BlockSpec((1, width), whole_block),
        ],
        compiler_params=ROOM,
        cost_estimate=FREE,
    )(row, b, columns, x, *parts)


def mixed_norm_back(parts, dn, hat, scale, g, row, columns):
    n = len(parts)
    depth = parts[0].shape[1]
    total, width = dn.shape
    rows = rows_of(total, 400)
    steps = total // rows

    def kernel(row_ref, dn_ref, hat_ref, scale_ref, g_ref, c_ref, *refs):
        o_ref, low_ref, a_ref, s_ref, acc = refs[n:]
        step = pl.program_id(0)

        @pl.when(step == 0)
        def start():
            grad = dn_ref[...].astype(F32)
            up = grad * c_ref[:, 3:4]
            hat = hat_ref[...]
            pull = jnp.sum(up, axis=0, keepdims=True) / total
            lean = jnp.sum(up * hat, axis=0, keepdims=True) / total
            out = g_ref[...].astype(F32) + scale_ref[...] * (up - pull - hat * lean)
            low = out.astype(BF16)
            o_ref[...] = out
            low_ref[...] = low
            s_ref[:, 0:1] = jnp.sum(low.astype(F32), axis=1, keepdims=True)
            s_ref[:, 1:2] = jnp.sum(grad * hat, axis=1, keepdims=True)
            s_ref[:, 2:3] = jnp.sum(grad, axis=1, keepdims=True)
            acc[...] = jnp.zeros_like(acc)

        cut = low_ref[pl.ds(pl.multiple_of(step * rows, 8), rows), :]
        for i in range(n):
            here = pl.ds(pl.multiple_of(lax.rem(row_ref[0] + i, n) * depth, 8), depth)
            acc[here, :] += lax.dot_general(refs[i][...], cut, NT, preferred_element_type=F32)

        @pl.when(step == steps - 1)
        def end():
            a_ref[...] = acc[...].astype(BF16)

    full = pl.BlockSpec((total, width), whole_block)
    return pl.pallas_call(
        kernel,
        out_shape=[
            jax.ShapeDtypeStruct((total, width), F32),
            jax.ShapeDtypeStruct((total, width), BF16),
            jax.ShapeDtypeStruct((n * depth, width), BF16),
            jax.ShapeDtypeStruct((total, 3), F32),
        ],
        grid=(steps,),
        in_specs=[
            SM,
            full,
            full,
            pl.BlockSpec((1, width), whole_block),
            full,
            pl.BlockSpec(columns.shape, whole_block),
        ]
        + [pl.BlockSpec((rows, depth), by_rows)] * n,
        out_specs=[
            full,
            full,
            pl.BlockSpec((n * depth, width), whole_block),
            pl.BlockSpec((total, 3), whole_block),
        ],
        scratch_shapes=[pltpu.VMEM((n * depth, width), F32)],
        compiler_params=ROOM,
        cost_estimate=FREE,
    )(row, dn, hat, scale, g, columns, *parts)


def norm_product_tn(a, b, normed, columns, scale, riding, col, n_col):
    rows = rows_of(a.shape[0], 448)
    steps = a.shape[0] // rows
    depth, tokens = a.shape[1], b.shape[1]
    cut, part = depth // n_col, tokens // n_col

    def kernel(col_ref, a_ref, b_ref, n_ref, g_ref, c_ref, r_ref, o_ref, f_ref, acc):
        @pl.when(pl.program_id(0) == 0)
        def start():
            acc[...] = lax.dot_general(a_ref[...], b_ref[...], NT, preferred_element_type=F32)

        @pl.when(pl.program_id(0) > 0)
        def more():
            acc[...] += lax.dot_general(a_ref[...], b_ref[...], NT, preferred_element_type=F32)

        @pl.when(pl.program_id(0) == steps - 1)
        def end():
            first = jnp.zeros((1, tokens), F32)
            second = jnp.zeros((1, tokens), F32)
            for j in range(n_col):
                at = pl.ds(j * cut, cut)
                p = acc[at, :]
                scaled = p * g_ref[at, 0:1]
                o_ref[j, 0:cut, :] = (scaled * c_ref[...]).astype(BF16)
                moved = p * (n_ref[at, :].astype(F32) - g_ref[at, 1:2])
                first += jnp.sum(scaled, axis=0, keepdims=True)
                second += jnp.sum(moved, axis=0, keepdims=True)
                f_ref[at, 0:1] = jnp.sum(moved, axis=1, keepdims=True) / g_ref[at, 0:1]
                f_ref[at, 1:2] = jnp.sum(p, axis=1, keepdims=True)
                for c in range(n_col):

                    @pl.when(col_ref[0] == c)
                    def ride():
                        here = slice(c * part, (c + 1) * part)
                        own = scaled[:, here] * c_ref[:, here] + r_ref[at, :]
                        o_ref[j, 0:cut, here] = own.astype(BF16)

            lines = []
            for line in (first, second):
                high = line.astype(BF16).astype(F32)
                lines += [high, line - high]
            lines = jnp.concatenate(lines + [jnp.zeros((12, tokens), F32)]).astype(BF16)
            for j in range(n_col):
                o_ref[j, cut : cut + 16, :] = lines

    return pl.pallas_call(
        kernel,
        out_shape=[
            jax.ShapeDtypeStruct((n_col, cut + 16, tokens), BF16),
            jax.ShapeDtypeStruct((depth, 2), F32),
        ],
        grid=(steps,),
        in_specs=[
            SM,
            pl.BlockSpec((rows, depth), by_rows),
            pl.BlockSpec((rows, tokens), by_rows),
            pl.BlockSpec((depth, tokens), whole_block),
            pl.BlockSpec(columns.shape, whole_block),
            pl.BlockSpec((1, tokens), whole_block),
            pl.BlockSpec((depth, part), whole_block),
        ],
        out_specs=[
            pl.BlockSpec((n_col, cut + 16, tokens), lambda i: (0, 0, 0)),
            pl.BlockSpec((depth, 2), whole_block),
        ],
        scratch_shapes=[pltpu.VMEM((depth, tokens), F32)],
        compiler_params=ROOM,
        cost_estimate=FREE,
    )(col, a, b, normed, columns, scale, riding)


def token_product(a, b, index, parts, of_a):
    rows_a = a.shape[0] // (parts if of_a else 1)
    rows_b = b.shape[0] // (1 if of_a else parts)
    rows = rows_of(rows_a, 448)
    steps = rows_a // rows

    def kernel(index_ref, a_ref, b_ref, o_ref):
        o_ref[...] = lax.dot_general(
            a_ref[...], b_ref[...], TN, preferred_element_type=F32
        ).astype(BF16)

    if of_a:
        a_map, b_map = (lambda i, r: (r[0] * steps + i, 0)), whole_block
    else:
        a_map, b_map = by_rows, (lambda i, r: (r[0], 0))
    return pl.pallas_call(
        kernel,
        out_shape=jax.ShapeDtypeStruct((rows_a, rows_b), BF16),
        grid_spec=pltpu.PrefetchScalarGridSpec(
            num_scalar_prefetch=1,
            grid=(steps,),
            in_specs=[
                pl.BlockSpec((rows, a.shape[1]), a_map),
                pl.BlockSpec((rows_b, b.shape[1]), b_map),
            ],
            out_specs=pl.BlockSpec((rows, rows_b), by_rows),
        ),
        compiler_params=ROOM,
        cost_estimate=FREE,
    )(index, a, b)


def gelu_parts(u):
    inner = 0.7978845608 * (u + 0.044715 * u * u * u)
    t = jnp.tanh(inner)
    value = 0.5 * u * (1.0 + t)
    slope = 0.5 * (1.0 + t) + 0.5 * u * (1.0 - t * t) * 0.7978845608 * (1.0 + 0.134145 * u * u)
    return value, slope


def hidden_layer(up, down, n, bias, n2, g, row):
    ff, depth = up.shape
    tokens = n2.shape[1]
    rows = rows_of(ff // n, 400)
    cuts = ff // n // rows
    steps = ff // rows

    def kernel(row_ref, up_ref, down_ref, bias_ref, n_ref, g_ref, h_ref, d_ref, p_ref, s_ref, acc):
        step = pl.program_id(0)
        u = jnp.dot(up_ref[...], n_ref[...], preferred_element_type=F32) + bias_ref[...]
        value, slope = gelu_parts(u)
        h_ref[...] = value.astype(BF16)
        dh = jnp.dot(down_ref[...], g_ref[...], preferred_element_type=F32)
        du = (dh * slope).astype(BF16)
        d_ref[...] = du
        s_ref[...] = jnp.sum(du.astype(F32), axis=1, keepdims=True)

        @pl.when(step == 0)
        def start():
            acc[...] = lax.dot_general(up_ref[...], du, NT, preferred_element_type=F32)

        @pl.when(step > 0)
        def more():
            acc[...] += lax.dot_general(up_ref[...], du, NT, preferred_element_type=F32)

        @pl.when(step == steps - 1)
        def end():
            p_ref[...] = acc[...].astype(BF16)

    mine = lambda i, r: (lax.rem(r[0] * cuts + i, steps), 0)
    full = lambda i, r: (0, 0)
    return pl.pallas_call(
        kernel,
        out_shape=[
            jax.ShapeDtypeStruct((ff, tokens), BF16),
            jax.ShapeDtypeStruct((ff, tokens), BF16),
            jax.ShapeDtypeStruct((depth, tokens), BF16),
            jax.ShapeDtypeStruct((ff, 1), F32),
        ],
        grid_spec=pltpu.PrefetchScalarGridSpec(
            num_scalar_prefetch=1,
            grid=(steps,),
            in_specs=[
                pl.BlockSpec((rows, depth), mine),
                pl.BlockSpec((rows, depth), lambda i, r: (i, 0)),
                pl.BlockSpec((rows, 1), mine),
                pl.BlockSpec((depth, tokens), full),
                pl.BlockSpec((depth, tokens), full),
            ],
            out_specs=[
                pl.BlockSpec((rows, tokens), mine),
                pl.BlockSpec((rows, tokens), mine),
                pl.BlockSpec((depth, tokens), full),
                pl.BlockSpec((rows, 1), mine),
            ],
            scratch_shapes=[pltpu.VMEM((depth, tokens), F32)],
        ),
        compiler_params=ROOM,
        cost_estimate=FREE,
    )(row, up, down, bias, n2, g)


def turned(parts):
    n = len(parts)
    depth, wide = parts[0].shape

    def kernel(*refs):
        o_ref = refs[n]
        for i in range(n):
            for first in range(0, wide, 256):
                size = min(256, wide - first)
                at = lax.broadcasted_iota(jnp.int32, (size, size), 0)
                ones = (at == lax.broadcasted_iota(jnp.int32, (size, size), 1)).astype(BF16)
                cut = refs[i][:, first : first + size]
                out = lax.dot_general(ones, cut, TN, preferred_element_type=F32)
                o_ref[i * wide + first : i * wide + first + size, :] = out.astype(BF16)

    return pl.pallas_call(
        kernel,
        out_shape=jax.ShapeDtypeStruct((n * wide, depth), BF16),
        in_specs=[V] * n,
        out_specs=V,
        compiler_params=ROOM,
        cost_estimate=FREE,
    )(*parts)


def gate(values, others):
    def kernel(*refs):
        pass

    out = pl.pallas_call(
        kernel,
        out_shape=[jax.ShapeDtypeStruct(v.shape, v.dtype) for v in values],
        in_specs=[ANY] * (len(values) + len(others)),
        out_specs=[ANY] * len(values),
        input_output_aliases={i: i for i in range(len(values))},
        cost_estimate=FREE,
    )(*values, *others)
    return list(out)


def turn(value, axis, steps):
    size = lax.axis_size(axis)
    if steps % size == 0:
        return value
    return lax.ppermute(value, axis, [(i, (i + steps) % size) for i in range(size)])


def block(value, index, size, axis):
    return lax.dynamic_slice_in_dim(value, index * size, size, axis)


def row_sum(parts):
    total = parts[0].astype(F32)
    for step in range(1, len(parts)):
        total = total + turn(parts[step], "row", step).astype(F32)
    return total


def swap_with(value, bit):
    return lax.ppermute(value, "dp", [(i, i ^ bit) for i in range(4)])


def pick(value, index, axis=0):
    return lax.dynamic_index_in_dim(value, index, axis, keepdims=False)


def dot(a, b):
    return jnp.dot(a, b, preferred_element_type=F32)


def ordered(parts, base, sign):
    size = len(parts)
    stacked = jnp.stack(parts)
    return [pick(stacked, (sign * (j - base)) % size) for j in range(size)]


class Shares:
    def __init__(self, rows, tile):
        self.rows = rows
        self.size = -(-rows // (4 * tile)) * tile
        self.starts = [(rows - self.size) * s // (3 * tile) * tile for s in range(3)]
        self.starts.append(rows - self.size)
        ends = self.starts[1:] + [rows]
        self.lengths = [b - a for a, b in zip(self.starts, ends)]

    def take(self, value, share, axis):
        start = jnp.array(self.starts, jnp.int32)[share]
        return lax.dynamic_slice_in_dim(value, start, self.size, axis)

    def lay(self, parts, axis):
        return jnp.concatenate(
            [lax.slice_in_dim(p, 0, n, axis=axis) for p, n in zip(parts, self.lengths)], axis
        )

    def join(self, parts, me, axis):
        odd, high = me % 2 == 1, me // 2 == 1
        picked = [
            jnp.where(
                high,
                jnp.where(odd, parts[3 ^ s], parts[2 ^ s]),
                jnp.where(odd, parts[1 ^ s], parts[s]),
            )
            for s in range(4)
        ]
        return self.lay(picked, axis)


def assemble(parts, shares, me):
    n, wide = parts[0].shape[0], parts[0].shape[2]

    def kernel(me_ref, *refs):
        o_ref, sems = refs[-2:]
        for act in ("start", "wait"):
            for m in range(4):
                for s in range(4):

                    @pl.when(me_ref[0] ^ m == s)
                    def move():
                        rows = pl.ds(0, shares.lengths[s])
                        to = pl.ds(shares.starts[s], shares.lengths[s])
                        pairs = [(refs[m].at[:, rows], o_ref.at[:, to])]
                        if m == 3 and len(parts) == 5:
                            low, high = pl.ds(0, n // 2), pl.ds(n // 2, n // 2)
                            pairs = [
                                (refs[3].at[:, rows], o_ref.at[low, to]),
                                (refs[4].at[:, rows], o_ref.at[high, to]),
                            ]
                        for k, (source, target) in enumerate(pairs):
                            copy = pltpu.make_async_copy(source, target, sems.at[m + k])
                            getattr(copy, act)()

    return pl.pallas_call(
        kernel,
        out_shape=jax.ShapeDtypeStruct((n, shares.rows, wide), parts[0].dtype),
        in_specs=[SM] + [ANY] * len(parts),
        out_specs=V,
        scratch_shapes=[pltpu.SemaphoreType.DMA((5,))],
        compiler_params=ROOM,
        cost_estimate=FREE,
    )(me, *parts)


def small_sum(value, axes):
    for axis in axes:
        size = lax.axis_size(axis)
        if size & (size - 1):
            value = lax.psum(value, axis)
            continue
        bit = 1
        while bit < size:
            value = value + lax.ppermute(value, axis, [(i, i ^ bit) for i in range(size)])
            bit *= 2
    return value


def go_up(value, first, last):
    return lax.ppermute(value, "col", [(i, i + 1) for i in range(first, last + 1)])


def go_down(value, first, last):
    return lax.ppermute(value, "col", [(i, i - 1) for i in range(first, last + 1)])


def row_join(parts, axis):
    row = lax.axis_index("row")
    if len(parts) == 2:
        low = row == 0
        parts = [jnp.where(low, parts[0], parts[1]), jnp.where(low, parts[1], parts[0])]
    else:
        parts = ordered(parts, row, 1)
    return jnp.concatenate(parts, axis)


def swap_all(value):
    return [swap_with(value, 1), swap_with(value, 2), swap_with(value, 3)]


class Heads:
    def __init__(self, n_col, width, heads, blocks):
        self.size = n_col * width // heads
        self.firsts = [width * c // self.size for c in range(n_col)]
        lasts = [-(-width * (c + 1) // self.size) for c in range(n_col)]
        self.slots = max(b - a for a, b in zip(self.firsts, lasts))
        self.window = self.slots * self.size
        self.before = [width * c - f * self.size for c, f in enumerate(self.firsts)]
        self.after = [self.window - width - b for b in self.before]
        self.edge = max(self.before + self.after)
        full = (1 << blocks) - 1
        shares = {0: 0, 1: 2, 2: 9, 3: 13, 4: 15}

        def left_share(column):
            part = column % self.size
            return shares[round(4 * part / self.size)] if blocks == 4 else 0

        self.first_mask = [full & ~left_share(b) for b in self.before]
        self.last_mask = []
        for c, f in enumerate(self.firsts):
            end = width * (c + 1)
            begin = (f + self.slots - 1) * self.size
            if begin >= end:
                self.last_mask.append(0)
            elif begin + self.size <= end:
                self.last_mask.append(full)
            else:
                self.last_mask.append(left_share(end - begin))


def edges(value, axis, heads):
    n = lax.axis_size("col")
    edge, width = heads.edge, value.shape[axis]
    left = go_up(lax.slice_in_dim(value, width - edge, width, axis=axis), 0, n - 2)
    right = go_down(lax.slice_in_dim(value, 0, edge, axis=axis), 1, n - 1)
    return left, right


def widen(value, left, right, axis, heads, col):
    wide = jnp.concatenate([left, value, right], axis)
    before = jnp.array(heads.before, jnp.int32)[col]
    return lax.dynamic_slice_in_dim(wide, heads.edge - before, heads.window, axis)


def narrow_cuts(value, axis, heads, col, width):
    edge = heads.edge
    before = jnp.array(heads.before, jnp.int32)[col]
    shape = list(value.shape)
    shape[axis] = width + 2 * edge
    wide = lax.dynamic_update_slice_in_dim(
        jnp.zeros(shape, value.dtype), value, edge - before, axis
    )
    to_left = lax.slice_in_dim(wide, 0, edge, axis=axis)
    to_right = lax.slice_in_dim(wide, edge + width, width + 2 * edge, axis=axis)
    return wide, to_left, to_right


def narrow(wide, front, tail, axis, heads, width):
    edge = heads.edge
    pads = [(0, 0)] * wide.ndim
    pads[axis] = (0, width - edge)
    own = lax.slice_in_dim(wide, edge, edge + width, axis=axis).astype(F32)
    own = own + jnp.pad(front, pads).astype(F32)
    pads[axis] = (width - edge, 0)
    return own + jnp.pad(tail, pads).astype(F32)


def moments(values):
    mean = jnp.mean(values, axis=0, keepdims=True)
    centred = values - mean
    variance = jnp.mean(centred * centred, axis=0, keepdims=True)
    return mean, lax.rsqrt(variance + EPSILON)


def body(
    tokens,
    cotangent,
    w_qkv,
    q_bias,
    v_bias,
    w_out,
    out_bias,
    w_up,
    up_bias,
    w_down,
    down_bias,
    ln1_gain,
    ln1_bias,
    ln2_gain,
    ln2_bias,
    key_start,
):
    n_row, n_col = lax.axis_size("row"), lax.axis_size("col")
    row, col = lax.axis_index("row"), lax.axis_index("col")
    seqs, rows, width = tokens.shape
    length = seqs * rows
    depth = width * n_col
    part = length // n_col
    in_rows = w_up.shape[0]
    ff = w_up.shape[1]
    ff_rows = w_down.shape[0]
    ff_part = ff_rows // n_col
    heads = Heads(n_col, width, key_start.shape[0], rows * n_row // BLK)
    size, window = heads.size, heads.window
    firsts = jnp.array(heads.firsts, jnp.int32) * size
    begin = firsts[col]

    shares = Shares(width, 16)
    dp = lax.axis_index("dp")
    row_at = row[None].astype(jnp.int32)
    col_at = col[None].astype(jnp.int32)
    other_rows = [((row + i) % n_row)[None].astype(jnp.int32) for i in range(n_row)]


    x = tokens.reshape(length, width).T
    g = cotangent.reshape(length, width).T
    place_in = col * n_row + row
    half = n_col // 2

    def between_owners(value_of, steps, back):
        got = []
        for step in steps:
            pairs = []
            for r in range(n_row):
                for c in range(n_col):
                    to = r * n_col + (c - step) % n_col
                    here, there = r * n_col + c, (to % n_row) * n_col + to // n_row
                    pairs.append((there, here) if back else (here, there))
            got.append(lax.ppermute(value_of(step), ("row", "col"), pairs))
        return got

    x_all = lax.all_gather(x, "col", axis=0, tiled=True)
    wq = w_qkv.transpose(0, 2, 1)
    w3_own = widen(wq, *edges(wq, 1, heads), 1, heads, col)
    w3_parts = [w3_own] + [turn(w3_own, "row", -step) for step in range(1, n_row)]
    w3 = row_join(w3_parts, 2).reshape(3 * window, depth)
    params = jnp.stack([ln1_gain, ln1_bias, ln2_gain, ln2_bias, out_bias, q_bias, v_bias])
    params = [turn(params, "col", step) for step in range(n_col)]
    params = jnp.concatenate(ordered(params, col, -1), 1)
    gain1, shift1, gain2, shift2, bias_out, bias_q, bias_v = [p[:, None] for p in params]
    bias3 = jnp.concatenate(
        [
            lax.dynamic_slice_in_dim(bias_q, begin, window, 0),
            jnp.zeros((window, 1), F32),
            lax.dynamic_slice_in_dim(bias_v, begin, window, 0),
        ]
    )
    no_bias = jnp.zeros((depth, 1), F32)
    columns = jnp.concatenate([gain1, shift1, bias_out, gain2, shift2, no_bias], 1)
    meta = jnp.stack(
        [
            jnp.array(heads.firsts, jnp.int32)[col],
            row,
            jnp.array(heads.first_mask, jnp.int32)[col],
            jnp.array(heads.last_mask, jnp.int32)[col],
        ]
    )
    up_parts = [w_up] + [turn(w_up, "row", -step) for step in range(1, n_row)]
    up_turned = row_join(up_parts, 0).T
    out_own = shares.take(w_out.T, dp, 0)
    down_own = shares.take(w_down.T, dp, 0)
    x_all, g, out_own, down_own, w3, meta, columns, bias3 = gate(
        [x_all, g, out_own, down_own, w3, meta, columns, bias3], [up_turned]
    )

    g_all = lax.all_gather(g, "col", axis=0, tiled=True)
    moved_out = [out_own] + [turn(out_own, "col", -step) for step in range(1, n_col)]
    x_float = x_all.astype(F32)
    mean1, rstd1 = moments(x_float)
    n1 = ((x_float - mean1) * rstd1 * gain1 + shift1).astype(BF16)
    triple = product(w3, n1, bias3).reshape(3, window, length)
    triple, *rest = gate([triple] + moved_out[1:], [])
    moved_out = moved_out[:1] + rest

    pieces = [triple] + [turn(triple, "row", -step) for step in range(1, n_row)]
    moved_out = jnp.stack(ordered(moved_out, col, 1))
    moved_out, *rest = gate([moved_out] + pieces[1:], [])
    pieces = pieces[:1] + rest

    near_out = [swap_with(moved_out, 1), swap_with(moved_out, 2)]
    *cuts, mixed, norms = attn_fwd(meta, key_start, pieces, heads.slots, size)
    far_cuts = [near_out[0][:half], near_out[1][half:]]
    *cuts, near_x, near_y, far_x, far_y, down_own = gate(
        list(cuts) + near_out + far_cuts + [down_own], []
    )

    def move_down(step):
        return block(down_own, (col - step) % n_col, ff_part, 1)

    far_out = [swap_with(far_x, 2), swap_with(far_y, 1)]
    moved_down = between_owners(move_down, range(half), False)
    mixed_own = row_sum(cuts).astype(BF16)
    mixed_own, g_all, *rest = gate([mixed_own, g_all] + moved_down + far_out, [])
    moved_down, far_out = rest[:half], rest[half:]

    dp_at = dp[None].astype(jnp.int32)
    got = [
        turn(block(mixed_own, (col + step) % n_col, part, 1), "col", step) for step in range(n_col)
    ]
    out_weights = assemble([moved_out, near_x, near_y] + far_out, shares, dp_at)
    out_weights = [out_weights] + [turn(out_weights, "row", -step) for step in range(1, n_row)]
    x_part = block(x_all, col, part, 1)
    down_own, x_part, *rest = gate([down_own, x_part] + got[1:] + out_weights[1:], [])
    got = got[:1] + rest[: n_col - 1]
    out_weights = out_weights[:1] + rest[n_col - 1 :]
    out_weights = [w.reshape(depth, in_rows) for w in out_weights]

    moved_down = moved_down + between_owners(move_down, range(half, n_col), False)
    got = ordered(got, col, -1)
    lapped = [heads.firsts[j] * size for j in range(n_col)]
    attention = sum(
        jnp.pad(piece, ((at, depth - at - window), (0, 0))) for piece, at in zip(got, lapped)
    )
    resid, hat2, n2_own, rstd2 = mixed_norm(out_weights, attention, row_at, columns, x_part)
    moved_down = jnp.stack(ordered(moved_down, place_in, 1))
    n2_own, g, moved_down = gate([n2_own, g, moved_down], [])

    n2_all = lax.all_gather(n2_own, "col", axis=1, tiled=True)
    down_weights = assemble([moved_down] + swap_all(moved_down), shares, dp_at)
    down_weights = [turn(down_weights, "row", -step) for step in range(n_row)]
    down_weights = [w.reshape(depth, ff_part) for w in down_weights]
    down_turned = turned(down_weights)
    g_sums = jnp.sum(g.astype(F32), axis=1)
    n2_all, down_turned = gate([n2_all, down_turned], [g_sums])

    hidden_all, du_all, part2, du_sums = hidden_layer(
        up_turned, down_turned, n_row, up_bias[:, None], n2_all, g_all, row_at
    )
    part2, hidden_all, du_all = gate([part2, hidden_all, du_all], [])

    def relay_cut(value, far, cut, bit):
        return (cut.take(value, dp ^ (3 - bit), 1).astype(F32) + far.astype(F32)).astype(BF16)

    def share_sum(value, cut, near, relayed):
        own = cut.take(value, dp, 1).astype(F32)
        return (own + near.astype(F32) + relayed.astype(F32)).astype(BF16)

    def up_product(r):
        return token_product(n2_all, du_all, r, n_row, True)

    def down_product(r):
        return token_product(g_all, hidden_all, r, n_row, False).reshape(n_col, width, ff_part)

    dn2 = lax.psum_scatter(part2, "col", scatter_dimension=1, tiled=True)
    up_grad = [up_product(r) for r in other_rows[1:]]
    n2_all, hidden_all, *up_grad = gate([n2_all, hidden_all] + up_grad, [])

    up_grad = [turn(p, "row", i + 1) for i, p in enumerate(up_grad)]
    up_grad = [up_product(other_rows[0])] + up_grad
    down_grad = [down_product(r) for r in other_rows[1:]]
    hidden_all, *rest = gate([hidden_all] + up_grad + down_grad, [])
    up_grad, down_grad = rest[:n_row], rest[n_row:]
    up_rows = width if in_rows % width == 0 else in_rows
    up_shares, fine = Shares(up_rows, 8), Shares(width, 8)
    up_grad = sum(p.astype(F32) for p in up_grad).astype(BF16)
    up_grad = up_grad.reshape(in_rows // up_rows, up_rows, ff)
    up_far = up_shares.take(up_grad, dp ^ 3, 1)
    up_far, hidden_all, *down_grad = gate([up_far, hidden_all] + down_grad, [])

    up_far = swap_with(up_far, 1)
    down_grad = [turn(p, "row", i + 1) for i, p in enumerate(down_grad)]
    down_grad = [down_product(other_rows[0])] + down_grad
    hidden_all, *down_grad = gate([hidden_all] + down_grad, [])
    down_grad = sum(p.astype(F32) for p in down_grad).astype(BF16)
    down_far = fine.take(down_grad, dp ^ 3, 1)
    down_far, hidden_all = gate([down_far, hidden_all], [])

    down_far = swap_with(down_far, 2)
    up_near = up_shares.take(up_grad, dp ^ 1, 1)
    down_near = fine.take(down_grad, dp ^ 2, 1)
    du_row = du_sums[:, 0]
    shrunk = split_product(down_weights, hidden_all, row_at, columns, 5, BF16)
    own_sum = block(shrunk, col, part, 1).astype(F32) + resid
    shrunk = lax.dynamic_update_slice_in_dim(shrunk, own_sum.astype(BF16), col * part, 1)
    up_relay = relay_cut(up_grad, up_far, up_shares, 1)
    down_relay = relay_cut(down_grad, down_far, fine, 2)
    g_part = block(g_all, col, part, 1)
    dn2, shrunk, up_relay, down_relay, up_near, down_near, du_row, g_part = gate(
        [dn2, shrunk, up_relay, down_relay, up_near, down_near, du_row, g_part], []
    )

    up_near = swap_with(up_near, 1)
    down_near = swap_with(down_near, 2)
    dr, db, da, sums2 = mixed_norm_back(out_weights, dn2, hat2, rstd2, g_part, row_at, columns)
    early = jnp.concatenate([sums2.T.reshape(-1), du_row, g_sums])
    da_cuts = [
        lax.dynamic_slice_in_dim(da, firsts[(col + step) % n_col], window, 0)
        for step in range(n_col)
    ]
    db, shrunk, up_near, down_near, up_relay, down_relay, *da_cuts = gate(
        [db, shrunk, up_near, down_near, up_relay, down_relay] + da_cuts, []
    )

    got = [turn(cut, "col", step) for step, cut in enumerate(da_cuts)]
    up_relay = swap_with(up_relay, 2)
    down_relay = swap_with(down_relay, 1)
    out_grad = [token_product(db, attention, r, n_row, False) for r in other_rows[::-1]][::-1]
    out_grad = [o.reshape(n_col, width, in_rows) for o in out_grad]
    rest = gate(got[1:] + out_grad + [up_relay, down_relay, shrunk], [])
    got, rest = got[:1] + rest[: n_col - 1], rest[n_col - 1 :]
    out_grad, (up_relay, down_relay, shrunk) = rest[:n_row], rest[n_row:]

    outputs = lax.psum_scatter(shrunk, "col", scatter_dimension=0, tiled=True)
    da_own = jnp.concatenate(ordered(got, col, -1), 1)
    da_pieces = [da_own] + [turn(da_own, "row", -step) for step in range(1, n_row)]
    out_grad = row_sum(out_grad).astype(BF16)
    up_share = share_sum(up_grad, up_shares, up_near, up_relay)
    down_share = share_sum(down_grad, fine, down_near, down_relay)
    out_sent = jnp.stack([fine.take(out_grad, dp ^ 1, 1), fine.take(out_grad, dp ^ 3, 1)])
    *rest, out_sent, up_share, down_share = gate(
        da_pieces[1:] + [out_sent, up_share, down_share], []
    )
    da_pieces = [da_own] + rest

    out_first = swap_with(out_sent, 1)
    up_y = swap_with(up_share, 2)

    def move_home(step):
        return pick(down_share, (place_in + step) % n_col)

    down_home = between_owners(move_home, range(half), True)
    dqkv = attn_bwd(meta, key_start, pieces, da_pieces, mixed, norms, heads.slots, size)
    *rest, out_first, up_y, up_share, down_share = gate(
        list(dqkv) + down_home + [out_first, up_y, up_share, down_share], []
    )
    dqkv, down_home = rest[:n_row], rest[n_row:]
    out_near, out_far = out_first[0], out_first[1]
    out_relay = relay_cut(out_grad, out_far, fine, 1)

    out_relay = swap_with(out_relay, 2)
    up_x = swap_with(up_share, 1)
    down_home = down_home + between_owners(move_home, range(half, n_col), True)
    dqkv = row_sum(dqkv).astype(BF16).reshape(3 * window, length)
    out_near, out_grad, *down_home = gate([out_near, out_grad] + down_home, [dqkv])
    homes = jnp.stack(ordered(down_home, col, -1))
    out_share = share_sum(out_grad, fine, out_near, out_relay)
    qkv_parts = [
        token_product(dqkv, n1, r, n_row, False).reshape(3, window, in_rows)
        for r in other_rows[:0:-1]
    ][::-1]
    dqkv, homes, outputs, up_x, out_share, *qkv_parts = gate(
        [dqkv, homes, outputs, up_x, out_share] + qkv_parts, []
    )

    homes_near = [swap_with(homes, 1), swap_with(homes, 2)]
    own = token_product(dqkv, n1, other_rows[0], n_row, False).reshape(3, window, in_rows)
    qkv_grad = row_sum([own] + qkv_parts).astype(BF16)
    wide, to_left, to_right = narrow_cuts(qkv_grad, 1, heads, col, width)
    dqkv, wide, to_left, to_right, out_share, up_y, *homes_near = gate(
        [dqkv, wide, to_left, to_right, out_share, up_y] + homes_near, []
    )

    out_home = lax.psum_scatter(out_share, "col", scatter_dimension=0, tiled=True)
    tail, front = go_down(to_left, 1, n_col - 1), go_up(to_right, 0, n_col - 2)
    homes_far = swap_with(homes_near[1], 1)
    up_far = swap_with(up_x, 2)
    dn1, norm1 = norm_product_tn(w3, dqkv, n1, columns, rstd1, dr, col_at, n_col)
    qkv_grad = narrow(wide, front, tail, 1, heads, width).astype(BF16)
    qkv_sent = [fine.take(qkv_grad, dp ^ m, 1) for m in (1, 2, 3)]
    dn1, dqkv, homes_far, up_far, out_home, *qkv_sent = gate(
        [dn1, dqkv, homes_far, up_far, out_home] + qkv_sent, [norm1]
    )

    dx = lax.psum_scatter(dn1, "col", scatter_dimension=0, tiled=True)
    qkv_got = [swap_with(v, m) for v, m in zip(qkv_sent, (1, 2, 3))]
    out_all = [swap_with(out_home, 1), swap_with(out_home, 2)]
    homes, homes_far, norm1, outputs, dqkv = gate(
        [homes, homes_far, norm1, outputs, dqkv], qkv_sent
    )
    homes = fine.join([homes] + homes_near + [homes_far], dp, 1).astype(F32)
    down_grad = jnp.concatenate([homes[j] for j in range(n_col)], 1)
    outputs = (outputs.astype(F32) + down_bias[:, None]).astype(BF16)
    dq_dv = jnp.sum(dqkv.astype(F32), axis=1).reshape(3, window)
    sums = lax.dynamic_update_slice_in_dim(jnp.zeros((2, depth), F32), dq_dv[::2], begin, 1)
    small = jnp.concatenate([sums.reshape(-1), norm1.T.reshape(-1), early])[None]
    small = small_sum(small, ("row",))[0]
    sums, local = small[: 7 * depth].reshape(7, depth), small[7 * depth :]
    sums = small_sum(sums, ("col",))
    sums = lax.dynamic_slice_in_dim(sums, col * width, width, 1)
    small = jnp.concatenate([sums.reshape(-1), local])
    deep = -(-small.shape[0] // in_rows)
    small = jnp.pad(small, (0, deep * in_rows - small.shape[0])).reshape(deep, in_rows)
    rounded = lax.reduce_precision(small, 8, 7)
    rest = (small - rounded).astype(BF16)
    rounded = rounded.astype(BF16)
    qkv_share = fine.take(qkv_grad, dp, 1).astype(F32)
    qkv_share = (qkv_share + sum(q.astype(F32) for q in qkv_got)).astype(BF16)
    ends = 3 * fine.size
    payload = jnp.concatenate([qkv_share.reshape(ends, in_rows), rounded, rest])
    up_far, payload, *out_all = gate([up_far, payload] + out_all, [down_grad, outputs])

    qkv_all = swap_all(payload)
    out_all.append(swap_with(out_all[0], 2))
    up_grad = up_shares.join([up_share, up_x, up_y, up_far], dp, 1).astype(F32)
    up_grad = up_grad.reshape(in_rows, ff)
    hat1 = (x.astype(F32) - mean1) * rstd1
    dx = dx.reshape(width + 16, length)
    lines = dx[width : width + 4].astype(F32)
    lines = (lines[0::2] + lines[1::2]) / depth
    input_grad = dx[:width].astype(F32) - rstd1 * (lines[0:1] + hat1 * lines[1:2])
    input_grad = input_grad.astype(BF16)
    *out_all, a, b, c = gate(out_all + qkv_all, [up_grad, input_grad])

    out_grad = fine.join([out_home] + out_all, dp, 1).astype(F32)[0]
    small = sum(v[ends:].astype(F32) for v in (payload, a, b, c))
    small = (small[:deep] + small[deep:]).reshape(-1)
    sums, local = small[: 7 * width].reshape(7, width), small[7 * width : 8 * width + ff]
    qkv_all = [v[:ends].reshape(3, fine.size, in_rows) for v in (payload, a, b, c)]
    qkv_grad = fine.join(qkv_all, dp, 1).astype(F32)
    return (
        outputs.T.reshape(tokens.shape),
        input_grad.T.reshape(tokens.shape),
        qkv_grad.transpose(0, 2, 1),
        sums[0],
        sums[1],
        out_grad.T,
        sums[4],
        up_grad,
        local[:ff],
        down_grad.T,
        local[ff:],
        sums[2],
        sums[3],
        sums[5],
        sums[6],
    )


def solution(mesh):
    inputs = (
        P("dp", "row", "col"),
        P("dp", "row", "col"),
        P(None, "row", "col"),
        P("col"),
        P("col"),
        P("row", "col"),
        P("col"),
        P("row", "col"),
        P("col"),
        P("row", "col"),
        P("col"),
        P("col"),
        P("col"),
        P("col"),
        P("col"),
        P(),
    )
    return jax.shard_map(
        body, mesh=mesh, in_specs=inputs, out_specs=inputs[:15], check_vma=False
    )
```

```python
import functools

import jax
import jax.numpy as jnp
from jax import lax
from jax.experimental import pallas as pl
from jax.experimental.pallas import tpu as pltpu
from jax.sharding import PartitionSpec as P

BLK = 512
EPSILON = 1e-05
LOG2E = 1.4426950408889634
BF16 = jnp.bfloat16
F32 = jnp.float32

FREE = pl.CostEstimate(flops=0, bytes_accessed=0, transcendentals=0)
ROOM = pltpu.CompilerParams(vmem_limit_bytes=56 * 2**20)

NT=(((0,),(0,)),((),()))
TN=(((1,),(1,)),((),()))

def plan_tiles(meta, ks, own, load, n_slots, n_blocks, n_row, n_heads):
    for i in range(n_row): load[i]=0
    def level(lv,_):
        cost=n_blocks-lv
        def tile(t,_):
            slot=t//n_blocks; qb=t%n_blocks
            head=meta[0]+slot
            here=head<n_heads
            hd=jnp.minimum(head,n_heads-1)
            n=qb+1-ks[hd,qb]
            mask=jnp.where(slot==0,meta[2],jnp.where(slot==n_slots-1,meta[3],(1<<n_blocks)-1))
            here=jnp.logical_and(here,((mask>>qb)&1)==1)
            @pl.when(cost==n_blocks)
            def _(): own[t]=-1
            @pl.when(jnp.logical_and(here,n==cost))
            def _():
                best=load[0]; who=jnp.int32(0)
                for i in range(1,n_row):
                    less=load[i]<best
                    best=jnp.where(less,load[i],best); who=jnp.where(less,i,who)
                own[t]=who
                load[who]=best+cost
            return 0
        lax.fori_loop(0,n_slots*n_blocks,tile,0)
        return 0
    lax.fori_loop(0,n_blocks,level,0)

def fetch(pieces, whole, sems, row, n_row, width):
    copies=[]
    for i,p in enumerate(pieces):
        at=lax.rem(row+i,n_row)*width
        c=pltpu.make_async_copy(p, whole.at[...,pl.ds(pl.multiple_of(at,width),width)], sems.at[i])
        c.start(); copies.append(c)
    return copies

def fwd_kernel(n_row,n_slots,hd,n_heads,meta,ks,*refs):
    pieces=refs[:n_row]; cuts=refs[n_row:2*n_row]; o_ref,lse_ref,whole,own,load,sems=refs[2*n_row:]
    S=whole.shape[2]; nb=S//BLK; width=S//n_row
    row=meta[1]
    copies=fetch(pieces,whole,sems,row,n_row,width)
    plan_tiles(meta,ks,own,load,n_slots,nb,n_row,n_heads)
    o_ref[...]=jnp.zeros_like(o_ref)
    for c in copies: c.wait()
    c2=hd**-0.5*LOG2E
    diag=lax.broadcasted_iota(jnp.int32,(BLK,BLK),0)<=lax.broadcasted_iota(jnp.int32,(BLK,BLK),1)
    def tile(t,_):
        @pl.when(own[t]==row)
        def _():
            slot=t//nb; qb=t%nb
            first=ks[meta[0]+slot,qb]
            hs=pl.ds(pl.multiple_of(slot*hd,hd),hd)
            qs=pl.ds(pl.multiple_of(qb*BLK,BLK),BLK)
            q=whole[0,hs,qs]
            def scores(kb_ds):
                return lax.dot_general(whole[1,hs,kb_ds],q,NT,preferred_element_type=jnp.float32)
            s=jnp.where(diag,scores(qs),-1e30)
            m=jnp.max(s,axis=0,keepdims=True)
            p=jnp.exp2((s-m)*c2)
            l=jnp.sum(p,axis=0,keepdims=True)
            acc=jnp.dot(whole[2,hs,qs],p.astype(jnp.bfloat16),preferred_element_type=jnp.float32)
            def step(kb,carry):
                m,l,acc=carry
                kd=pl.ds(pl.multiple_of(kb*BLK,BLK),BLK)
                s=scores(kd)
                mn=jnp.maximum(m,jnp.max(s,axis=0,keepdims=True))
                a=jnp.exp2((m-mn)*c2)
                p=jnp.exp2((s-mn)*c2)
                l=l*a+jnp.sum(p,axis=0,keepdims=True)
                acc=acc*a+jnp.dot(whole[2,hs,kd],p.astype(jnp.bfloat16),preferred_element_type=jnp.float32)
                return mn,l,acc
            m,l,acc=lax.fori_loop(first,qb,step,(m,l,acc))
            o_ref[hs,qs]=(acc/l).astype(jnp.bfloat16)
            lse_ref[pl.ds(slot,1),qs]=m*c2+jnp.log2(l)
        return 0
    lax.fori_loop(0,n_slots*nb,tile,0)
    for i,cut in enumerate(cuts):
        cut[...]=o_ref[:,pl.ds(pl.multiple_of(lax.rem(row+i,n_row)*width,width),width)]

def bwd_kernel(n_row,n_slots,hd,n_heads,meta,ks,*refs):
    pieces=refs[:n_row]; das=refs[n_row:2*n_row]
    o_ref,lse_ref=refs[2*n_row:2*n_row+2]; cuts=refs[2*n_row+2:3*n_row+2]
    d_ref,whole,da,acc,own,load,sems,sems2=refs[3*n_row+2:]
    S=whole.shape[2]; nb=S//BLK; width=S//n_row
    row=meta[1]
    copies=fetch(pieces,whole,sems,row,n_row,width)+fetch(das,da,sems2,row,n_row,width)
    plan_tiles(meta,ks,own,load,n_slots,nb,n_row,n_heads)
    d_ref[...]=jnp.zeros_like(d_ref)
    acc[...]=jnp.zeros_like(acc)
    for c in copies: c.wait()
    scale=hd**-0.5; c2=scale*LOG2E
    diag=lax.broadcasted_iota(jnp.int32,(BLK,BLK),0)<=lax.broadcasted_iota(jnp.int32,(BLK,BLK),1)
    def tile(t,_):
        @pl.when(own[t]==row)
        def _():
            slot=t//nb; qb=t%nb
            first=ks[meta[0]+slot,qb]
            hs=pl.ds(pl.multiple_of(slot*hd,hd),hd)
            qs=pl.ds(pl.multiple_of(qb*BLK,BLK),BLK)
            q=whole[0,hs,qs]
            up=da[hs,qs]
            lse=lse_ref[pl.ds(slot,1),qs]
            delta=jnp.sum(up.astype(jnp.float32)*o_ref[hs,qs].astype(jnp.float32),axis=0,keepdims=True)
            def block(kd,masked):
                k=whole[1,hs,kd]
                s=lax.dot_general(k,q,NT,preferred_element_type=jnp.float32)
                p=jnp.exp2(s*c2-lse)
                if masked: p=jnp.where(diag,p,0.0)
                dp=lax.dot_general(whole[2,hs,kd],up,NT,preferred_element_type=jnp.float32)
                ds=(p*(dp-delta)).astype(jnp.bfloat16)
                acc[1,hs,kd]+=lax.dot_general(up,p.astype(jnp.bfloat16),TN,preferred_element_type=jnp.float32)
                acc[0,hs,kd]+=lax.dot_general(q,ds,TN,preferred_element_type=jnp.float32)
                return jnp.dot(k,ds,preferred_element_type=jnp.float32)
            dq=block(qs,True)
            dq=lax.fori_loop(first,qb,lambda kb,dq:dq+block(pl.ds(pl.multiple_of(kb*BLK,BLK),BLK),False),dq)
            d_ref[hs,qs]=(dq*scale).astype(jnp.bfloat16)
        return 0
    lax.fori_loop(0,n_slots*nb,tile,0)
    for i,cut in enumerate(cuts):
        at=pl.ds(pl.multiple_of(lax.rem(row+i,n_row)*width,width),width)
        cut[0]=d_ref[:,at]
        cut[1]=(acc[0,:,at]*scale).astype(jnp.bfloat16)
        cut[2]=acc[1,:,at].astype(jnp.bfloat16)

V=pl.BlockSpec(memory_space=pltpu.VMEM); SM=pl.BlockSpec(memory_space=pltpu.SMEM); ANY=pl.BlockSpec(memory_space=pl.ANY)
def attn_fwd(meta,ks,pieces,n_slots,hd):
    n_row=len(pieces); _,H,T=pieces[0].shape; S=T*n_row; nb=S//BLK
    return pl.pallas_call(functools.partial(fwd_kernel,n_row,n_slots,hd,ks.shape[0]),
      out_shape=[jax.ShapeDtypeStruct((H,T),jnp.bfloat16)]*n_row+[jax.ShapeDtypeStruct((H,S),jnp.bfloat16),jax.ShapeDtypeStruct((n_slots,S),jnp.float32)],
      in_specs=[SM,SM]+[ANY]*n_row,out_specs=[V]*(n_row+2),
      scratch_shapes=[pltpu.VMEM((3,H,S),jnp.bfloat16),pltpu.SMEM((n_slots*nb,),jnp.int32),pltpu.SMEM((n_row,),jnp.int32),pltpu.SemaphoreType.DMA((n_row,))],
      compiler_params=pltpu.CompilerParams(vmem_limit_bytes=48*2**20),
      cost_estimate=FREE,
    )(meta,ks,*pieces)
def attn_bwd(meta,ks,pieces,das,o,lse,n_slots,hd):
    n_row=len(pieces); _,H,T=pieces[0].shape; S=T*n_row; nb=S//BLK
    return pl.pallas_call(functools.partial(bwd_kernel,n_row,n_slots,hd,ks.shape[0]),
      out_shape=[jax.ShapeDtypeStruct((3,H,T),jnp.bfloat16)]*n_row,
      in_specs=[SM,SM]+[ANY]*(2*n_row)+[V,V],out_specs=[V]*n_row,
      scratch_shapes=[pltpu.VMEM((H,S),jnp.bfloat16),pltpu.VMEM((3,H,S),jnp.bfloat16),pltpu.VMEM((H,S),jnp.bfloat16),pltpu.VMEM((2,H,S),jnp.float32),pltpu.SMEM((n_slots*nb,),jnp.int32),pltpu.SMEM((n_row,),jnp.int32),pltpu.SemaphoreType.DMA((n_row,)),pltpu.SemaphoreType.DMA((n_row,))],
      compiler_params=pltpu.CompilerParams(vmem_limit_bytes=56*2**20),
      cost_estimate=FREE,
    )(meta,ks,*pieces,*das,o,lse)


def rows_of(total, most):
    for rows in range(min(total, most) // 16 * 16, 0, -16):
        if total % rows == 0:
            return rows
    return total


def by_rows(i, *refs):
    return (i, 0)


def whole_block(i, *refs):
    return (0, 0)


def product_kernel(a_ref, b_ref, bias_ref, o_ref):
    o_ref[...] = (
        jnp.dot(a_ref[...], b_ref[...], preferred_element_type=F32) + bias_ref[...]
    ).astype(o_ref.dtype)


def product(a, b, bias):
    rows = rows_of(a.shape[0], 448)
    return pl.pallas_call(
        product_kernel,
        out_shape=jax.ShapeDtypeStruct((a.shape[0], b.shape[1]), BF16),
        grid=(a.shape[0] // rows,),
        in_specs=[
            pl.BlockSpec((rows, a.shape[1]), by_rows),
            pl.BlockSpec(b.shape, whole_block),
            pl.BlockSpec((rows, 1), by_rows),
        ],
        out_specs=pl.BlockSpec((rows, b.shape[1]), by_rows),
        compiler_params=ROOM,
        cost_estimate=FREE,
    )(a, b, bias)


def split_product(parts, b, row, columns, which, dtype):
    n = len(parts)
    total, depth = parts[0].shape
    width = b.shape[1]
    rows = rows_of(total, 400)

    def kernel(row_ref, b_ref, bias_ref, *refs):
        out = bias_ref[:, which : which + 1] + jnp.zeros((rows, width), F32)
        for i in range(n):
            at = pl.multiple_of(lax.rem(row_ref[0] + i, n) * depth, 8)
            out = out + jnp.dot(refs[i][...], b_ref[pl.ds(at, depth), :], preferred_element_type=F32)
        refs[n][...] = out.astype(dtype)

    return pl.pallas_call(
        kernel,
        out_shape=jax.ShapeDtypeStruct((total, width), dtype),
        grid=(total // rows,),
        in_specs=[
            SM,
            pl.BlockSpec(b.shape, whole_block),
            pl.BlockSpec((rows, columns.shape[1]), by_rows),
        ]
        + [pl.BlockSpec((rows, depth), by_rows)] * n,
        out_specs=pl.BlockSpec((rows, width), by_rows),
        compiler_params=ROOM,
        cost_estimate=FREE,
    )(row, b, columns, *parts)


def mixed_norm(parts, b, row, columns, x):
    n = len(parts)
    total, depth = parts[0].shape
    width = b.shape[1]
    rows = rows_of(total, 400)
    steps = total // rows

    def kernel(row_ref, b_ref, c_ref, x_ref, *refs):
        o_ref, hat_ref, norm_ref, scale_ref = refs[n:]
        step = pl.program_id(0)
        at = pl.ds(pl.multiple_of(step * rows, 8), rows)
        out = c_ref[at, 2:3] + x_ref[...].astype(F32)
        for i in range(n):
            here = pl.multiple_of(lax.rem(row_ref[0] + i, n) * depth, 8)
            out = out + jnp.dot(
                refs[i][...], b_ref[pl.ds(here, depth), :], preferred_element_type=F32
            )
        o_ref[at, :] = out

        @pl.when(step == steps - 1)
        def end():
            mean = jnp.sum(o_ref[...], axis=0, keepdims=True) / total
            centred = o_ref[...] - mean
            scale = lax.rsqrt(jnp.sum(centred * centred, axis=0, keepdims=True) / total + EPSILON)
            hat = centred * scale
            hat_ref[...] = hat
            norm_ref[...] = (hat * c_ref[:, 3:4] + c_ref[:, 4:5]).astype(BF16)
            scale_ref[...] = scale

    return pl.pallas_call(
        kernel,
        out_shape=[
            jax.ShapeDtypeStruct((total, width), F32),
            jax.ShapeDtypeStruct((total, width), F32),
            jax.ShapeDtypeStruct((total, width), BF16),
            jax.ShapeDtypeStruct((1, width), F32),
        ],
        grid=(steps,),
        in_specs=[
            SM,
            pl.BlockSpec(b.shape, whole_block),
            pl.BlockSpec(columns.shape, whole_block),
            pl.BlockSpec((rows, width), by_rows),
        ]
        + [pl.BlockSpec((rows, depth), by_rows)] * n,
        out_specs=[
            pl.BlockSpec((total, width), whole_block),
            pl.BlockSpec((total, width), whole_block),
            pl.BlockSpec((total, width), whole_block),
            pl.BlockSpec((1, width), whole_block),
        ],
        compiler_params=ROOM,
        cost_estimate=FREE,
    )(row, b, columns, x, *parts)


def mixed_norm_back(parts, dn, hat, scale, g, row, columns):
    n = len(parts)
    depth = parts[0].shape[1]
    total, width = dn.shape
    rows = rows_of(total, 400)
    steps = total // rows

    def kernel(row_ref, dn_ref, hat_ref, scale_ref, g_ref, c_ref, *refs):
        o_ref, low_ref, a_ref, s_ref, acc = refs[n:]
        step = pl.program_id(0)

        @pl.when(step == 0)
        def start():
            grad = dn_ref[...].astype(F32)
            up = grad * c_ref[:, 3:4]
            hat = hat_ref[...]
            pull = jnp.sum(up, axis=0, keepdims=True) / total
            lean = jnp.sum(up * hat, axis=0, keepdims=True) / total
            out = g_ref[...].astype(F32) + scale_ref[...] * (up - pull - hat * lean)
            low = out.astype(BF16)
            o_ref[...] = out
            low_ref[...] = low
            s_ref[:, 0:1] = jnp.sum(low.astype(F32), axis=1, keepdims=True)
            s_ref[:, 1:2] = jnp.sum(grad * hat, axis=1, keepdims=True)
            s_ref[:, 2:3] = jnp.sum(grad, axis=1, keepdims=True)
            acc[...] = jnp.zeros_like(acc)

        cut = low_ref[pl.ds(pl.multiple_of(step * rows, 8), rows), :]
        for i in range(n):
            here = pl.ds(pl.multiple_of(lax.rem(row_ref[0] + i, n) * depth, 8), depth)
            acc[here, :] += lax.dot_general(refs[i][...], cut, NT, preferred_element_type=F32)

        @pl.when(step == steps - 1)
        def end():
            a_ref[...] = acc[...].astype(BF16)

    full = pl.BlockSpec((total, width), whole_block)
    return pl.pallas_call(
        kernel,
        out_shape=[
            jax.ShapeDtypeStruct((total, width), F32),
            jax.ShapeDtypeStruct((total, width), BF16),
            jax.ShapeDtypeStruct((n * depth, width), BF16),
            jax.ShapeDtypeStruct((total, 3), F32),
        ],
        grid=(steps,),
        in_specs=[
            SM,
            full,
            full,
            pl.BlockSpec((1, width), whole_block),
            full,
            pl.BlockSpec(columns.shape, whole_block),
        ]
        + [pl.BlockSpec((rows, depth), by_rows)] * n,
        out_specs=[
            full,
            full,
            pl.BlockSpec((n * depth, width), whole_block),
            pl.BlockSpec((total, 3), whole_block),
        ],
        scratch_shapes=[pltpu.VMEM((n * depth, width), F32)],
        compiler_params=ROOM,
        cost_estimate=FREE,
    )(row, dn, hat, scale, g, columns, *parts)


def norm_product_tn(a, b, normed, columns, scale, riding, col, n_col):
    rows = rows_of(a.shape[0], 448)
    steps = a.shape[0] // rows
    depth, tokens = a.shape[1], b.shape[1]
    cut, part = depth // n_col, tokens // n_col

    def kernel(col_ref, a_ref, b_ref, n_ref, g_ref, c_ref, r_ref, o_ref, f_ref, acc):
        @pl.when(pl.program_id(0) == 0)
        def start():
            acc[...] = lax.dot_general(a_ref[...], b_ref[...], NT, preferred_element_type=F32)

        @pl.when(pl.program_id(0) > 0)
        def more():
            acc[...] += lax.dot_general(a_ref[...], b_ref[...], NT, preferred_element_type=F32)

        @pl.when(pl.program_id(0) == steps - 1)
        def end():
            first = jnp.zeros((1, tokens), F32)
            second = jnp.zeros((1, tokens), F32)
            for j in range(n_col):
                at = pl.ds(j * cut, cut)
                p = acc[at, :]
                scaled = p * g_ref[at, 0:1]
                o_ref[j, 0:cut, :] = (scaled * c_ref[...]).astype(BF16)
                moved = p * (n_ref[at, :].astype(F32) - g_ref[at, 1:2])
                first += jnp.sum(scaled, axis=0, keepdims=True)
                second += jnp.sum(moved, axis=0, keepdims=True)
                f_ref[at, 0:1] = jnp.sum(moved, axis=1, keepdims=True) / g_ref[at, 0:1]
                f_ref[at, 1:2] = jnp.sum(p, axis=1, keepdims=True)
                for c in range(n_col):

                    @pl.when(col_ref[0] == c)
                    def ride():
                        here = slice(c * part, (c + 1) * part)
                        own = scaled[:, here] * c_ref[:, here] + r_ref[at, :]
                        o_ref[j, 0:cut, here] = own.astype(BF16)

            lines = []
            for line in (first, second):
                high = line.astype(BF16).astype(F32)
                lines += [high, line - high]
            lines = jnp.concatenate(lines + [jnp.zeros((12, tokens), F32)]).astype(BF16)
            for j in range(n_col):
                o_ref[j, cut : cut + 16, :] = lines

    return pl.pallas_call(
        kernel,
        out_shape=[
            jax.ShapeDtypeStruct((n_col, cut + 16, tokens), BF16),
            jax.ShapeDtypeStruct((depth, 2), F32),
        ],
        grid=(steps,),
        in_specs=[
            SM,
            pl.BlockSpec((rows, depth), by_rows),
            pl.BlockSpec((rows, tokens), by_rows),
            pl.BlockSpec((depth, tokens), whole_block),
            pl.BlockSpec(columns.shape, whole_block),
            pl.BlockSpec((1, tokens), whole_block),
            pl.BlockSpec((depth, part), whole_block),
        ],
        out_specs=[
            pl.BlockSpec((n_col, cut + 16, tokens), lambda i: (0, 0, 0)),
            pl.BlockSpec((depth, 2), whole_block),
        ],
        scratch_shapes=[pltpu.VMEM((depth, tokens), F32)],
        compiler_params=ROOM,
        cost_estimate=FREE,
    )(col, a, b, normed, columns, scale, riding)


def token_product(a, b, index, parts, of_a):
    rows_a = a.shape[0] // (parts if of_a else 1)
    rows_b = b.shape[0] // (1 if of_a else parts)
    rows = rows_of(rows_a, 448)
    steps = rows_a // rows

    def kernel(index_ref, a_ref, b_ref, o_ref):
        o_ref[...] = lax.dot_general(
            a_ref[...], b_ref[...], TN, preferred_element_type=F32
        ).astype(BF16)

    if of_a:
        a_map, b_map = (lambda i, r: (r[0] * steps + i, 0)), whole_block
    else:
        a_map, b_map = by_rows, (lambda i, r: (r[0], 0))
    return pl.pallas_call(
        kernel,
        out_shape=jax.ShapeDtypeStruct((rows_a, rows_b), BF16),
        grid_spec=pltpu.PrefetchScalarGridSpec(
            num_scalar_prefetch=1,
            grid=(steps,),
            in_specs=[
                pl.BlockSpec((rows, a.shape[1]), a_map),
                pl.BlockSpec((rows_b, b.shape[1]), b_map),
            ],
            out_specs=pl.BlockSpec((rows, rows_b), by_rows),
        ),
        compiler_params=ROOM,
        cost_estimate=FREE,
    )(index, a, b)


def gelu_parts(u):
    inner = 0.7978845608 * (u + 0.044715 * u * u * u)
    t = jnp.tanh(inner)
    value = 0.5 * u * (1.0 + t)
    slope = 0.5 * (1.0 + t) + 0.5 * u * (1.0 - t * t) * 0.7978845608 * (1.0 + 0.134145 * u * u)
    return value, slope


def hidden_layer(up, down, n, bias, n2, g, row):
    ff, depth = up.shape
    tokens = n2.shape[1]
    rows = rows_of(ff // n, 400)
    cuts = ff // n // rows
    steps = ff // rows

    def kernel(row_ref, up_ref, down_ref, bias_ref, n_ref, g_ref, h_ref, d_ref, p_ref, s_ref, acc):
        step = pl.program_id(0)
        u = jnp.dot(up_ref[...], n_ref[...], preferred_element_type=F32) + bias_ref[...]
        value, slope = gelu_parts(u)
        h_ref[...] = value.astype(BF16)
        dh = jnp.dot(down_ref[...], g_ref[...], preferred_element_type=F32)
        du = (dh * slope).astype(BF16)
        d_ref[...] = du
        s_ref[...] = jnp.sum(du.astype(F32), axis=1, keepdims=True)

        @pl.when(step == 0)
        def start():
            acc[...] = lax.dot_general(up_ref[...], du, NT, preferred_element_type=F32)

        @pl.when(step > 0)
        def more():
            acc[...] += lax.dot_general(up_ref[...], du, NT, preferred_element_type=F32)

        @pl.when(step == steps - 1)
        def end():
            p_ref[...] = acc[...].astype(BF16)

    mine = lambda i, r: (lax.rem(r[0] * cuts + i, steps), 0)
    full = lambda i, r: (0, 0)
    return pl.pallas_call(
        kernel,
        out_shape=[
            jax.ShapeDtypeStruct((ff, tokens), BF16),
            jax.ShapeDtypeStruct((ff, tokens), BF16),
            jax.ShapeDtypeStruct((depth, tokens), BF16),
            jax.ShapeDtypeStruct((ff, 1), F32),
        ],
        grid_spec=pltpu.PrefetchScalarGridSpec(
            num_scalar_prefetch=1,
            grid=(steps,),
            in_specs=[
                pl.BlockSpec((rows, depth), mine),
                pl.BlockSpec((rows, depth), lambda i, r: (i, 0)),
                pl.BlockSpec((rows, 1), mine),
                pl.BlockSpec((depth, tokens), full),
                pl.BlockSpec((depth, tokens), full),
            ],
            out_specs=[
                pl.BlockSpec((rows, tokens), mine),
                pl.BlockSpec((rows, tokens), mine),
                pl.BlockSpec((depth, tokens), full),
                pl.BlockSpec((rows, 1), mine),
            ],
            scratch_shapes=[pltpu.VMEM((depth, tokens), F32)],
        ),
        compiler_params=ROOM,
        cost_estimate=FREE,
    )(row, up, down, bias, n2, g)


def turned(parts):
    n = len(parts)
    depth, wide = parts[0].shape

    def kernel(*refs):
        o_ref = refs[n]
        for i in range(n):
            for first in range(0, wide, 256):
                size = min(256, wide - first)
                at = lax.broadcasted_iota(jnp.int32, (size, size), 0)
                ones = (at == lax.broadcasted_iota(jnp.int32, (size, size), 1)).astype(BF16)
                cut = refs[i][:, first : first + size]
                out = lax.dot_general(ones, cut, TN, preferred_element_type=F32)
                o_ref[i * wide + first : i * wide + first + size, :] = out.astype(BF16)

    return pl.pallas_call(
        kernel,
        out_shape=jax.ShapeDtypeStruct((n * wide, depth), BF16),
        in_specs=[V] * n,
        out_specs=V,
        compiler_params=ROOM,
        cost_estimate=FREE,
    )(*parts)


def gate(values, others):
    def kernel(*refs):
        pass

    out = pl.pallas_call(
        kernel,
        out_shape=[jax.ShapeDtypeStruct(v.shape, v.dtype) for v in values],
        in_specs=[ANY] * (len(values) + len(others)),
        out_specs=[ANY] * len(values),
        input_output_aliases={i: i for i in range(len(values))},
        cost_estimate=FREE,
    )(*values, *others)
    return list(out)


def turn(value, axis, steps):
    size = lax.axis_size(axis)
    if steps % size == 0:
        return value
    return lax.ppermute(value, axis, [(i, (i + steps) % size) for i in range(size)])


def block(value, index, size, axis):
    return lax.dynamic_slice_in_dim(value, index * size, size, axis)


def row_sum(parts):
    total = parts[0].astype(F32)
    for step in range(1, len(parts)):
        total = total + turn(parts[step], "row", step).astype(F32)
    return total


def swap_with(value, bit):
    return lax.ppermute(value, "dp", [(i, i ^ bit) for i in range(4)])


def pick(value, index, axis=0):
    return lax.dynamic_index_in_dim(value, index, axis, keepdims=False)


def dot(a, b):
    return jnp.dot(a, b, preferred_element_type=F32)


def ordered(parts, base, sign):
    size = len(parts)
    stacked = jnp.stack(parts)
    return [pick(stacked, (sign * (j - base)) % size) for j in range(size)]


class Shares:
    def __init__(self, rows, tile):
        self.rows = rows
        self.size = -(-rows // (4 * tile)) * tile
        self.starts = [(rows - self.size) * s // (3 * tile) * tile for s in range(3)]
        self.starts.append(rows - self.size)
        ends = self.starts[1:] + [rows]
        self.lengths = [b - a for a, b in zip(self.starts, ends)]

    def take(self, value, share, axis):
        start = jnp.array(self.starts, jnp.int32)[share]
        return lax.dynamic_slice_in_dim(value, start, self.size, axis)

    def lay(self, parts, axis):
        return jnp.concatenate(
            [lax.slice_in_dim(p, 0, n, axis=axis) for p, n in zip(parts, self.lengths)], axis
        )

    def join(self, parts, me, axis):
        odd, high = me % 2 == 1, me // 2 == 1
        picked = [
            jnp.where(
                high,
                jnp.where(odd, parts[3 ^ s], parts[2 ^ s]),
                jnp.where(odd, parts[1 ^ s], parts[s]),
            )
            for s in range(4)
        ]
        return self.lay(picked, axis)


def assemble(parts, shares, me):
    n, wide = parts[0].shape[0], parts[0].shape[2]

    def kernel(me_ref, *refs):
        o_ref, sems = refs[-2:]
        for act in ("start", "wait"):
            for m in range(4):
                for s in range(4):

                    @pl.when(me_ref[0] ^ m == s)
                    def move():
                        rows = pl.ds(0, shares.lengths[s])
                        to = pl.ds(shares.starts[s], shares.lengths[s])
                        pairs = [(refs[m].at[:, rows], o_ref.at[:, to])]
                        if m == 3 and len(parts) == 5:
                            low, high = pl.ds(0, n // 2), pl.ds(n // 2, n // 2)
                            pairs = [
                                (refs[3].at[:, rows], o_ref.at[low, to]),
                                (refs[4].at[:, rows], o_ref.at[high, to]),
                            ]
                        for k, (source, target) in enumerate(pairs):
                            copy = pltpu.make_async_copy(source, target, sems.at[m + k])
                            getattr(copy, act)()

    return pl.pallas_call(
        kernel,
        out_shape=jax.ShapeDtypeStruct((n, shares.rows, wide), parts[0].dtype),
        in_specs=[SM] + [ANY] * len(parts),
        out_specs=V,
        scratch_shapes=[pltpu.SemaphoreType.DMA((5,))],
        compiler_params=ROOM,
        cost_estimate=FREE,
    )(me, *parts)


def join_wide(parts, shares, me):
    wide = parts[0].shape[1]
    size = shares.size

    def kernel(me_ref, *refs):
        o_ref = refs[4]
        for m in range(4):
            for s in range(4):

                @pl.when(me_ref[0] ^ m == s)
                def move():
                    first, rows = shares.starts[s], shares.lengths[s]
                    held = refs[m][...].astype(F32)
                    for k in range(3):
                        cut = held[k * size : k * size + rows]
                        o_ref[k, first : first + rows, :] = cut

    return pl.pallas_call(
        kernel,
        out_shape=jax.ShapeDtypeStruct((3, shares.rows, wide), F32),
        in_specs=[SM] + [V] * 4,
        out_specs=V,
        compiler_params=ROOM,
        cost_estimate=FREE,
    )(me, *parts)


def small_sum(value, axes):
    for axis in axes:
        size = lax.axis_size(axis)
        if size & (size - 1):
            value = lax.psum(value, axis)
            continue
        bit = 1
        while bit < size:
            value = value + lax.ppermute(value, axis, [(i, i ^ bit) for i in range(size)])
            bit *= 2
    return value


def go_up(value, first, last):
    return lax.ppermute(value, "col", [(i, i + 1) for i in range(first, last + 1)])


def go_down(value, first, last):
    return lax.ppermute(value, "col", [(i, i - 1) for i in range(first, last + 1)])


def row_join(parts, axis):
    row = lax.axis_index("row")
    if len(parts) == 2:
        low = row == 0
        parts = [jnp.where(low, parts[0], parts[1]), jnp.where(low, parts[1], parts[0])]
    else:
        parts = ordered(parts, row, 1)
    return jnp.concatenate(parts, axis)


def swap_all(value):
    return [swap_with(value, 1), swap_with(value, 2), swap_with(value, 3)]


class Heads:
    def __init__(self, n_col, width, heads, blocks):
        self.size = n_col * width // heads
        self.firsts = [width * c // self.size for c in range(n_col)]
        lasts = [-(-width * (c + 1) // self.size) for c in range(n_col)]
        self.slots = max(b - a for a, b in zip(self.firsts, lasts))
        self.window = self.slots * self.size
        self.before = [width * c - f * self.size for c, f in enumerate(self.firsts)]
        self.after = [self.window - width - b for b in self.before]
        self.edge = max(self.before + self.after)
        full = (1 << blocks) - 1
        shares = {0: 0, 1: 2, 2: 9, 3: 13, 4: 15}

        def left_share(column):
            part = column % self.size
            return shares[round(4 * part / self.size)] if blocks == 4 else 0

        self.first_mask = [full & ~left_share(b) for b in self.before]
        self.last_mask = []
        for c, f in enumerate(self.firsts):
            end = width * (c + 1)
            begin = (f + self.slots - 1) * self.size
            if begin >= end:
                self.last_mask.append(0)
            elif begin + self.size <= end:
                self.last_mask.append(full)
            else:
                self.last_mask.append(left_share(end - begin))


def edges(value, axis, heads):
    n = lax.axis_size("col")
    edge, width = heads.edge, value.shape[axis]
    left = go_up(lax.slice_in_dim(value, width - edge, width, axis=axis), 0, n - 2)
    right = go_down(lax.slice_in_dim(value, 0, edge, axis=axis), 1, n - 1)
    return left, right


def widen(value, left, right, axis, heads, col):
    wide = jnp.concatenate([left, value, right], axis)
    before = jnp.array(heads.before, jnp.int32)[col]
    return lax.dynamic_slice_in_dim(wide, heads.edge - before, heads.window, axis)


def narrow_cuts(value, axis, heads, col, width):
    edge = heads.edge
    before = jnp.array(heads.before, jnp.int32)[col]
    shape = list(value.shape)
    shape[axis] = width + 2 * edge
    wide = lax.dynamic_update_slice_in_dim(
        jnp.zeros(shape, value.dtype), value, edge - before, axis
    )
    to_left = lax.slice_in_dim(wide, 0, edge, axis=axis)
    to_right = lax.slice_in_dim(wide, edge + width, width + 2 * edge, axis=axis)
    return wide, to_left, to_right


def narrow(wide, front, tail, axis, heads, width):
    edge = heads.edge
    pads = [(0, 0)] * wide.ndim
    pads[axis] = (0, width - edge)
    own = lax.slice_in_dim(wide, edge, edge + width, axis=axis).astype(F32)
    own = own + jnp.pad(front, pads).astype(F32)
    pads[axis] = (width - edge, 0)
    return own + jnp.pad(tail, pads).astype(F32)


def moments(values):
    mean = jnp.mean(values, axis=0, keepdims=True)
    centred = values - mean
    variance = jnp.mean(centred * centred, axis=0, keepdims=True)
    return mean, lax.rsqrt(variance + EPSILON)


def body(
    tokens,
    cotangent,
    w_qkv,
    q_bias,
    v_bias,
    w_out,
    out_bias,
    w_up,
    up_bias,
    w_down,
    down_bias,
    ln1_gain,
    ln1_bias,
    ln2_gain,
    ln2_bias,
    key_start,
):
    n_row, n_col = lax.axis_size("row"), lax.axis_size("col")
    row, col = lax.axis_index("row"), lax.axis_index("col")
    seqs, rows, width = tokens.shape
    length = seqs * rows
    depth = width * n_col
    part = length // n_col
    in_rows = w_up.shape[0]
    ff = w_up.shape[1]
    ff_rows = w_down.shape[0]
    ff_part = ff_rows // n_col
    heads = Heads(n_col, width, key_start.shape[0], rows * n_row // BLK)
    size, window = heads.size, heads.window
    firsts = jnp.array(heads.firsts, jnp.int32) * size
    begin = firsts[col]

    shares = Shares(width, 16)
    dp = lax.axis_index("dp")
    row_at = row[None].astype(jnp.int32)
    col_at = col[None].astype(jnp.int32)
    other_rows = [((row + i) % n_row)[None].astype(jnp.int32) for i in range(n_row)]


    x = tokens.reshape(length, width).T
    g = cotangent.reshape(length, width).T
    place_in = col * n_row + row
    half = n_col // 2

    def between_owners(value_of, steps, back):
        got = []
        for step in steps:
            pairs = []
            for r in range(n_row):
                for c in range(n_col):
                    to = r * n_col + (c - step) % n_col
                    here, there = r * n_col + c, (to % n_row) * n_col + to // n_row
                    pairs.append((there, here) if back else (here, there))
            got.append(lax.ppermute(value_of(step), ("row", "col"), pairs))
        return got

    x_all = lax.all_gather(x, "col", axis=0, tiled=True)
    wq = w_qkv.transpose(0, 2, 1)
    w3_own = widen(wq, *edges(wq, 1, heads), 1, heads, col)
    w3_parts = [w3_own] + [turn(w3_own, "row", -step) for step in range(1, n_row)]
    w3 = row_join(w3_parts, 2).reshape(3 * window, depth)
    params = jnp.stack([ln1_gain, ln1_bias, ln2_gain, ln2_bias, out_bias, q_bias, v_bias])
    params = [turn(params, "col", step) for step in range(n_col)]
    params = jnp.concatenate(ordered(params, col, -1), 1)
    gain1, shift1, gain2, shift2, bias_out, bias_q, bias_v = [p[:, None] for p in params]
    bias3 = jnp.concatenate(
        [
            lax.dynamic_slice_in_dim(bias_q, begin, window, 0),
            jnp.zeros((window, 1), F32),
            lax.dynamic_slice_in_dim(bias_v, begin, window, 0),
        ]
    )
    no_bias = jnp.zeros((depth, 1), F32)
    columns = jnp.concatenate([gain1, shift1, bias_out, gain2, shift2, no_bias], 1)
    meta = jnp.stack(
        [
            jnp.array(heads.firsts, jnp.int32)[col],
            row,
            jnp.array(heads.first_mask, jnp.int32)[col],
            jnp.array(heads.last_mask, jnp.int32)[col],
        ]
    )
    up_parts = [w_up] + [turn(w_up, "row", -step) for step in range(1, n_row)]
    up_turned = row_join(up_parts, 0).T
    out_own = shares.take(w_out.T, dp, 0)
    down_own = shares.take(w_down.T, dp, 0)
    x_all, g, out_own, down_own, w3, meta, columns, bias3 = gate(
        [x_all, g, out_own, down_own, w3, meta, columns, bias3], [up_turned]
    )

    g_all = lax.all_gather(g, "col", axis=0, tiled=True)
    moved_out = [out_own] + [turn(out_own, "col", -step) for step in range(1, n_col)]
    x_float = x_all.astype(F32)
    mean1, rstd1 = moments(x_float)
    n1 = ((x_float - mean1) * rstd1 * gain1 + shift1).astype(BF16)
    triple = product(w3, n1, bias3).reshape(3, window, length)
    triple, *rest = gate([triple] + moved_out[1:], [])
    moved_out = moved_out[:1] + rest

    pieces = [triple] + [turn(triple, "row", -step) for step in range(1, n_row)]
    moved_out = jnp.stack(ordered(moved_out, col, 1))
    moved_out, *rest = gate([moved_out] + pieces[1:], [])
    pieces = pieces[:1] + rest

    near_out = [swap_with(moved_out, 1), swap_with(moved_out, 2)]
    *cuts, mixed, norms = attn_fwd(meta, key_start, pieces, heads.slots, size)
    far_cuts = [near_out[0][:half], near_out[1][half:]]
    *cuts, near_x, near_y, far_x, far_y, down_own = gate(
        list(cuts) + near_out + far_cuts + [down_own], []
    )

    def move_down(step):
        return block(down_own, (col - step) % n_col, ff_part, 1)

    far_out = [swap_with(far_x, 2), swap_with(far_y, 1)]
    moved_down = between_owners(move_down, range(half), False)
    mixed_own = row_sum(cuts).astype(BF16)
    mixed_own, g_all, *rest = gate([mixed_own, g_all] + moved_down + far_out, [])
    moved_down, far_out = rest[:half], rest[half:]

    dp_at = dp[None].astype(jnp.int32)
    got = [
        turn(block(mixed_own, (col + step) % n_col, part, 1), "col", step) for step in range(n_col)
    ]
    out_weights = assemble([moved_out, near_x, near_y] + far_out, shares, dp_at)
    out_weights = [out_weights] + [turn(out_weights, "row", -step) for step in range(1, n_row)]
    x_part = block(x_all, col, part, 1)
    down_own, x_part, *rest = gate([down_own, x_part] + got[1:] + out_weights[1:], [])
    got = got[:1] + rest[: n_col - 1]
    out_weights = out_weights[:1] + rest[n_col - 1 :]
    out_weights = [w.reshape(depth, in_rows) for w in out_weights]

    moved_down = moved_down + between_owners(move_down, range(half, n_col), False)
    got = ordered(got, col, -1)
    lapped = [heads.firsts[j] * size for j in range(n_col)]
    attention = sum(
        jnp.pad(piece, ((at, depth - at - window), (0, 0))) for piece, at in zip(got, lapped)
    )
    resid, hat2, n2_own, rstd2 = mixed_norm(out_weights, attention, row_at, columns, x_part)
    moved_down = jnp.stack(ordered(moved_down, place_in, 1))
    n2_own, g, moved_down = gate([n2_own, g, moved_down], [])

    n2_all = lax.all_gather(n2_own, "col", axis=1, tiled=True)
    down_weights = assemble([moved_down] + swap_all(moved_down), shares, dp_at)
    down_weights = [turn(down_weights, "row", -step) for step in range(n_row)]
    down_weights = [w.reshape(depth, ff_part) for w in down_weights]
    down_turned = turned(down_weights)
    g_sums = jnp.sum(g.astype(F32), axis=1)
    n2_all, down_turned = gate([n2_all, down_turned], [g_sums])

    hidden_all, du_all, part2, du_sums = hidden_layer(
        up_turned, down_turned, n_row, up_bias[:, None], n2_all, g_all, row_at
    )
    part2, hidden_all, du_all = gate([part2, hidden_all, du_all], [])

    def relay_cut(value, far, cut, bit):
        return (cut.take(value, dp ^ (3 - bit), 1).astype(F32) + far.astype(F32)).astype(BF16)

    def share_sum(value, cut, near, relayed):
        own = cut.take(value, dp, 1).astype(F32)
        return (own + near.astype(F32) + relayed.astype(F32)).astype(BF16)

    def up_product(r):
        return token_product(n2_all, du_all, r, n_row, True)

    def down_product(r):
        return token_product(g_all, hidden_all, r, n_row, False).reshape(n_col, width, ff_part)

    dn2 = lax.psum_scatter(part2, "col", scatter_dimension=1, tiled=True)
    up_grad = [up_product(r) for r in other_rows[1:]]
    n2_all, hidden_all, *up_grad = gate([n2_all, hidden_all] + up_grad, [])

    up_grad = [turn(p, "row", i + 1) for i, p in enumerate(up_grad)]
    up_grad = [up_product(other_rows[0])] + up_grad
    down_grad = [down_product(r) for r in other_rows[1:]]
    hidden_all, *rest = gate([hidden_all] + up_grad + down_grad, [])
    up_grad, down_grad = rest[:n_row], rest[n_row:]
    up_rows = width if in_rows % width == 0 else in_rows
    up_shares, fine = Shares(up_rows, 8), Shares(width, 8)
    up_grad = sum(p.astype(F32) for p in up_grad).astype(BF16)
    up_grad = up_grad.reshape(in_rows // up_rows, up_rows, ff)
    up_far = up_shares.take(up_grad, dp ^ 3, 1)
    up_far, hidden_all, *down_grad = gate([up_far, hidden_all] + down_grad, [])

    up_far = swap_with(up_far, 1)
    down_grad = [turn(p, "row", i + 1) for i, p in enumerate(down_grad)]
    down_grad = [down_product(other_rows[0])] + down_grad
    hidden_all, *down_grad = gate([hidden_all] + down_grad, [])
    down_grad = sum(p.astype(F32) for p in down_grad).astype(BF16)
    down_far = fine.take(down_grad, dp ^ 3, 1)
    down_far, hidden_all = gate([down_far, hidden_all], [])

    down_far = swap_with(down_far, 2)
    up_near = up_shares.take(up_grad, dp ^ 1, 1)
    down_near = fine.take(down_grad, dp ^ 2, 1)
    du_row = du_sums[:, 0]
    shrunk = split_product(down_weights, hidden_all, row_at, columns, 5, BF16)
    own_sum = block(shrunk, col, part, 1).astype(F32) + resid
    shrunk = lax.dynamic_update_slice_in_dim(shrunk, own_sum.astype(BF16), col * part, 1)
    up_relay = relay_cut(up_grad, up_far, up_shares, 1)
    down_relay = relay_cut(down_grad, down_far, fine, 2)
    g_part = block(g_all, col, part, 1)
    dn2, shrunk, up_relay, down_relay, up_near, down_near, du_row, g_part = gate(
        [dn2, shrunk, up_relay, down_relay, up_near, down_near, du_row, g_part], []
    )

    up_near = swap_with(up_near, 1)
    down_near = swap_with(down_near, 2)
    dr, db, da, sums2 = mixed_norm_back(out_weights, dn2, hat2, rstd2, g_part, row_at, columns)
    early = jnp.concatenate([sums2.T.reshape(-1), du_row, g_sums])
    da_cuts = [
        lax.dynamic_slice_in_dim(da, firsts[(col + step) % n_col], window, 0)
        for step in range(n_col)
    ]
    db, shrunk, up_near, down_near, up_relay, down_relay, *da_cuts = gate(
        [db, shrunk, up_near, down_near, up_relay, down_relay] + da_cuts, []
    )

    got = [turn(cut, "col", step) for step, cut in enumerate(da_cuts)]
    up_relay = swap_with(up_relay, 2)
    down_relay = swap_with(down_relay, 1)
    out_grad = [token_product(db, attention, r, n_row, False) for r in other_rows[::-1]][::-1]
    out_grad = [o.reshape(n_col, width, in_rows) for o in out_grad]
    rest = gate(got[1:] + out_grad + [up_relay, down_relay, shrunk], [])
    got, rest = got[:1] + rest[: n_col - 1], rest[n_col - 1 :]
    out_grad, (up_relay, down_relay, shrunk) = rest[:n_row], rest[n_row:]

    outputs = lax.psum_scatter(shrunk, "col", scatter_dimension=0, tiled=True)
    da_own = jnp.concatenate(ordered(got, col, -1), 1)
    da_pieces = [da_own] + [turn(da_own, "row", -step) for step in range(1, n_row)]
    out_grad = row_sum(out_grad).astype(BF16)
    up_share = share_sum(up_grad, up_shares, up_near, up_relay)
    down_share = share_sum(down_grad, fine, down_near, down_relay)
    out_sent = jnp.stack([fine.take(out_grad, dp ^ 1, 1), fine.take(out_grad, dp ^ 3, 1)])
    *rest, out_sent, up_share, down_share = gate(
        da_pieces[1:] + [out_sent, up_share, down_share], []
    )
    da_pieces = [da_own] + rest

    out_first = swap_with(out_sent, 1)
    up_y = swap_with(up_share, 2)

    def move_home(step):
        return pick(down_share, (place_in + step) % n_col)

    down_home = between_owners(move_home, range(half), True)
    dqkv = attn_bwd(meta, key_start, pieces, da_pieces, mixed, norms, heads.slots, size)
    *rest, out_first, up_y, up_share, down_share = gate(
        list(dqkv) + down_home + [out_first, up_y, up_share, down_share], []
    )
    dqkv, down_home = rest[:n_row], rest[n_row:]
    out_near, out_far = out_first[0], out_first[1]
    out_relay = relay_cut(out_grad, out_far, fine, 1)

    out_relay = swap_with(out_relay, 2)
    up_x = swap_with(up_share, 1)
    down_home = down_home + between_owners(move_home, range(half, n_col), True)
    dqkv = row_sum(dqkv).astype(BF16).reshape(3 * window, length)
    out_near, out_grad, *down_home = gate([out_near, out_grad] + down_home, [dqkv])
    homes = jnp.stack(ordered(down_home, col, -1))
    out_share = share_sum(out_grad, fine, out_near, out_relay)
    qkv_parts = [
        token_product(dqkv, n1, r, n_row, False).reshape(3, window, in_rows)
        for r in other_rows[:0:-1]
    ][::-1]
    dqkv, homes, outputs, up_x, out_share, *qkv_parts = gate(
        [dqkv, homes, outputs, up_x, out_share] + qkv_parts, []
    )

    homes_near = [swap_with(homes, 1), swap_with(homes, 2)]
    own = token_product(dqkv, n1, other_rows[0], n_row, False).reshape(3, window, in_rows)
    qkv_grad = row_sum([own] + qkv_parts).astype(BF16)
    wide, to_left, to_right = narrow_cuts(qkv_grad, 1, heads, col, width)
    dqkv, wide, to_left, to_right, out_share, up_y, *homes_near = gate(
        [dqkv, wide, to_left, to_right, out_share, up_y] + homes_near, []
    )

    out_home = lax.psum_scatter(out_share, "col", scatter_dimension=0, tiled=True)
    tail, front = go_down(to_left, 1, n_col - 1), go_up(to_right, 0, n_col - 2)
    homes_far = swap_with(homes_near[1], 1)
    up_far = swap_with(up_x, 2)
    dn1, norm1 = norm_product_tn(w3, dqkv, n1, columns, rstd1, dr, col_at, n_col)
    qkv_grad = narrow(wide, front, tail, 1, heads, width).astype(BF16)
    qkv_sent = [fine.take(qkv_grad, dp ^ m, 1) for m in (1, 2, 3)]
    dn1, dqkv, homes_far, up_far, out_home, *qkv_sent = gate(
        [dn1, dqkv, homes_far, up_far, out_home] + qkv_sent, [norm1]
    )

    dx = lax.psum_scatter(dn1, "col", scatter_dimension=0, tiled=True)
    qkv_got = [swap_with(v, m) for v, m in zip(qkv_sent, (1, 2, 3))]
    out_all = [swap_with(out_home, 1), swap_with(out_home, 2)]
    homes, homes_far, norm1, outputs, dqkv = gate(
        [homes, homes_far, norm1, outputs, dqkv], qkv_sent
    )
    homes = fine.join([homes] + homes_near + [homes_far], dp, 1).astype(F32)
    down_grad = jnp.concatenate([homes[j] for j in range(n_col)], 1)
    outputs = (outputs.astype(F32) + down_bias[:, None]).astype(BF16)
    dq_dv = jnp.sum(dqkv.astype(F32), axis=1).reshape(3, window)
    sums = lax.dynamic_update_slice_in_dim(jnp.zeros((2, depth), F32), dq_dv[::2], begin, 1)
    small = jnp.concatenate([sums.reshape(-1), norm1.T.reshape(-1), early])[None]
    small = small_sum(small, ("row",))[0]
    sums, local = small[: 7 * depth].reshape(7, depth), small[7 * depth :]
    sums = small_sum(sums, ("col",))
    sums = lax.dynamic_slice_in_dim(sums, col * width, width, 1)
    small = jnp.concatenate([sums.reshape(-1), local])
    deep = -(-small.shape[0] // in_rows)
    small = jnp.pad(small, (0, deep * in_rows - small.shape[0])).reshape(deep, in_rows)
    rounded = lax.reduce_precision(small, 8, 7)
    rest = (small - rounded).astype(BF16)
    rounded = rounded.astype(BF16)
    qkv_share = fine.take(qkv_grad, dp, 1).astype(F32)
    qkv_share = (qkv_share + sum(q.astype(F32) for q in qkv_got)).astype(BF16)
    ends = 3 * fine.size
    payload = jnp.concatenate([qkv_share.reshape(ends, in_rows), rounded, rest])
    up_far, payload, *out_all = gate([up_far, payload] + out_all, [down_grad, outputs])

    qkv_all = swap_all(payload)
    out_all.append(swap_with(out_all[0], 2))
    up_grad = up_shares.join([up_share, up_x, up_y, up_far], dp, 1).astype(F32)
    up_grad = up_grad.reshape(in_rows, ff)
    hat1 = (x.astype(F32) - mean1) * rstd1
    dx = dx.reshape(width + 16, length)
    lines = dx[width : width + 4].astype(F32)
    lines = (lines[0::2] + lines[1::2]) / depth
    input_grad = dx[:width].astype(F32) - rstd1 * (lines[0:1] + hat1 * lines[1:2])
    input_grad = input_grad.astype(BF16)
    *out_all, a, b, c = gate(out_all + qkv_all, [up_grad, input_grad])

    out_grad = fine.join([out_home] + out_all, dp, 1).astype(F32)[0]
    small = sum(v[ends:].astype(F32) for v in (payload, a, b, c))
    small = (small[:deep] + small[deep:]).reshape(-1)
    sums, local = small[: 7 * width].reshape(7, width), small[7 * width : 8 * width + ff]
    qkv_grad = join_wide([payload, a, b, c], fine, dp[None].astype(jnp.int32))
    return (
        outputs.T.reshape(tokens.shape),
        input_grad.T.reshape(tokens.shape),
        qkv_grad.transpose(0, 2, 1),
        sums[0],
        sums[1],
        out_grad.T,
        sums[4],
        up_grad,
        local[:ff],
        down_grad.T,
        local[ff:],
        sums[2],
        sums[3],
        sums[5],
        sums[6],
    )


def solution(mesh):
    inputs = (
        P("dp", "row", "col"),
        P("dp", "row", "col"),
        P(None, "row", "col"),
        P("col"),
        P("col"),
        P("row", "col"),
        P("col"),
        P("row", "col"),
        P("col"),
        P("row", "col"),
        P("col"),
        P("col"),
        P("col"),
        P("col"),
        P("col"),
        P(),
    )
    return jax.shard_map(
        body, mesh=mesh, in_specs=inputs, out_specs=inputs[:15], check_vma=False
    )
```

```python
import functools

import jax
import jax.numpy as jnp
from jax import lax
from jax.experimental import pallas as pl
from jax.experimental.pallas import tpu as pltpu
from jax.sharding import PartitionSpec as P

BLK = 512
EPSILON = 1e-05
LOG2E = 1.4426950408889634
BF16 = jnp.bfloat16
F32 = jnp.float32

FREE = pl.CostEstimate(flops=0, bytes_accessed=0, transcendentals=0)
ROOM = pltpu.CompilerParams(vmem_limit_bytes=56 * 2**20)

NT=(((0,),(0,)),((),()))
TN=(((1,),(1,)),((),()))

def plan_tiles(meta, ks, own, load, n_slots, n_blocks, n_row, n_heads):
    for i in range(n_row): load[i]=0
    def level(lv,_):
        cost=n_blocks-lv
        def tile(t,_):
            slot=t//n_blocks; qb=t%n_blocks
            head=meta[0]+slot
            here=head<n_heads
            hd=jnp.minimum(head,n_heads-1)
            n=qb+1-ks[hd,qb]
            mask=jnp.where(slot==0,meta[2],jnp.where(slot==n_slots-1,meta[3],(1<<n_blocks)-1))
            here=jnp.logical_and(here,((mask>>qb)&1)==1)
            @pl.when(cost==n_blocks)
            def _(): own[t]=-1
            @pl.when(jnp.logical_and(here,n==cost))
            def _():
                best=load[0]; who=jnp.int32(0)
                for i in range(1,n_row):
                    less=load[i]<best
                    best=jnp.where(less,load[i],best); who=jnp.where(less,i,who)
                own[t]=who
                load[who]=best+cost
            return 0
        lax.fori_loop(0,n_slots*n_blocks,tile,0)
        return 0
    lax.fori_loop(0,n_blocks,level,0)

def fetch(pieces, whole, sems, row, n_row, width):
    copies=[]
    for i,p in enumerate(pieces):
        at=lax.rem(row+i,n_row)*width
        c=pltpu.make_async_copy(p, whole.at[...,pl.ds(pl.multiple_of(at,width),width)], sems.at[i])
        c.start(); copies.append(c)
    return copies

def fwd_kernel(n_row,n_slots,hd,n_heads,meta,ks,*refs):
    pieces=refs[:n_row]; cuts=refs[n_row:2*n_row]; o_ref,lse_ref,whole,own,load,sems=refs[2*n_row:]
    S=whole.shape[2]; nb=S//BLK; width=S//n_row
    row=meta[1]
    copies=fetch(pieces,whole,sems,row,n_row,width)
    plan_tiles(meta,ks,own,load,n_slots,nb,n_row,n_heads)
    o_ref[...]=jnp.zeros_like(o_ref)
    for c in copies: c.wait()
    c2=hd**-0.5*LOG2E
    diag=lax.broadcasted_iota(jnp.int32,(BLK,BLK),0)<=lax.broadcasted_iota(jnp.int32,(BLK,BLK),1)
    def tile(t,_):
        @pl.when(own[t]==row)
        def _():
            slot=t//nb; qb=t%nb
            first=ks[meta[0]+slot,qb]
            hs=pl.ds(pl.multiple_of(slot*hd,hd),hd)
            qs=pl.ds(pl.multiple_of(qb*BLK,BLK),BLK)
            q=whole[0,hs,qs]
            def scores(kb_ds):
                return lax.dot_general(whole[1,hs,kb_ds],q,NT,preferred_element_type=jnp.float32)
            s=jnp.where(diag,scores(qs),-1e30)
            m=jnp.max(s,axis=0,keepdims=True)
            p=jnp.exp2((s-m)*c2)
            l=jnp.sum(p,axis=0,keepdims=True)
            acc=jnp.dot(whole[2,hs,qs],p.astype(jnp.bfloat16),preferred_element_type=jnp.float32)
            def step(kb,carry):
                m,l,acc=carry
                kd=pl.ds(pl.multiple_of(kb*BLK,BLK),BLK)
                s=scores(kd)
                mn=jnp.maximum(m,jnp.max(s,axis=0,keepdims=True))
                a=jnp.exp2((m-mn)*c2)
                p=jnp.exp2((s-mn)*c2)
                l=l*a+jnp.sum(p,axis=0,keepdims=True)
                acc=acc*a+jnp.dot(whole[2,hs,kd],p.astype(jnp.bfloat16),preferred_element_type=jnp.float32)
                return mn,l,acc
            m,l,acc=lax.fori_loop(first,qb,step,(m,l,acc))
            o_ref[hs,qs]=(acc/l).astype(jnp.bfloat16)
            lse_ref[pl.ds(slot,1),qs]=m*c2+jnp.log2(l)
        return 0
    lax.fori_loop(0,n_slots*nb,tile,0)
    for i,cut in enumerate(cuts):
        cut[...]=o_ref[:,pl.ds(pl.multiple_of(lax.rem(row+i,n_row)*width,width),width)]

def bwd_kernel(n_row,n_slots,hd,n_heads,meta,ks,*refs):
    pieces=refs[:n_row]; das=refs[n_row:2*n_row]
    o_ref,lse_ref=refs[2*n_row:2*n_row+2]; cuts=refs[2*n_row+2:3*n_row+2]
    d_ref,whole,da,acc,own,load,sems,sems2=refs[3*n_row+2:]
    S=whole.shape[2]; nb=S//BLK; width=S//n_row
    row=meta[1]
    copies=fetch(pieces,whole,sems,row,n_row,width)+fetch(das,da,sems2,row,n_row,width)
    plan_tiles(meta,ks,own,load,n_slots,nb,n_row,n_heads)
    d_ref[...]=jnp.zeros_like(d_ref)
    acc[...]=jnp.zeros_like(acc)
    for c in copies: c.wait()
    scale=hd**-0.5; c2=scale*LOG2E
    diag=lax.broadcasted_iota(jnp.int32,(BLK,BLK),0)<=lax.broadcasted_iota(jnp.int32,(BLK,BLK),1)
    def tile(t,_):
        @pl.when(own[t]==row)
        def _():
            slot=t//nb; qb=t%nb
            first=ks[meta[0]+slot,qb]
            hs=pl.ds(pl.multiple_of(slot*hd,hd),hd)
            qs=pl.ds(pl.multiple_of(qb*BLK,BLK),BLK)
            q=whole[0,hs,qs]
            up=da[hs,qs]
            lse=lse_ref[pl.ds(slot,1),qs]
            delta=jnp.sum(up.astype(jnp.float32)*o_ref[hs,qs].astype(jnp.float32),axis=0,keepdims=True)
            def block(kd,masked):
                k=whole[1,hs,kd]
                s=lax.dot_general(k,q,NT,preferred_element_type=jnp.float32)
                p=jnp.exp2(s*c2-lse)
                if masked: p=jnp.where(diag,p,0.0)
                dp=lax.dot_general(whole[2,hs,kd],up,NT,preferred_element_type=jnp.float32)
                ds=(p*(dp-delta)).astype(jnp.bfloat16)
                acc[1,hs,kd]+=lax.dot_general(up,p.astype(jnp.bfloat16),TN,preferred_element_type=jnp.float32)
                acc[0,hs,kd]+=lax.dot_general(q,ds,TN,preferred_element_type=jnp.float32)
                return jnp.dot(k,ds,preferred_element_type=jnp.float32)
            dq=block(qs,True)
            dq=lax.fori_loop(first,qb,lambda kb,dq:dq+block(pl.ds(pl.multiple_of(kb*BLK,BLK),BLK),False),dq)
            d_ref[hs,qs]=(dq*scale).astype(jnp.bfloat16)
        return 0
    lax.fori_loop(0,n_slots*nb,tile,0)
    for i,cut in enumerate(cuts):
        at=pl.ds(pl.multiple_of(lax.rem(row+i,n_row)*width,width),width)
        cut[0]=d_ref[:,at]
        cut[1]=(acc[0,:,at]*scale).astype(jnp.bfloat16)
        cut[2]=acc[1,:,at].astype(jnp.bfloat16)

V=pl.BlockSpec(memory_space=pltpu.VMEM); SM=pl.BlockSpec(memory_space=pltpu.SMEM); ANY=pl.BlockSpec(memory_space=pl.ANY)
def attn_fwd(meta,ks,pieces,n_slots,hd):
    n_row=len(pieces); _,H,T=pieces[0].shape; S=T*n_row; nb=S//BLK
    return pl.pallas_call(functools.partial(fwd_kernel,n_row,n_slots,hd,ks.shape[0]),
      out_shape=[jax.ShapeDtypeStruct((H,T),jnp.bfloat16)]*n_row+[jax.ShapeDtypeStruct((H,S),jnp.bfloat16),jax.ShapeDtypeStruct((n_slots,S),jnp.float32)],
      in_specs=[SM,SM]+[ANY]*n_row,out_specs=[V]*(n_row+2),
      scratch_shapes=[pltpu.VMEM((3,H,S),jnp.bfloat16),pltpu.SMEM((n_slots*nb,),jnp.int32),pltpu.SMEM((n_row,),jnp.int32),pltpu.SemaphoreType.DMA((n_row,))],
      compiler_params=pltpu.CompilerParams(vmem_limit_bytes=48*2**20),
      cost_estimate=FREE,
    )(meta,ks,*pieces)
def attn_bwd(meta,ks,pieces,das,o,lse,n_slots,hd):
    n_row=len(pieces); _,H,T=pieces[0].shape; S=T*n_row; nb=S//BLK
    return pl.pallas_call(functools.partial(bwd_kernel,n_row,n_slots,hd,ks.shape[0]),
      out_shape=[jax.ShapeDtypeStruct((3,H,T),jnp.bfloat16)]*n_row,
      in_specs=[SM,SM]+[ANY]*(2*n_row)+[V,V],out_specs=[V]*n_row,
      scratch_shapes=[pltpu.VMEM((H,S),jnp.bfloat16),pltpu.VMEM((3,H,S),jnp.bfloat16),pltpu.VMEM((H,S),jnp.bfloat16),pltpu.VMEM((2,H,S),jnp.float32),pltpu.SMEM((n_slots*nb,),jnp.int32),pltpu.SMEM((n_row,),jnp.int32),pltpu.SemaphoreType.DMA((n_row,)),pltpu.SemaphoreType.DMA((n_row,))],
      compiler_params=pltpu.CompilerParams(vmem_limit_bytes=56*2**20),
      cost_estimate=FREE,
    )(meta,ks,*pieces,*das,o,lse)


def rows_of(total, most):
    for rows in range(min(total, most) // 16 * 16, 0, -16):
        if total % rows == 0:
            return rows
    return total


def by_rows(i, *refs):
    return (i, 0)


def whole_block(i, *refs):
    return (0, 0)


def product_kernel(a_ref, b_ref, bias_ref, o_ref):
    o_ref[...] = (
        jnp.dot(a_ref[...], b_ref[...], preferred_element_type=F32) + bias_ref[...]
    ).astype(o_ref.dtype)


def product(a, b, bias):
    rows = rows_of(a.shape[0], 448)
    return pl.pallas_call(
        product_kernel,
        out_shape=jax.ShapeDtypeStruct((a.shape[0], b.shape[1]), BF16),
        grid=(a.shape[0] // rows,),
        in_specs=[
            pl.BlockSpec((rows, a.shape[1]), by_rows),
            pl.BlockSpec(b.shape, whole_block),
            pl.BlockSpec((rows, 1), by_rows),
        ],
        out_specs=pl.BlockSpec((rows, b.shape[1]), by_rows),
        compiler_params=ROOM,
        cost_estimate=FREE,
    )(a, b, bias)


def split_product(parts, b, row, columns, which, dtype):
    n = len(parts)
    total, depth = parts[0].shape
    width = b.shape[1]
    rows = rows_of(total, 400)

    def kernel(row_ref, b_ref, bias_ref, *refs):
        out = bias_ref[:, which : which + 1] + jnp.zeros((rows, width), F32)
        for i in range(n):
            at = pl.multiple_of(lax.rem(row_ref[0] + i, n) * depth, 8)
            out = out + jnp.dot(refs[i][...], b_ref[pl.ds(at, depth), :], preferred_element_type=F32)
        refs[n][...] = out.astype(dtype)

    return pl.pallas_call(
        kernel,
        out_shape=jax.ShapeDtypeStruct((total, width), dtype),
        grid=(total // rows,),
        in_specs=[
            SM,
            pl.BlockSpec(b.shape, whole_block),
            pl.BlockSpec((rows, columns.shape[1]), by_rows),
        ]
        + [pl.BlockSpec((rows, depth), by_rows)] * n,
        out_specs=pl.BlockSpec((rows, width), by_rows),
        compiler_params=ROOM,
        cost_estimate=FREE,
    )(row, b, columns, *parts)


def mixed_norm(parts, b, row, columns, x):
    n = len(parts)
    total, depth = parts[0].shape
    width = b.shape[1]
    rows = rows_of(total, 400)
    steps = total // rows

    def kernel(row_ref, b_ref, c_ref, x_ref, *refs):
        o_ref, hat_ref, norm_ref, scale_ref = refs[n:]
        step = pl.program_id(0)
        at = pl.ds(pl.multiple_of(step * rows, 8), rows)
        out = c_ref[at, 2:3] + x_ref[...].astype(F32)
        for i in range(n):
            here = pl.multiple_of(lax.rem(row_ref[0] + i, n) * depth, 8)
            out = out + jnp.dot(
                refs[i][...], b_ref[pl.ds(here, depth), :], preferred_element_type=F32
            )
        o_ref[at, :] = out

        @pl.when(step == steps - 1)
        def end():
            mean = jnp.sum(o_ref[...], axis=0, keepdims=True) / total
            centred = o_ref[...] - mean
            scale = lax.rsqrt(jnp.sum(centred * centred, axis=0, keepdims=True) / total + EPSILON)
            hat = centred * scale
            hat_ref[...] = hat
            norm_ref[...] = (hat * c_ref[:, 3:4] + c_ref[:, 4:5]).astype(BF16)
            scale_ref[...] = scale

    return pl.pallas_call(
        kernel,
        out_shape=[
            jax.ShapeDtypeStruct((total, width), F32),
            jax.ShapeDtypeStruct((total, width), F32),
            jax.ShapeDtypeStruct((total, width), BF16),
            jax.ShapeDtypeStruct((1, width), F32),
        ],
        grid=(steps,),
        in_specs=[
            SM,
            pl.BlockSpec(b.shape, whole_block),
            pl.BlockSpec(columns.shape, whole_block),
            pl.BlockSpec((rows, width), by_rows),
        ]
        + [pl.BlockSpec((rows, depth), by_rows)] * n,
        out_specs=[
            pl.BlockSpec((total, width), whole_block),
            pl.BlockSpec((total, width), whole_block),
            pl.BlockSpec((total, width), whole_block),
            pl.BlockSpec((1, width), whole_block),
        ],
        compiler_params=ROOM,
        cost_estimate=FREE,
    )(row, b, columns, x, *parts)


def mixed_norm_back(parts, dn, hat, scale, g, row, columns):
    n = len(parts)
    depth = parts[0].shape[1]
    total, width = dn.shape
    rows = rows_of(total, 400)
    steps = total // rows

    def kernel(row_ref, dn_ref, hat_ref, scale_ref, g_ref, c_ref, *refs):
        o_ref, low_ref, a_ref, s_ref, acc = refs[n:]
        step = pl.program_id(0)

        @pl.when(step == 0)
        def start():
            grad = dn_ref[...].astype(F32)
            up = grad * c_ref[:, 3:4]
            hat = hat_ref[...]
            pull = jnp.sum(up, axis=0, keepdims=True) / total
            lean = jnp.sum(up * hat, axis=0, keepdims=True) / total
            out = g_ref[...].astype(F32) + scale_ref[...] * (up - pull - hat * lean)
            low = out.astype(BF16)
            o_ref[...] = out
            low_ref[...] = low
            s_ref[:, 0:1] = jnp.sum(low.astype(F32), axis=1, keepdims=True)
            s_ref[:, 1:2] = jnp.sum(grad * hat, axis=1, keepdims=True)
            s_ref[:, 2:3] = jnp.sum(grad, axis=1, keepdims=True)
            acc[...] = jnp.zeros_like(acc)

        cut = low_ref[pl.ds(pl.multiple_of(step * rows, 8), rows), :]
        for i in range(n):
            here = pl.ds(pl.multiple_of(lax.rem(row_ref[0] + i, n) * depth, 8), depth)
            acc[here, :] += lax.dot_general(refs[i][...], cut, NT, preferred_element_type=F32)

        @pl.when(step == steps - 1)
        def end():
            a_ref[...] = acc[...].astype(BF16)

    full = pl.BlockSpec((total, width), whole_block)
    return pl.pallas_call(
        kernel,
        out_shape=[
            jax.ShapeDtypeStruct((total, width), F32),
            jax.ShapeDtypeStruct((total, width), BF16),
            jax.ShapeDtypeStruct((n * depth, width), BF16),
            jax.ShapeDtypeStruct((total, 3), F32),
        ],
        grid=(steps,),
        in_specs=[
            SM,
            full,
            full,
            pl.BlockSpec((1, width), whole_block),
            full,
            pl.BlockSpec(columns.shape, whole_block),
        ]
        + [pl.BlockSpec((rows, depth), by_rows)] * n,
        out_specs=[
            full,
            full,
            pl.BlockSpec((n * depth, width), whole_block),
            pl.BlockSpec((total, 3), whole_block),
        ],
        scratch_shapes=[pltpu.VMEM((n * depth, width), F32)],
        compiler_params=ROOM,
        cost_estimate=FREE,
    )(row, dn, hat, scale, g, columns, *parts)


def norm_product_tn(a, b, normed, columns, scale, riding, col, n_col):
    rows = rows_of(a.shape[0], 448)
    steps = a.shape[0] // rows
    depth, tokens = a.shape[1], b.shape[1]
    cut, part = depth // n_col, tokens // n_col

    def kernel(col_ref, a_ref, b_ref, n_ref, g_ref, c_ref, r_ref, o_ref, f_ref, acc):
        @pl.when(pl.program_id(0) == 0)
        def start():
            acc[...] = lax.dot_general(a_ref[...], b_ref[...], NT, preferred_element_type=F32)

        @pl.when(pl.program_id(0) > 0)
        def more():
            acc[...] += lax.dot_general(a_ref[...], b_ref[...], NT, preferred_element_type=F32)

        @pl.when(pl.program_id(0) == steps - 1)
        def end():
            first = jnp.zeros((1, tokens), F32)
            second = jnp.zeros((1, tokens), F32)
            for j in range(n_col):
                at = pl.ds(j * cut, cut)
                p = acc[at, :]
                scaled = p * g_ref[at, 0:1]
                o_ref[j, 0:cut, :] = (scaled * c_ref[...]).astype(BF16)
                moved = p * (n_ref[at, :].astype(F32) - g_ref[at, 1:2])
                first += jnp.sum(scaled, axis=0, keepdims=True)
                second += jnp.sum(moved, axis=0, keepdims=True)
                f_ref[at, 0:1] = jnp.sum(moved, axis=1, keepdims=True) / g_ref[at, 0:1]
                f_ref[at, 1:2] = jnp.sum(p, axis=1, keepdims=True)
                for c in range(n_col):

                    @pl.when(col_ref[0] == c)
                    def ride():
                        here = slice(c * part, (c + 1) * part)
                        own = scaled[:, here] * c_ref[:, here] + r_ref[at, :]
                        o_ref[j, 0:cut, here] = own.astype(BF16)

            lines = []
            for line in (first, second):
                high = line.astype(BF16).astype(F32)
                lines += [high, line - high]
            lines = jnp.concatenate(lines + [jnp.zeros((12, tokens), F32)]).astype(BF16)
            for j in range(n_col):
                o_ref[j, cut : cut + 16, :] = lines

    return pl.pallas_call(
        kernel,
        out_shape=[
            jax.ShapeDtypeStruct((n_col, cut + 16, tokens), BF16),
            jax.ShapeDtypeStruct((depth, 2), F32),
        ],
        grid=(steps,),
        in_specs=[
            SM,
            pl.BlockSpec((rows, depth), by_rows),
            pl.BlockSpec((rows, tokens), by_rows),
            pl.BlockSpec((depth, tokens), whole_block),
            pl.BlockSpec(columns.shape, whole_block),
            pl.BlockSpec((1, tokens), whole_block),
            pl.BlockSpec((depth, part), whole_block),
        ],
        out_specs=[
            pl.BlockSpec((n_col, cut + 16, tokens), lambda i: (0, 0, 0)),
            pl.BlockSpec((depth, 2), whole_block),
        ],
        scratch_shapes=[pltpu.VMEM((depth, tokens), F32)],
        compiler_params=ROOM,
        cost_estimate=FREE,
    )(col, a, b, normed, columns, scale, riding)


def token_product(a, b, index, parts, of_a):
    rows_a = a.shape[0] // (parts if of_a else 1)
    rows_b = b.shape[0] // (1 if of_a else parts)
    rows = rows_of(rows_a, 448)
    steps = rows_a // rows

    def kernel(index_ref, a_ref, b_ref, o_ref):
        o_ref[...] = lax.dot_general(
            a_ref[...], b_ref[...], TN, preferred_element_type=F32
        ).astype(BF16)

    if of_a:
        a_map, b_map = (lambda i, r: (r[0] * steps + i, 0)), whole_block
    else:
        a_map, b_map = by_rows, (lambda i, r: (r[0], 0))
    return pl.pallas_call(
        kernel,
        out_shape=jax.ShapeDtypeStruct((rows_a, rows_b), BF16),
        grid_spec=pltpu.PrefetchScalarGridSpec(
            num_scalar_prefetch=1,
            grid=(steps,),
            in_specs=[
                pl.BlockSpec((rows, a.shape[1]), a_map),
                pl.BlockSpec((rows_b, b.shape[1]), b_map),
            ],
            out_specs=pl.BlockSpec((rows, rows_b), by_rows),
        ),
        compiler_params=ROOM,
        cost_estimate=FREE,
    )(index, a, b)


def gelu_parts(u):
    inner = 0.7978845608 * (u + 0.044715 * u * u * u)
    t = jnp.tanh(inner)
    value = 0.5 * u * (1.0 + t)
    slope = 0.5 * (1.0 + t) + 0.5 * u * (1.0 - t * t) * 0.7978845608 * (1.0 + 0.134145 * u * u)
    return value, slope


def hidden_layer(up, down, n, bias, n2, g, row):
    ff, depth = up.shape
    tokens = n2.shape[1]
    rows = rows_of(ff // n, 400)
    cuts = ff // n // rows
    steps = ff // rows

    def kernel(row_ref, up_ref, down_ref, bias_ref, n_ref, g_ref, h_ref, d_ref, p_ref, s_ref, acc):
        step = pl.program_id(0)
        u = jnp.dot(up_ref[...], n_ref[...], preferred_element_type=F32) + bias_ref[...]
        value, slope = gelu_parts(u)
        h_ref[...] = value.astype(BF16)
        dh = jnp.dot(down_ref[...], g_ref[...], preferred_element_type=F32)
        du = (dh * slope).astype(BF16)
        d_ref[...] = du
        s_ref[...] = jnp.sum(du.astype(F32), axis=1, keepdims=True)

        @pl.when(step == 0)
        def start():
            acc[...] = lax.dot_general(up_ref[...], du, NT, preferred_element_type=F32)

        @pl.when(step > 0)
        def more():
            acc[...] += lax.dot_general(up_ref[...], du, NT, preferred_element_type=F32)

        @pl.when(step == steps - 1)
        def end():
            p_ref[...] = acc[...].astype(BF16)

    mine = lambda i, r: (lax.rem(r[0] * cuts + i, steps), 0)
    full = lambda i, r: (0, 0)
    return pl.pallas_call(
        kernel,
        out_shape=[
            jax.ShapeDtypeStruct((ff, tokens), BF16),
            jax.ShapeDtypeStruct((ff, tokens), BF16),
            jax.ShapeDtypeStruct((depth, tokens), BF16),
            jax.ShapeDtypeStruct((ff, 1), F32),
        ],
        grid_spec=pltpu.PrefetchScalarGridSpec(
            num_scalar_prefetch=1,
            grid=(steps,),
            in_specs=[
                pl.BlockSpec((rows, depth), mine),
                pl.BlockSpec((rows, depth), lambda i, r: (i, 0)),
                pl.BlockSpec((rows, 1), mine),
                pl.BlockSpec((depth, tokens), full),
                pl.BlockSpec((depth, tokens), full),
            ],
            out_specs=[
                pl.BlockSpec((rows, tokens), mine),
                pl.BlockSpec((rows, tokens), mine),
                pl.BlockSpec((depth, tokens), full),
                pl.BlockSpec((rows, 1), mine),
            ],
            scratch_shapes=[pltpu.VMEM((depth, tokens), F32)],
        ),
        compiler_params=ROOM,
        cost_estimate=FREE,
    )(row, up, down, bias, n2, g)


def turned(parts):
    n = len(parts)
    depth, wide = parts[0].shape

    def kernel(*refs):
        o_ref = refs[n]
        for i in range(n):
            for first in range(0, wide, 256):
                size = min(256, wide - first)
                at = lax.broadcasted_iota(jnp.int32, (size, size), 0)
                ones = (at == lax.broadcasted_iota(jnp.int32, (size, size), 1)).astype(BF16)
                cut = refs[i][:, first : first + size]
                out = lax.dot_general(ones, cut, TN, preferred_element_type=F32)
                o_ref[i * wide + first : i * wide + first + size, :] = out.astype(BF16)

    return pl.pallas_call(
        kernel,
        out_shape=jax.ShapeDtypeStruct((n * wide, depth), BF16),
        in_specs=[V] * n,
        out_specs=V,
        compiler_params=ROOM,
        cost_estimate=FREE,
    )(*parts)


def gate(values, others):
    def kernel(*refs):
        pass

    out = pl.pallas_call(
        kernel,
        out_shape=[jax.ShapeDtypeStruct(v.shape, v.dtype) for v in values],
        in_specs=[ANY] * (len(values) + len(others)),
        out_specs=[ANY] * len(values),
        input_output_aliases={i: i for i in range(len(values))},
        cost_estimate=FREE,
    )(*values, *others)
    return list(out)


def turn(value, axis, steps):
    size = lax.axis_size(axis)
    if steps % size == 0:
        return value
    return lax.ppermute(value, axis, [(i, (i + steps) % size) for i in range(size)])


def block(value, index, size, axis):
    return lax.dynamic_slice_in_dim(value, index * size, size, axis)


def row_sum(parts):
    total = parts[0].astype(F32)
    for step in range(1, len(parts)):
        total = total + turn(parts[step], "row", step).astype(F32)
    return total


def swap_with(value, bit):
    return lax.ppermute(value, "dp", [(i, i ^ bit) for i in range(4)])


def pick(value, index, axis=0):
    return lax.dynamic_index_in_dim(value, index, axis, keepdims=False)


def dot(a, b):
    return jnp.dot(a, b, preferred_element_type=F32)


def ordered(parts, base, sign):
    size = len(parts)
    stacked = jnp.stack(parts)
    return [pick(stacked, (sign * (j - base)) % size) for j in range(size)]


class Shares:
    def __init__(self, rows, tile):
        self.rows = rows
        self.size = -(-rows // (4 * tile)) * tile
        self.starts = [(rows - self.size) * s // (3 * tile) * tile for s in range(3)]
        self.starts.append(rows - self.size)
        ends = self.starts[1:] + [rows]
        self.lengths = [b - a for a, b in zip(self.starts, ends)]

    def take(self, value, share, axis):
        start = jnp.array(self.starts, jnp.int32)[share]
        return lax.dynamic_slice_in_dim(value, start, self.size, axis)

    def lay(self, parts, axis):
        return jnp.concatenate(
            [lax.slice_in_dim(p, 0, n, axis=axis) for p, n in zip(parts, self.lengths)], axis
        )

    def join(self, parts, me, axis):
        odd, high = me % 2 == 1, me // 2 == 1
        picked = [
            jnp.where(
                high,
                jnp.where(odd, parts[3 ^ s], parts[2 ^ s]),
                jnp.where(odd, parts[1 ^ s], parts[s]),
            )
            for s in range(4)
        ]
        return self.lay(picked, axis)


def assemble(parts, shares, me):
    n, wide = parts[0].shape[0], parts[0].shape[2]

    def kernel(me_ref, *refs):
        o_ref, sems = refs[-2:]
        for act in ("start", "wait"):
            for m in range(4):
                for s in range(4):

                    @pl.when(me_ref[0] ^ m == s)
                    def move():
                        rows = pl.ds(0, shares.lengths[s])
                        to = pl.ds(shares.starts[s], shares.lengths[s])
                        pairs = [(refs[m].at[:, rows], o_ref.at[:, to])]
                        if m == 3 and len(parts) == 5:
                            low, high = pl.ds(0, n // 2), pl.ds(n // 2, n // 2)
                            pairs = [
                                (refs[3].at[:, rows], o_ref.at[low, to]),
                                (refs[4].at[:, rows], o_ref.at[high, to]),
                            ]
                        for k, (source, target) in enumerate(pairs):
                            copy = pltpu.make_async_copy(source, target, sems.at[m + k])
                            getattr(copy, act)()

    return pl.pallas_call(
        kernel,
        out_shape=jax.ShapeDtypeStruct((n, shares.rows, wide), parts[0].dtype),
        in_specs=[SM] + [ANY] * len(parts),
        out_specs=V,
        scratch_shapes=[pltpu.SemaphoreType.DMA((5,))],
        compiler_params=ROOM,
        cost_estimate=FREE,
    )(me, *parts)


def join_wide(parts, shares, me, count):
    wide = parts[0].shape[1]
    size = shares.size

    def kernel(me_ref, *refs):
        o_ref = refs[4]
        for m in range(4):
            for s in range(4):

                @pl.when(me_ref[0] ^ m == s)
                def move():
                    first, rows = shares.starts[s], shares.lengths[s]
                    held = refs[m][...].astype(F32)
                    for k in range(count):
                        cut = held[k * size : k * size + rows]
                        o_ref[k, first : first + rows, :] = cut

    return pl.pallas_call(
        kernel,
        out_shape=jax.ShapeDtypeStruct((count, shares.rows, wide), F32),
        in_specs=[SM] + [V] * 4,
        out_specs=V,
        compiler_params=ROOM,
        cost_estimate=FREE,
    )(me, *parts)


def small_sum(value, axes):
    for axis in axes:
        size = lax.axis_size(axis)
        if size & (size - 1):
            value = lax.psum(value, axis)
            continue
        bit = 1
        while bit < size:
            value = value + lax.ppermute(value, axis, [(i, i ^ bit) for i in range(size)])
            bit *= 2
    return value


def go_up(value, first, last):
    return lax.ppermute(value, "col", [(i, i + 1) for i in range(first, last + 1)])


def go_down(value, first, last):
    return lax.ppermute(value, "col", [(i, i - 1) for i in range(first, last + 1)])


def row_join(parts, axis):
    row = lax.axis_index("row")
    if len(parts) == 2:
        low = row == 0
        parts = [jnp.where(low, parts[0], parts[1]), jnp.where(low, parts[1], parts[0])]
    else:
        parts = ordered(parts, row, 1)
    return jnp.concatenate(parts, axis)


def swap_all(value):
    return [swap_with(value, 1), swap_with(value, 2), swap_with(value, 3)]


class Heads:
    def __init__(self, n_col, width, heads, blocks):
        self.size = n_col * width // heads
        self.firsts = [width * c // self.size for c in range(n_col)]
        lasts = [-(-width * (c + 1) // self.size) for c in range(n_col)]
        self.slots = max(b - a for a, b in zip(self.firsts, lasts))
        self.window = self.slots * self.size
        self.before = [width * c - f * self.size for c, f in enumerate(self.firsts)]
        self.after = [self.window - width - b for b in self.before]
        self.edge = max(self.before + self.after)
        full = (1 << blocks) - 1
        shares = {0: 0, 1: 2, 2: 9, 3: 13, 4: 15}

        def left_share(column):
            part = column % self.size
            return shares[round(4 * part / self.size)] if blocks == 4 else 0

        self.first_mask = [full & ~left_share(b) for b in self.before]
        self.last_mask = []
        for c, f in enumerate(self.firsts):
            end = width * (c + 1)
            begin = (f + self.slots - 1) * self.size
            if begin >= end:
                self.last_mask.append(0)
            elif begin + self.size <= end:
                self.last_mask.append(full)
            else:
                self.last_mask.append(left_share(end - begin))


def edges(value, axis, heads):
    n = lax.axis_size("col")
    edge, width = heads.edge, value.shape[axis]
    left = go_up(lax.slice_in_dim(value, width - edge, width, axis=axis), 0, n - 2)
    right = go_down(lax.slice_in_dim(value, 0, edge, axis=axis), 1, n - 1)
    return left, right


def widen(value, left, right, axis, heads, col):
    wide = jnp.concatenate([left, value, right], axis)
    before = jnp.array(heads.before, jnp.int32)[col]
    return lax.dynamic_slice_in_dim(wide, heads.edge - before, heads.window, axis)


def narrow_cuts(value, axis, heads, col, width):
    edge = heads.edge
    before = jnp.array(heads.before, jnp.int32)[col]
    shape = list(value.shape)
    shape[axis] = width + 2 * edge
    wide = lax.dynamic_update_slice_in_dim(
        jnp.zeros(shape, value.dtype), value, edge - before, axis
    )
    to_left = lax.slice_in_dim(wide, 0, edge, axis=axis)
    to_right = lax.slice_in_dim(wide, edge + width, width + 2 * edge, axis=axis)
    return wide, to_left, to_right


def narrow(wide, front, tail, axis, heads, width):
    edge = heads.edge
    pads = [(0, 0)] * wide.ndim
    pads[axis] = (0, width - edge)
    own = lax.slice_in_dim(wide, edge, edge + width, axis=axis).astype(F32)
    own = own + jnp.pad(front, pads).astype(F32)
    pads[axis] = (width - edge, 0)
    return own + jnp.pad(tail, pads).astype(F32)


def moments(values):
    mean = jnp.mean(values, axis=0, keepdims=True)
    centred = values - mean
    variance = jnp.mean(centred * centred, axis=0, keepdims=True)
    return mean, lax.rsqrt(variance + EPSILON)


def body(
    tokens,
    cotangent,
    w_qkv,
    q_bias,
    v_bias,
    w_out,
    out_bias,
    w_up,
    up_bias,
    w_down,
    down_bias,
    ln1_gain,
    ln1_bias,
    ln2_gain,
    ln2_bias,
    key_start,
):
    n_row, n_col = lax.axis_size("row"), lax.axis_size("col")
    row, col = lax.axis_index("row"), lax.axis_index("col")
    seqs, rows, width = tokens.shape
    length = seqs * rows
    depth = width * n_col
    part = length // n_col
    in_rows = w_up.shape[0]
    ff = w_up.shape[1]
    ff_rows = w_down.shape[0]
    ff_part = ff_rows // n_col
    heads = Heads(n_col, width, key_start.shape[0], rows * n_row // BLK)
    size, window = heads.size, heads.window
    firsts = jnp.array(heads.firsts, jnp.int32) * size
    begin = firsts[col]

    shares = Shares(width, 16)
    dp = lax.axis_index("dp")
    row_at = row[None].astype(jnp.int32)
    col_at = col[None].astype(jnp.int32)
    other_rows = [((row + i) % n_row)[None].astype(jnp.int32) for i in range(n_row)]


    x = tokens.reshape(length, width).T
    g = cotangent.reshape(length, width).T
    place_in = col * n_row + row
    half = n_col // 2

    def between_owners(value_of, steps, back):
        got = []
        for step in steps:
            pairs = []
            for r in range(n_row):
                for c in range(n_col):
                    to = r * n_col + (c - step) % n_col
                    here, there = r * n_col + c, (to % n_row) * n_col + to // n_row
                    pairs.append((there, here) if back else (here, there))
            got.append(lax.ppermute(value_of(step), ("row", "col"), pairs))
        return got

    x_all = lax.all_gather(x, "col", axis=0, tiled=True)
    wq = w_qkv.transpose(0, 2, 1)
    w3_own = widen(wq, *edges(wq, 1, heads), 1, heads, col)
    w3_parts = [w3_own] + [turn(w3_own, "row", -step) for step in range(1, n_row)]
    w3 = row_join(w3_parts, 2).reshape(3 * window, depth)
    params = jnp.stack([ln1_gain, ln1_bias, ln2_gain, ln2_bias, out_bias, q_bias, v_bias])
    params = [turn(params, "col", step) for step in range(n_col)]
    params = jnp.concatenate(ordered(params, col, -1), 1)
    gain1, shift1, gain2, shift2, bias_out, bias_q, bias_v = [p[:, None] for p in params]
    bias3 = jnp.concatenate(
        [
            lax.dynamic_slice_in_dim(bias_q, begin, window, 0),
            jnp.zeros((window, 1), F32),
            lax.dynamic_slice_in_dim(bias_v, begin, window, 0),
        ]
    )
    no_bias = jnp.zeros((depth, 1), F32)
    columns = jnp.concatenate([gain1, shift1, bias_out, gain2, shift2, no_bias], 1)
    meta = jnp.stack(
        [
            jnp.array(heads.firsts, jnp.int32)[col],
            row,
            jnp.array(heads.first_mask, jnp.int32)[col],
            jnp.array(heads.last_mask, jnp.int32)[col],
        ]
    )
    up_parts = [w_up] + [turn(w_up, "row", -step) for step in range(1, n_row)]
    up_turned = row_join(up_parts, 0).T
    out_own = shares.take(w_out.T, dp, 0)
    down_own = shares.take(w_down.T, dp, 0)
    x_all, g, out_own, down_own, w3, meta, columns, bias3 = gate(
        [x_all, g, out_own, down_own, w3, meta, columns, bias3], [up_turned]
    )

    g_all = lax.all_gather(g, "col", axis=0, tiled=True)
    moved_out = [out_own] + [turn(out_own, "col", -step) for step in range(1, n_col)]
    x_float = x_all.astype(F32)
    mean1, rstd1 = moments(x_float)
    n1 = ((x_float - mean1) * rstd1 * gain1 + shift1).astype(BF16)
    triple = product(w3, n1, bias3).reshape(3, window, length)
    triple, *rest = gate([triple] + moved_out[1:], [])
    moved_out = moved_out[:1] + rest

    pieces = [triple] + [turn(triple, "row", -step) for step in range(1, n_row)]
    moved_out = jnp.stack(ordered(moved_out, col, 1))
    moved_out, *rest = gate([moved_out] + pieces[1:], [])
    pieces = pieces[:1] + rest

    near_out = [swap_with(moved_out, 1), swap_with(moved_out, 2)]
    *cuts, mixed, norms = attn_fwd(meta, key_start, pieces, heads.slots, size)
    far_cuts = [near_out[0][:half], near_out[1][half:]]
    *cuts, near_x, near_y, far_x, far_y, down_own = gate(
        list(cuts) + near_out + far_cuts + [down_own], []
    )

    def move_down(step):
        return block(down_own, (col - step) % n_col, ff_part, 1)

    far_out = [swap_with(far_x, 2), swap_with(far_y, 1)]
    moved_down = between_owners(move_down, range(half), False)
    mixed_own = row_sum(cuts).astype(BF16)
    mixed_own, g_all, *rest = gate([mixed_own, g_all] + moved_down + far_out, [])
    moved_down, far_out = rest[:half], rest[half:]

    dp_at = dp[None].astype(jnp.int32)
    got = [
        turn(block(mixed_own, (col + step) % n_col, part, 1), "col", step) for step in range(n_col)
    ]
    out_weights = assemble([moved_out, near_x, near_y] + far_out, shares, dp_at)
    out_weights = [out_weights] + [turn(out_weights, "row", -step) for step in range(1, n_row)]
    x_part = block(x_all, col, part, 1)
    down_own, x_part, *rest = gate([down_own, x_part] + got[1:] + out_weights[1:], [])
    got = got[:1] + rest[: n_col - 1]
    out_weights = out_weights[:1] + rest[n_col - 1 :]
    out_weights = [w.reshape(depth, in_rows) for w in out_weights]

    moved_down = moved_down + between_owners(move_down, range(half, n_col), False)
    got = ordered(got, col, -1)
    lapped = [heads.firsts[j] * size for j in range(n_col)]
    attention = sum(
        jnp.pad(piece, ((at, depth - at - window), (0, 0))) for piece, at in zip(got, lapped)
    )
    resid, hat2, n2_own, rstd2 = mixed_norm(out_weights, attention, row_at, columns, x_part)
    moved_down = jnp.stack(ordered(moved_down, place_in, 1))
    n2_own, g, moved_down = gate([n2_own, g, moved_down], [])

    n2_all = lax.all_gather(n2_own, "col", axis=1, tiled=True)
    down_weights = assemble([moved_down] + swap_all(moved_down), shares, dp_at)
    down_weights = [turn(down_weights, "row", -step) for step in range(n_row)]
    down_weights = [w.reshape(depth, ff_part) for w in down_weights]
    down_turned = turned(down_weights)
    g_sums = jnp.sum(g.astype(F32), axis=1)
    n2_all, down_turned = gate([n2_all, down_turned], [g_sums])

    hidden_all, du_all, part2, du_sums = hidden_layer(
        up_turned, down_turned, n_row, up_bias[:, None], n2_all, g_all, row_at
    )
    part2, hidden_all, du_all = gate([part2, hidden_all, du_all], [])

    def relay_cut(value, far, cut, bit):
        return (cut.take(value, dp ^ (3 - bit), 1).astype(F32) + far.astype(F32)).astype(BF16)

    def share_sum(value, cut, near, relayed):
        own = cut.take(value, dp, 1).astype(F32)
        return (own + near.astype(F32) + relayed.astype(F32)).astype(BF16)

    def up_product(r):
        return token_product(n2_all, du_all, r, n_row, True)

    def down_product(r):
        return token_product(g_all, hidden_all, r, n_row, False).reshape(n_col, width, ff_part)

    dn2 = lax.psum_scatter(part2, "col", scatter_dimension=1, tiled=True)
    up_grad = [up_product(r) for r in other_rows[1:]]
    n2_all, hidden_all, *up_grad = gate([n2_all, hidden_all] + up_grad, [])

    up_grad = [turn(p, "row", i + 1) for i, p in enumerate(up_grad)]
    up_grad = [up_product(other_rows[0])] + up_grad
    down_grad = [down_product(r) for r in other_rows[1:]]
    hidden_all, *rest = gate([hidden_all] + up_grad + down_grad, [])
    up_grad, down_grad = rest[:n_row], rest[n_row:]
    up_rows = width if in_rows % width == 0 else in_rows
    up_shares, fine = Shares(up_rows, 8), Shares(width, 8)
    up_grad = sum(p.astype(F32) for p in up_grad).astype(BF16)
    up_grad = up_grad.reshape(in_rows // up_rows, up_rows, ff)
    up_far = up_shares.take(up_grad, dp ^ 3, 1)
    up_far, hidden_all, *down_grad = gate([up_far, hidden_all] + down_grad, [])

    up_far = swap_with(up_far, 1)
    down_grad = [turn(p, "row", i + 1) for i, p in enumerate(down_grad)]
    down_grad = [down_product(other_rows[0])] + down_grad
    hidden_all, *down_grad = gate([hidden_all] + down_grad, [])
    down_grad = sum(p.astype(F32) for p in down_grad).astype(BF16)
    down_far = fine.take(down_grad, dp ^ 3, 1)
    down_far, hidden_all = gate([down_far, hidden_all], [])

    down_far = swap_with(down_far, 2)
    up_near = up_shares.take(up_grad, dp ^ 1, 1)
    down_near = fine.take(down_grad, dp ^ 2, 1)
    du_row = du_sums[:, 0]
    shrunk = split_product(down_weights, hidden_all, row_at, columns, 5, BF16)
    own_sum = block(shrunk, col, part, 1).astype(F32) + resid
    shrunk = lax.dynamic_update_slice_in_dim(shrunk, own_sum.astype(BF16), col * part, 1)
    up_relay = relay_cut(up_grad, up_far, up_shares, 1)
    down_relay = relay_cut(down_grad, down_far, fine, 2)
    g_part = block(g_all, col, part, 1)
    dn2, shrunk, up_relay, down_relay, up_near, down_near, du_row, g_part = gate(
        [dn2, shrunk, up_relay, down_relay, up_near, down_near, du_row, g_part], []
    )

    up_near = swap_with(up_near, 1)
    down_near = swap_with(down_near, 2)
    dr, db, da, sums2 = mixed_norm_back(out_weights, dn2, hat2, rstd2, g_part, row_at, columns)
    early = jnp.concatenate([sums2.T.reshape(-1), du_row, g_sums])
    da_cuts = [
        lax.dynamic_slice_in_dim(da, firsts[(col + step) % n_col], window, 0)
        for step in range(n_col)
    ]
    db, shrunk, up_near, down_near, up_relay, down_relay, *da_cuts = gate(
        [db, shrunk, up_near, down_near, up_relay, down_relay] + da_cuts, []
    )

    got = [turn(cut, "col", step) for step, cut in enumerate(da_cuts)]
    up_relay = swap_with(up_relay, 2)
    down_relay = swap_with(down_relay, 1)
    out_grad = [token_product(db, attention, r, n_row, False) for r in other_rows[::-1]][::-1]
    out_grad = [o.reshape(n_col, width, in_rows) for o in out_grad]
    rest = gate(got[1:] + out_grad + [up_relay, down_relay, shrunk], [])
    got, rest = got[:1] + rest[: n_col - 1], rest[n_col - 1 :]
    out_grad, (up_relay, down_relay, shrunk) = rest[:n_row], rest[n_row:]

    outputs = lax.psum_scatter(shrunk, "col", scatter_dimension=0, tiled=True)
    da_own = jnp.concatenate(ordered(got, col, -1), 1)
    da_pieces = [da_own] + [turn(da_own, "row", -step) for step in range(1, n_row)]
    out_grad = row_sum(out_grad).astype(BF16)
    up_share = share_sum(up_grad, up_shares, up_near, up_relay)
    down_share = share_sum(down_grad, fine, down_near, down_relay)
    out_sent = jnp.stack([fine.take(out_grad, dp ^ 1, 1), fine.take(out_grad, dp ^ 3, 1)])
    *rest, out_sent, up_share, down_share = gate(
        da_pieces[1:] + [out_sent, up_share, down_share], []
    )
    da_pieces = [da_own] + rest

    out_first = swap_with(out_sent, 1)
    up_y = swap_with(up_share, 2)

    def move_home(step):
        return pick(down_share, (place_in + step) % n_col)

    down_home = between_owners(move_home, range(half), True)
    dqkv = attn_bwd(meta, key_start, pieces, da_pieces, mixed, norms, heads.slots, size)
    *rest, out_first, up_y, up_share, down_share = gate(
        list(dqkv) + down_home + [out_first, up_y, up_share, down_share], []
    )
    dqkv, down_home = rest[:n_row], rest[n_row:]
    out_near, out_far = out_first[0], out_first[1]
    out_relay = relay_cut(out_grad, out_far, fine, 1)

    out_relay = swap_with(out_relay, 2)
    up_x = swap_with(up_share, 1)
    down_home = down_home + between_owners(move_home, range(half, n_col), True)
    dqkv = row_sum(dqkv).astype(BF16).reshape(3 * window, length)
    out_near, out_grad, *down_home = gate([out_near, out_grad] + down_home, [dqkv])
    homes = jnp.stack(ordered(down_home, col, -1))
    out_share = share_sum(out_grad, fine, out_near, out_relay)
    qkv_parts = [
        token_product(dqkv, n1, r, n_row, False).reshape(3, window, in_rows)
        for r in other_rows[:0:-1]
    ][::-1]
    dqkv, homes, outputs, up_x, out_share, *qkv_parts = gate(
        [dqkv, homes, outputs, up_x, out_share] + qkv_parts, []
    )

    homes_near = [swap_with(homes, 1), swap_with(homes, 2)]
    own = token_product(dqkv, n1, other_rows[0], n_row, False).reshape(3, window, in_rows)
    qkv_grad = row_sum([own] + qkv_parts).astype(BF16)
    wide, to_left, to_right = narrow_cuts(qkv_grad, 1, heads, col, width)
    dqkv, wide, to_left, to_right, out_share, up_y, *homes_near = gate(
        [dqkv, wide, to_left, to_right, out_share, up_y] + homes_near, []
    )

    out_home = lax.psum_scatter(out_share, "col", scatter_dimension=0, tiled=True)
    tail, front = go_down(to_left, 1, n_col - 1), go_up(to_right, 0, n_col - 2)
    homes_far = swap_with(homes_near[1], 1)
    up_far = swap_with(up_x, 2)
    dn1, norm1 = norm_product_tn(w3, dqkv, n1, columns, rstd1, dr, col_at, n_col)
    qkv_grad = narrow(wide, front, tail, 1, heads, width).astype(BF16)
    qkv_sent = [fine.take(qkv_grad, dp ^ m, 1) for m in (1, 2, 3)]
    dn1, dqkv, homes_far, up_far, out_home, *qkv_sent = gate(
        [dn1, dqkv, homes_far, up_far, out_home] + qkv_sent, [norm1]
    )

    dx = lax.psum_scatter(dn1, "col", scatter_dimension=0, tiled=True)
    qkv_got = [swap_with(v, m) for v, m in zip(qkv_sent, (1, 2, 3))]
    out_all = [swap_with(out_home, 1), swap_with(out_home, 2)]
    homes, homes_far, norm1, outputs, dqkv = gate(
        [homes, homes_far, norm1, outputs, dqkv], qkv_sent
    )
    homes = fine.join([homes] + homes_near + [homes_far], dp, 1).astype(F32)
    down_grad = jnp.concatenate([homes[j] for j in range(n_col)], 1)
    outputs = (outputs.astype(F32) + down_bias[:, None]).astype(BF16)
    dq_dv = jnp.sum(dqkv.astype(F32), axis=1).reshape(3, window)
    sums = lax.dynamic_update_slice_in_dim(jnp.zeros((2, depth), F32), dq_dv[::2], begin, 1)
    small = jnp.concatenate([sums.reshape(-1), norm1.T.reshape(-1), early])[None]
    small = small_sum(small, ("row",))[0]
    sums, local = small[: 7 * depth].reshape(7, depth), small[7 * depth :]
    sums = small_sum(sums, ("col",))
    sums = lax.dynamic_slice_in_dim(sums, col * width, width, 1)
    small = jnp.concatenate([sums.reshape(-1), local])
    deep = -(-small.shape[0] // in_rows)
    small = jnp.pad(small, (0, deep * in_rows - small.shape[0])).reshape(deep, in_rows)
    rounded = lax.reduce_precision(small, 8, 7)
    rest = (small - rounded).astype(BF16)
    rounded = rounded.astype(BF16)
    qkv_share = fine.take(qkv_grad, dp, 1).astype(F32)
    qkv_share = (qkv_share + sum(q.astype(F32) for q in qkv_got)).astype(BF16)
    ends = 3 * fine.size
    payload = jnp.concatenate([qkv_share.reshape(ends, in_rows), rounded, rest])
    up_far, payload, *out_all = gate([up_far, payload] + out_all, [down_grad, outputs])

    qkv_all = swap_all(payload)
    out_all.append(swap_with(out_all[0], 2))
    up_grad = up_shares.join([up_share, up_x, up_y, up_far], dp, 1).astype(F32)
    up_grad = up_grad.reshape(in_rows, ff)
    hat1 = (x.astype(F32) - mean1) * rstd1
    dx = dx.reshape(width + 16, length)
    lines = dx[width : width + 4].astype(F32)
    lines = (lines[0::2] + lines[1::2]) / depth
    input_grad = dx[:width].astype(F32) - rstd1 * (lines[0:1] + hat1 * lines[1:2])
    input_grad = input_grad.astype(BF16)
    *out_all, a, b, c = gate(out_all + qkv_all, [up_grad, input_grad])

    out_grad = join_wide([v[0] for v in [out_home] + out_all], fine, dp_at, 1)[0]
    small = sum(v[ends:].astype(F32) for v in (payload, a, b, c))
    small = (small[:deep] + small[deep:]).reshape(-1)
    sums, local = small[: 7 * width].reshape(7, width), small[7 * width : 8 * width + ff]
    qkv_grad = join_wide([payload, a, b, c], fine, dp_at, 3)
    return (
        outputs.T.reshape(tokens.shape),
        input_grad.T.reshape(tokens.shape),
        qkv_grad.transpose(0, 2, 1),
        sums[0],
        sums[1],
        out_grad.T,
        sums[4],
        up_grad,
        local[:ff],
        down_grad.T,
        local[ff:],
        sums[2],
        sums[3],
        sums[5],
        sums[6],
    )


def solution(mesh):
    inputs = (
        P("dp", "row", "col"),
        P("dp", "row", "col"),
        P(None, "row", "col"),
        P("col"),
        P("col"),
        P("row", "col"),
        P("col"),
        P("row", "col"),
        P("col"),
        P("row", "col"),
        P("col"),
        P("col"),
        P("col"),
        P("col"),
        P("col"),
        P(),
    )
    return jax.shard_map(
        body, mesh=mesh, in_specs=inputs, out_specs=inputs[:15], check_vma=False
    )
```
